32 devices in a mesh: grp: 4 (over y, x), tp: 8 (over z, core).
Axes of the slice: x: 2, y: 2, z: 4, core: 2. Of those that a mesh axis runs over, the one named last changes fastest.
Arguments:
- hidden: bfloat16 [36864, 5120], P(('grp', 'tp')), may hold values from -6 to 6
- lengths: int32 [4, 8], P('grp'), may hold values from 1 to 1152, 3686 in all within a row
- kv_weight: bfloat16 [5120, 1024], P('grp', 'tp'), may hold values from -0.078125 to 0.078125
- input_gain: float32 [5120], replicated, may hold values from 0.1 to 1.9
- key_gain: float32 [128], replicated, may hold values from 0.1 to 1.9
Outputs:
- cache_pages: bfloat16 [160, 128, 1024], P(('grp', 'tp'))
The draws below stay inside these ranges and needn't reach their ends.
Inputs may be any that keep to these rules, and one draw needn't show every extreme that they name: In each group's row the 8 lengths sum to 3686 and the largest equals 1152.
All inputs are finite; a program needn't handle non-finite values.
Results may differ from the reference program's by a relative error of at most 0.0049.
Values may be sent and summed in bfloat16 or wider, within the bound.
No kernel may reach another device: no remote copies, remote signals or barrier semaphores. Data moves between devices by JAX's collectives and lax.ppermute only.
A program may use at most 64 MiB of HBM per device.

```python
import math
import jax
import jax.numpy as jnp
import numpy as np
from jax import lax

D = 5120
HD = 128
KVH = 4
BLK = 128
B_IN = 9
LIVE_SUM = 3686
B_BAL = 5
TOKENS = 36864
N_GRP = 4
N_TP = 8


def block_scale(rng, dims, split, least, top_value):
    level, own = 1.0, jax.random.fold_in(rng, 6)
    for dim, parts in split:
        heights = jnp.exp(jax.random.uniform(jax.random.fold_in(own, dim), (parts,), jnp.float32, least / len(split), top_value / len(split)))
        level = level * jnp.repeat(heights, dims[dim] // parts).reshape([-1 if axis == dim else 1 for axis in range(len(dims))])
    return level


def length_profile(count, total, reach, lean):
    portions = [(1 << 20) // math.isqrt(grade ** lean) + 1 for grade in range(2, count + 1)]
    rest, given = total - reach - (count - 1), [1] * (count - 1)
    while rest > 0:
        free = [i for i in range(count - 1) if given[i] < reach]
        whole, remaining = sum([portions[i] for i in free]), rest
        for i in free:
            extra = min(reach - given[i], max(1, remaining * portions[i] // whole), rest)
            given[i] = given[i] + extra
            rest = rest - extra
    return np.array([reach] + given)


def uneven(key, amount, total, bound, lean):
    if amount == 2:
        one = jax.random.randint(key, (), max(1, total - bound), min(bound, total - 1) + 1)
        return jnp.stack([one, total - one])
    sizes = jnp.asarray(length_profile(amount, total, bound, lean), jnp.int32)
    pairs = (amount - 1) // 2
    donor, sink = sizes[1:1 + 2 * pairs:2], sizes[2:2 + 2 * pairs:2]
    room = jnp.minimum(donor - 1, bound - sink)
    passed = jax.random.randint(jax.random.fold_in(key, 1), (pairs,), 0, 1 << 20) % (room + 1)
    sizes = sizes.at[1:1 + 2 * pairs:2].set(donor - passed).at[2:2 + 2 * pairs:2].set(sink + passed)
    return sizes[jax.random.permutation(jax.random.fold_in(key, 2), amount)]


def scatter_about(rng, shape, width, limit, split=(), kind=jnp.bfloat16):
    array = jax.random.normal(rng, shape, jnp.float32) * width
    if len(split) > 0:
        array = block_scale(rng, shape, split, -0.22, 0.18) * array
    return jnp.clip(array, min=-limit, max=limit).astype(kind)


def setup_inputs(seed: int = 0) -> dict:
    seeds = jax.random.split(jax.random.key(seed), 6)
    hidden = scatter_about(seeds[0], (TOKENS, D), 1.0, 6.0, ((0, 32),))
    lengths = jax.vmap(lambda own: uneven(own, N_TP, LIVE_SUM, B_IN * BLK, 2))(jax.random.split(seeds[1], N_GRP)).reshape((N_GRP, N_TP)).astype(jnp.int32)
    kv_weight = scatter_about(seeds[2], (D, 2 * KVH * HD), D ** -0.5, 0.078125, ((0, 4), (1, 8)))
    input_gain = jnp.clip(1.0 + 0.18 * jax.random.normal(seeds[3], (D,), jnp.float32), 0.1, 1.9)
    key_gain = jnp.clip(1.0 + 0.18 * jax.random.normal(seeds[4], (HD,), jnp.float32), 0.1, 1.9)
    return {"hidden": hidden, "lengths": lengths, "kv_weight": kv_weight, "input_gain": input_gain, "key_gain": key_gain}


rope_base = 1000000.0
norm_eps = 1e-06

def normalize(token_rows, input_gain):
    values = token_rows.astype(jnp.float32)
    row_scale = lax.rsqrt(lax.optimization_barrier(jnp.mean(values * values, axis=-1, keepdims=True)) + norm_eps)
    return (values * row_scale * input_gain).astype(jnp.bfloat16)

def finish(projected, positions, valid, key_gain):
    key_width = KVH * HD
    half_dim = HD // 2
    row_count = projected.shape[0]
    key_part = projected[:, :key_width].reshape(row_count, KVH, HD)
    key_scale = lax.rsqrt(lax.optimization_barrier(jnp.mean(key_part * key_part, axis=-1, keepdims=True)) + norm_eps)
    key_part = key_part * key_scale * key_gain
    exponent = jnp.arange(half_dim, dtype=jnp.float32) * (2.0 / HD)
    inverse = jnp.exp(exponent * -math.log(rope_base))
    angles = positions.astype(jnp.float32)[:, None] * inverse[None, :]
    cosine = jnp.cos(angles)[:, None, :]
    sine_part = jnp.sin(angles)[:, None, :]
    lower_half = key_part[..., :half_dim]
    upper_half = key_part[..., half_dim:]
    turned = jnp.concatenate([lower_half * cosine - upper_half * sine_part, upper_half * cosine + lower_half * sine_part], axis=-1)
    merged = jnp.concatenate([turned.reshape(row_count, key_width), projected[:, key_width:]], axis=-1)
    return jnp.where(valid[:, None], merged, 0.0).astype(jnp.bfloat16)

def reference(hidden, lengths, kv_weight, input_gain, key_gain):
    block_rows = hidden.reshape(N_GRP, N_TP * B_IN, BLK, D)
    block_counts = ((lengths + (BLK - 1)) // BLK).astype(jnp.int32)
    block_ends = jnp.cumsum(block_counts, axis=1).astype(jnp.int32)
    block_starts = (block_ends - block_counts).astype(jnp.int32)
    page_slots = jnp.arange(N_TP, dtype=jnp.int32)[:, None] + N_TP * jnp.arange(B_BAL, dtype=jnp.int32)[None, :]
    page_ranks = page_slots.reshape(-1)
    offsets = jnp.arange(BLK, dtype=jnp.int32)

    def one_group(group_data):
        group_blocks, group_len, group_ends, group_starts = group_data
        anchor = jnp.minimum(lax.optimization_barrier(jnp.sum((group_ends[None, :] <= page_ranks[:, None]).astype(jnp.int32), axis=1)).astype(jnp.int32), N_TP - 1)
        block_index = (page_ranks - group_starts[anchor]).astype(jnp.int32)
        page_live = page_ranks < group_ends[-1]
        flat_index = (anchor * B_IN + jnp.clip(block_index, 0, B_IN - 1)).astype(jnp.int32)
        token_rows = jnp.take(group_blocks, flat_index, axis=0).reshape(-1, D)
        positions = block_index[:, None] * BLK + offsets[None, :]
        valid = page_live[:, None] & (positions < group_len[anchor][:, None])
        projected = jnp.dot(normalize(token_rows, input_gain), kv_weight, preferred_element_type=jnp.float32)
        return finish(projected, positions.reshape(-1), valid.reshape(-1), key_gain).reshape(N_TP * B_BAL, BLK, 2 * KVH * HD)
    cache_pages = lax.map(one_group, (block_rows, lengths, block_ends, block_starts))
    return cache_pages.reshape(N_GRP * N_TP * B_BAL, BLK, 2 * KVH * HD)
```

```python
import functools
import math

import jax
import jax.numpy as jnp
import numpy as np
from jax import lax
from jax.experimental import pallas as pl
from jax.experimental.pallas import tpu as pltpu
from jax.sharding import PartitionSpec as P

HD = 128
KVH = 4
BLK = 128


rope_base = 1000000.0
norm_eps = 1e-06


def normalize(token_rows, input_gain):
    values = token_rows.astype(jnp.float32)
    row_scale = lax.rsqrt(jnp.mean(values * values, axis=-1, keepdims=True) + norm_eps)
    return (values * row_scale * input_gain).astype(jnp.bfloat16)


def finish(projected, positions, valid, key_gain):
    key_width = KVH * HD
    half_dim = HD // 2
    row_count = projected.shape[0]
    key_part = projected[:, :key_width].reshape(row_count, KVH, HD)
    key_scale = lax.rsqrt(jnp.mean(key_part * key_part, axis=-1, keepdims=True) + norm_eps)
    key_part = key_part * key_scale * key_gain
    exponent = jnp.arange(half_dim, dtype=jnp.float32) * (2.0 / HD)
    inverse = jnp.exp(exponent * -math.log(rope_base))
    angles = positions.astype(jnp.float32)[:, None] * inverse[None, :]
    cosine = jnp.cos(angles)[:, None, :]
    sine_part = jnp.sin(angles)[:, None, :]
    lower_half = key_part[..., :half_dim]
    upper_half = key_part[..., half_dim:]
    turned = jnp.concatenate(
        [
            lower_half * cosine - upper_half * sine_part,
            upper_half * cosine + lower_half * sine_part,
        ],
        axis=-1,
    )
    merged = jnp.concatenate(
        [turned.reshape(row_count, key_width), projected[:, key_width:]], axis=-1
    )
    return jnp.where(valid[:, None], merged, 0.0).astype(jnp.bfloat16)


def project(normed, kv_weight):
    all_rows = lax.all_gather(kv_weight, "grp", axis=0, tiled=True)
    return jnp.dot(
        normed,
        lax.all_gather(all_rows, "tp", axis=1, tiled=True),
        preferred_element_type=jnp.float32,
    )


def pages_per_device(tp_count, own_blocks):
    live_tokens = 2 * tp_count * own_blocks * BLK // 5
    return ((live_tokens + BLK - 1) // BLK + 2 * tp_count - 2) // tp_count


def general(hidden, lengths, kv_weight, input_gain, key_gain):
    tp_count = lax.axis_size("tp")
    my_index = lax.axis_index("tp")
    own_blocks = hidden.shape[0] // BLK
    page_count = pages_per_device(tp_count, own_blocks)
    per_peer = (own_blocks + tp_count - 1) // tp_count
    cache_width = 2 * KVH * HD
    group_len = lengths[0]
    block_counts = (group_len + (BLK - 1)) // BLK
    block_ends = jnp.cumsum(block_counts)
    block_starts = block_ends - block_counts
    offsets = jnp.arange(BLK, dtype=jnp.int32)
    my_start = block_starts[my_index]
    my_count = block_counts[my_index]
    my_length = group_len[my_index]
    outbound = (
        jnp.arange(tp_count, dtype=jnp.int32)[:, None] - my_start
    ) % tp_count + tp_count * jnp.arange(per_peer, dtype=jnp.int32)[None, :]
    outbound = outbound.reshape(-1)
    sending = outbound < my_count
    picked_local = jnp.minimum(outbound, own_blocks - 1)
    page_ranks = tp_count * jnp.arange(page_count, dtype=jnp.int32) + my_index
    anchor = jnp.minimum(
        jnp.sum((block_ends[None, :] <= page_ranks[:, None]).astype(jnp.int32), axis=1),
        tp_count - 1,
    )
    block_index = page_ranks - block_starts[anchor]
    page_live = page_ranks < block_ends[-1]
    chosen = anchor * per_peer + jnp.clip(block_index // tp_count, 0, per_peer - 1)
    projected = project(normalize(hidden, input_gain), kv_weight)
    own_pos = (jnp.arange(own_blocks, dtype=jnp.int32)[:, None] * BLK + offsets[None, :]).reshape(
        -1
    )
    own_cache = finish(projected, own_pos, own_pos < my_length, key_gain).reshape(
        own_blocks, BLK, cache_width
    )
    outgoing = jnp.where(
        sending[:, None, None],
        jnp.take(own_cache, picked_local, axis=0),
        jnp.zeros((), jnp.bfloat16),
    )
    arrived = lax.all_to_all(outgoing, "tp", split_axis=0, concat_axis=0, tiled=True)
    cache_pages = jnp.take(arrived, chosen, axis=0)
    return jnp.where(page_live[:, None, None], cache_pages, jnp.zeros((), jnp.bfloat16))


def slot_tables(nz):
    columns, arrival = [], []
    for z in range(nz):
        row, came = [z], [(0, 0)]
        for step in range(1, nz):
            if z + step < nz:
                row.append(z + step)
                came.append((step, 0))
            if z - step >= 0:
                row.append(z - step)
                came.append((step, 1))
        columns.append(row)
        arrival.append(came)
    return columns, arrival


def read_table(table, row, column):
    value = jnp.int32(table[0][column])
    for index in range(1, len(table)):
        value = jnp.where(row == index, jnp.int32(table[index][column]), value)
    return value


def line_steps(nz):
    steps = []
    for step in range(1, nz):
        down = [(2 * s + c, 2 * s - 2 + c) for s in range(1, nz) if s - 1 + step < nz for c in range(2)]
        up = [(2 * s + c, 2 * s + 2 + c) for s in range(nz - 1) if s + 1 - step >= 0 for c in range(2)]
        steps.append((down, up))
    return steps


def pick_slot(held, slot, nz):
    z = lax.axis_index("tp") // 2
    _, arrival = slot_tables(nz)
    picked = held[arrival[0][slot]]
    for chip in range(1, nz):
        if arrival[chip][slot] != arrival[chip - 1][slot]:
            picked = jnp.where(z >= chip, held[arrival[chip][slot]], picked)
    return picked


flip0 = [(i, i ^ 1) for i in range(4)]
flip1 = [(i, i ^ 2) for i in range(4)]


def sides(shard):
    return lax.ppermute(shard, "grp", flip0), lax.ppermute(shard, "grp", flip1)


def opposite(side_pairs):
    half = side_pairs[0][0].shape[0] // 2
    first = jnp.concatenate([side0[:half] for side0, _ in side_pairs])
    second = jnp.concatenate([side1[half:] for _, side1 in side_pairs])
    return lax.ppermute(first, "grp", flip1), lax.ppermute(second, "grp", flip0)


def scale_kernel(lengths_ref, place_ref, x_ref, out_ref):
    blocks = (lengths_ref[place_ref[1]] + (BLK - 1)) // BLK

    @pl.when(pl.program_id(0) < blocks)
    def _():
        values = x_ref[...].astype(jnp.float32)
        mean = jnp.mean(values * values, axis=-1, keepdims=True)
        out_ref[...] = jnp.broadcast_to(lax.rsqrt(mean + norm_eps), out_ref.shape)


def row_scales(lengths, place, hidden):
    rows, width = hidden.shape

    def live(i, lengths_ref, place_ref):
        return jnp.minimum(i, (lengths_ref[place_ref[1]] + (BLK - 1)) // BLK - 1), 0

    return pl.pallas_call(
        scale_kernel,
        grid_spec=pltpu.PrefetchScalarGridSpec(
            num_scalar_prefetch=2,
            grid=(rows // BLK,),
            in_specs=[pl.BlockSpec((BLK, width), live)],
            out_specs=pl.BlockSpec((BLK, HD), live),
        ),
        out_shape=jax.ShapeDtypeStruct((rows, HD), jnp.float32),
        compiler_params=pltpu.CompilerParams(vmem_limit_bytes=54 << 20),
        cost_estimate=pl.CostEstimate(
            flops=3 * rows * width, bytes_accessed=2 * rows * width, transcendentals=0
        ),
        name="row_scales",
    )(lengths, place, hidden)


def chip_facts(lengths_ref, chip):
    first = jnp.int32(0)
    for index in range(lengths_ref.shape[0]):
        count = (lengths_ref[index] + (BLK - 1)) // BLK
        first = first + jnp.where(index < 2 * chip, count, 0)
    return first, lengths_ref[2 * chip], lengths_ref[2 * chip + 1]


def project_kernel(slot_ids, tile, depth, deep, *refs):
    count = len(slot_ids)
    lengths_ref, place_ref, own_ref, sib_ref = refs[:4]
    near = refs[4 : 4 + 3 * count]
    far = refs[4 + 3 * count : 6 + 3 * count]
    own_scale, sib_scale, turn_ref, gain_ref, out_ref, over_ref = refs[6 + 3 * count : 12 + 3 * count]
    x_buf, w_buf, o_buf, x_sem, w_sem, o_sem = refs[12 + 3 * count :]
    tp_count = lengths_ref.shape[0]
    ahead = x_buf.shape[0]
    group, me = place_ref[0], place_ref[1]
    chip, core = me // 2, me % 2
    first, length0, length1 = chip_facts(lengths_ref, chip)
    count0 = (length0 + (BLK - 1)) // BLK
    own_len = jnp.where(core == 0, length0, length1)
    sib_len = jnp.where(core == 0, length1, length0)
    own_count = (own_len + (BLK - 1)) // BLK
    total = own_count + (sib_len + (BLK - 1)) // BLK
    tiles = (total + (tile - 1)) // tile

    def within(i):
        return jnp.where(i < own_count, i, i - own_count)

    def fetch(step, start):
        slot = lax.rem(step, ahead)
        for part in range(tile):
            i = step * tile + part
            rows = pl.ds(pl.multiple_of(within(i) * BLK, BLK), BLK)
            target = x_buf.at[slot, pl.ds(part * BLK, BLK)]

            @pl.when(i < own_count)
            def _():
                copy = pltpu.make_async_copy(own_ref.at[rows], target, x_sem.at[slot, part])
                copy.start() if start else copy.wait()

            @pl.when(jnp.logical_and(i >= own_count, i < total))
            def _():
                copy = pltpu.make_async_copy(sib_ref.at[rows], target, x_sem.at[slot, part])
                copy.start() if start else copy.wait()

    copies = []
    half = depth // 2
    for index in range(count):
        parts = [(near[3 * index + flip], flip, 0) for flip in range(3)]
        parts += [(far[side].at[pl.ds(index * half, half)], 3, side * half) for side in range(2)]
        for part, (source, flip, offset) in enumerate(parts):
            rows = pl.ds(pl.multiple_of((group ^ flip) * depth + offset, 16), source.shape[0])
            copies.append(
                pltpu.make_async_copy(
                    source, w_buf.at[rows, pl.ds(index * HD, HD)], w_sem.at[5 * index + part]
                )
            )
    fetch(jnp.int32(0), True)
    for copy in copies:
        copy.start()
    for step in range(1, ahead - 1):
        fetch(jnp.int32(step), True)
    for copy in copies:
        copy.wait()

    columns, _ = slot_tables(tp_count // 2)
    is_key = [2 * read_table(columns, chip, slot) + core < KVH for slot in slot_ids]

    def send(i, start):
        second = jnp.where(i < own_count, core, 1 - core)
        place = within(i) + second * count0

        @pl.when(jnp.logical_and(i < total, place < deep * tp_count))
        def _():
            target = out_ref.at[lax.rem(first + place, tp_count), place // tp_count]
            copy = pltpu.make_async_copy(o_buf.at[i], target, o_sem.at[i])
            copy.start() if start else copy.wait()

        @pl.when(jnp.logical_and(i < total, place >= deep * tp_count))
        def _():
            target = over_ref.at[place - deep * tp_count]
            copy = pltpu.make_async_copy(o_buf.at[i], target, o_sem.at[i])
            copy.start() if start else copy.wait()

    def one_tile(step, carry):
        fetch(step + (ahead - 1), True)
        fetch(step, False)
        product = jnp.dot(x_buf[lax.rem(step, ahead)], w_buf[...], preferred_element_type=jnp.float32)
        blocks = []
        for part in range(tile):
            i = jnp.minimum(step * tile + part, total - 1)
            rows = pl.ds(pl.multiple_of(within(i) * BLK, BLK), BLK)
            limit = jnp.where(i < own_count, own_len, sib_len) - within(i) * BLK
            valid = lax.broadcasted_iota(jnp.int32, (BLK, HD), 0) < limit
            scale = jnp.where(i < own_count, own_scale[rows, :], sib_scale[rows, :])
            blocks.append((step * tile + part, rows, valid, scale))
        for index in range(count):

            def scaled(part):
                cut = product[part * BLK : (part + 1) * BLK, index * HD : (index + 1) * HD]
                return cut * blocks[part][3]

            def keep(part, values):
                i, _, valid, _ = blocks[part]
                o_buf[i, index] = jnp.where(valid, values, 0.0).astype(jnp.bfloat16)

            @pl.when(is_key[index])
            def _():
                for part in range(tile):
                    rows = blocks[part][1]
                    values = scaled(part)
                    key_scale = lax.rsqrt(jnp.mean(values * values, axis=-1, keepdims=True) + norm_eps)
                    keys = values * key_scale * gain_ref[...]
                    turned = keys * turn_ref[rows, :HD] + pltpu.roll(keys, HD // 2, 1) * turn_ref[rows, HD:]
                    keep(part, turned)

            @pl.when(jnp.logical_not(is_key[index]))
            def _():
                for part in range(tile):
                    keep(part, scaled(part))

        for part in range(tile):
            send(step * tile + part, True)
        return carry

    lax.fori_loop(0, tiles, one_tile, 0)

    def drain(i, carry):
        send(i, False)
        return carry

    lax.fori_loop(0, total, drain, 0)


def project_slots(slot_ids, lengths, place, own, sibling, near, far, scales, turn, key_gain, deep):
    rows, width = own.shape
    tp_count = lengths.shape[0]
    own_blocks = rows // BLK
    depth = near[0][0].shape[0]
    count = len(slot_ids)
    tile = max(t for t in (1, 2, 3) if own_blocks % t == 0)
    ahead = 3
    spare = 2 * own_blocks - deep * tp_count
    anywhere = pl.BlockSpec(memory_space=pl.ANY)
    whole = pl.BlockSpec(memory_space=pltpu.VMEM)
    pieces = [piece for parts in near for piece in parts] + list(far)
    return pl.pallas_call(
        functools.partial(project_kernel, slot_ids, tile, depth, deep),
        in_specs=[pl.BlockSpec(memory_space=pltpu.SMEM)] * 2
        + [anywhere] * (2 + len(pieces))
        + [whole] * 4,
        out_specs=[anywhere, anywhere],
        out_shape=[
            jax.ShapeDtypeStruct((tp_count, deep, count, BLK, HD), jnp.bfloat16),
            jax.ShapeDtypeStruct((max(spare, 1), count, BLK, HD), jnp.bfloat16),
        ],
        scratch_shapes=[
            pltpu.VMEM((ahead, tile * BLK, width), jnp.bfloat16),
            pltpu.VMEM((width, count * HD), jnp.bfloat16),
            pltpu.VMEM((2 * own_blocks + tile, count, BLK, HD), jnp.bfloat16),
            pltpu.SemaphoreType.DMA((ahead, tile)),
            pltpu.SemaphoreType.DMA((5 * count,)),
            pltpu.SemaphoreType.DMA((2 * own_blocks,)),
        ],
        compiler_params=pltpu.CompilerParams(vmem_limit_bytes=54 << 20),
        cost_estimate=pl.CostEstimate(
            flops=4 * rows * width * count * HD,
            bytes_accessed=4 * rows * width + 2 * width * count * HD,
            transcendentals=0,
        ),
        name="project_slots",
    )(lengths, place, own, sibling, *pieces, scales[0], scales[1], turn, key_gain)


def page_source(lengths_ref, place_ref, page):
    tp_count = lengths_ref.shape[0]
    rank = page * tp_count + place_ref[1]
    end, chip, first = jnp.int32(0), jnp.int32(0), jnp.int32(0)
    for index in range(tp_count):
        end = end + (lengths_ref[index] + (BLK - 1)) // BLK
        if index % 2 == 1 and index + 1 < tp_count:
            passed = end <= rank
            chip = jnp.where(passed, index // 2 + 1, chip)
            first = jnp.where(passed, end, first)
    return rank < end, chip, rank - first


def assemble_kernel(groups, tp_count, deep, lengths_ref, place_ref, *refs):
    out_ref = refs[-1]
    live, chip, within = page_source(lengths_ref, place_ref, pl.program_id(0))
    columns, _ = slot_tables(tp_count // 2)
    over = within >= deep * tp_count
    spilled = len(refs) > 2 * len(groups) + 1
    per_group = 4 if spilled else 2

    @pl.when(live)
    def _():
        for place, slot_ids in enumerate(groups):
            for core in range(2):
                for index, slot in enumerate(slot_ids):
                    column = 2 * read_table(columns, chip, slot) + core
                    target = pl.ds(pl.multiple_of(column * HD, HD), HD)
                    block = refs[per_group * place + core][0, 0, index]
                    if spilled:
                        block = jnp.where(over, refs[per_group * place + 2 + core][0, 0, index], block)
                    out_ref[0, :, target] = block

    @pl.when(jnp.logical_not(live))
    def _():
        out_ref[...] = jnp.zeros_like(out_ref)


def assemble(groups, lengths, place, arrived, spilled, page_count, deep):
    tp_count = lengths.shape[0]
    operands, specs = [], []

    def spec_for(count, core, spill):
        def index_map(page, lengths_ref, place_ref):
            live, chip, within = page_source(lengths_ref, place_ref, page)
            if spill:
                position = jnp.clip(within - deep * tp_count, 0, spill - 1)
            else:
                position = jnp.clip(within // tp_count, 0, deep - 1)
            return 2 * chip + core, position, 0, 0, 0

        return pl.BlockSpec((1, 1, count, BLK, HD), index_map)

    for place_of, slot_ids in enumerate(groups):
        for core in range(2):
            operands.append(arrived[place_of])
            specs.append(spec_for(len(slot_ids), core, 0))
        if spilled is not None:
            for core in range(2):
                operands.append(spilled[place_of])
                specs.append(spec_for(len(slot_ids), core, spilled[place_of].shape[1]))
    return pl.pallas_call(
        functools.partial(assemble_kernel, groups, tp_count, deep),
        grid_spec=pltpu.PrefetchScalarGridSpec(
            num_scalar_prefetch=2,
            grid=(page_count,),
            in_specs=specs,
            out_specs=pl.BlockSpec((1, BLK, 2 * KVH * HD), lambda page, *_: (page, 0, 0)),
        ),
        out_shape=jax.ShapeDtypeStruct((page_count, BLK, 2 * KVH * HD), jnp.bfloat16),
        compiler_params=pltpu.CompilerParams(vmem_limit_bytes=54 << 20),
        name="assemble",
    )(lengths, place, *operands)


def rope_table(rows):
    exponent = jnp.arange(HD // 2, dtype=jnp.float32) * (2.0 / HD)
    inverse = jnp.exp(exponent * -math.log(rope_base))
    angles = jnp.arange(rows, dtype=jnp.float32)[:, None] * inverse[None, :]
    cosine, sine_part = jnp.cos(angles), jnp.sin(angles)
    return jnp.concatenate([cosine, cosine, -sine_part, sine_part], axis=1)


def exchange(sent):
    return lax.all_to_all(sent, "tp", split_axis=0, concat_axis=0, tiled=True)


def paired(hidden, lengths, kv_weight, input_gain, key_gain):
    tp_count = lax.axis_size("tp")
    nz = tp_count // 2
    group, me = lax.axis_index("grp"), lax.axis_index("tp")
    rows = hidden.shape[0]
    own_blocks = rows // BLK
    depth = kv_weight.shape[0]
    deep = 2 * own_blocks // tp_count
    page_count = pages_per_device(tp_count, own_blocks)
    group_len = lengths[0]
    place = jnp.stack([group, me]).astype(jnp.int32)
    swap = [(i, i ^ 1) for i in range(tp_count)]

    own_gain = lax.dynamic_slice(input_gain, (group * depth,), (depth,))
    shard = (kv_weight.astype(jnp.float32) * own_gain[:, None]).astype(jnp.bfloat16)
    sibling = lax.ppermute(hidden, "tp", swap)
    gain = key_gain.reshape(1, HD)

    steps = line_steps(nz)
    held, slots = {(0, 0): shard}, [shard]
    groups = [tuple(range(start, min(start + 2, nz))) for start in range(0, nz, 2)]
    arrived, over = [], []
    below, above = shard, shard
    turn, scale, other_scale = None, None, None
    sent = None
    step = 0
    for slot_ids in groups:
        rounds = [slot_ids] if slots[slot_ids[0] :] and len(slots) > slot_ids[-1] else [(slot,) for slot in slot_ids]
        near = []
        for part in range(len(rounds) + 1):
            moved, beside = (), {}
            if part < len(rounds):
                crossed = sides(jnp.concatenate([slots[slot] for slot in rounds[part]]))
            else:
                if step >= 2 and other_scale is None:
                    other_scale = beside["other"] = lax.ppermute(scale, "tp", swap)
                crossed = opposite([pair[1:] for pair in near])
            if step < len(steps):
                down, up = steps[step]
                step += 1
                moved = lax.ppermute(above, "tp", down), lax.ppermute(below, "tp", up)
            if scale is None:
                scale = beside["scale"] = row_scales(group_len, place, hidden)
            elif turn is None:
                turn = beside["turn"] = rope_table(rows)
                beside["sibling"] = sibling
            elif sent is not None:
                beside["sent"] = sent
            moved, crossed, beside = lax.optimization_barrier((moved, crossed, beside))
            turn, scale = beside.get("turn", turn), beside.get("scale", scale)
            sibling, other_scale = beside.get("sibling", sibling), beside.get("other", other_scale)
            if "sent" in beside:
                arrived.append(exchange(beside["sent"]))
                sent = None
            if moved:
                above, below = moved
                held[(step, 0)], held[(step, 1)] = moved
            if part < len(rounds):
                for index, slot in enumerate(rounds[part]):
                    cut = slice(index * depth, (index + 1) * depth)
                    near.append((slots[slot], crossed[0][cut], crossed[1][cut]))
            while len(slots) < nz and all(
                arrival[len(slots)] in held for arrival in slot_tables(nz)[1]
            ):
                slots.append(pick_slot(held, len(slots), nz))
        sent, rest = project_slots(
            slot_ids, group_len, place, hidden, sibling, near, crossed, (scale, other_scale), turn, gain, deep
        )
        over.append(rest)
    arrived.append(exchange(sent))

    def plain(operands):
        return assemble(groups, group_len, place, operands[0], None, page_count, deep)

    if 2 * own_blocks == deep * tp_count:
        return plain((arrived, over))

    def spilling(operands):
        spilled = []
        for rest in operands[1]:
            got = [rest]
            for flip in range(1, tp_count):
                got.append(lax.ppermute(rest, "tp", [(i, i ^ flip) for i in range(tp_count)]))
            spilled.append(jnp.take(jnp.stack(got), jnp.arange(tp_count) ^ me, axis=0))
        return assemble(groups, group_len, place, operands[0], spilled, page_count, deep)

    counts = (group_len + (BLK - 1)) // BLK
    most = jnp.max(counts[0::2] + counts[1::2])
    return lax.cond(most > deep * tp_count, spilling, plain, (arrived, over))


def local(hidden, lengths, kv_weight, input_gain, key_gain):
    tp_count = lax.axis_size("tp")
    fits = (
        lax.axis_size("grp") == 4
        and tp_count & (tp_count - 1) == 0
        and kv_weight.shape[1] == HD
        and kv_weight.shape[0] % 256 == 0
        and 2 * (hidden.shape[0] // BLK) >= tp_count
    )
    chosen = paired if fits else general
    return chosen(hidden, lengths, kv_weight, input_gain, key_gain)


def solution(mesh):
    placed = (P(("grp", "tp"), None), P("grp", None), P("grp", "tp"), P(), P())
    return jax.shard_map(
        local, mesh=mesh, in_specs=placed, out_specs=P(("grp", "tp"), None, None), check_vma=False
    )
```

```python
import functools
import math

import jax
import jax.numpy as jnp
import numpy as np
from jax import lax
from jax.experimental import pallas as pl
from jax.experimental.pallas import tpu as pltpu
from jax.sharding import PartitionSpec as P

HD = 128
KVH = 4
BLK = 128


rope_base = 1000000.0
norm_eps = 1e-06


def normalize(token_rows, input_gain):
    values = token_rows.astype(jnp.float32)
    row_scale = lax.rsqrt(jnp.mean(values * values, axis=-1, keepdims=True) + norm_eps)
    return (values * row_scale * input_gain).astype(jnp.bfloat16)


def finish(projected, positions, valid, key_gain):
    key_width = KVH * HD
    half_dim = HD // 2
    row_count = projected.shape[0]
    key_part = projected[:, :key_width].reshape(row_count, KVH, HD)
    key_scale = lax.rsqrt(jnp.mean(key_part * key_part, axis=-1, keepdims=True) + norm_eps)
    key_part = key_part * key_scale * key_gain
    exponent = jnp.arange(half_dim, dtype=jnp.float32) * (2.0 / HD)
    inverse = jnp.exp(exponent * -math.log(rope_base))
    angles = positions.astype(jnp.float32)[:, None] * inverse[None, :]
    cosine = jnp.cos(angles)[:, None, :]
    sine_part = jnp.sin(angles)[:, None, :]
    lower_half = key_part[..., :half_dim]
    upper_half = key_part[..., half_dim:]
    turned = jnp.concatenate(
        [
            lower_half * cosine - upper_half * sine_part,
            upper_half * cosine + lower_half * sine_part,
        ],
        axis=-1,
    )
    merged = jnp.concatenate(
        [turned.reshape(row_count, key_width), projected[:, key_width:]], axis=-1
    )
    return jnp.where(valid[:, None], merged, 0.0).astype(jnp.bfloat16)


def project(normed, kv_weight):
    all_rows = lax.all_gather(kv_weight, "grp", axis=0, tiled=True)
    return jnp.dot(
        normed,
        lax.all_gather(all_rows, "tp", axis=1, tiled=True),
        preferred_element_type=jnp.float32,
    )


def pages_per_device(tp_count, own_blocks):
    live_tokens = 2 * tp_count * own_blocks * BLK // 5
    return ((live_tokens + BLK - 1) // BLK + 2 * tp_count - 2) // tp_count


def general(hidden, lengths, kv_weight, input_gain, key_gain):
    tp_count = lax.axis_size("tp")
    my_index = lax.axis_index("tp")
    own_blocks = hidden.shape[0] // BLK
    page_count = pages_per_device(tp_count, own_blocks)
    per_peer = (own_blocks + tp_count - 1) // tp_count
    cache_width = 2 * KVH * HD
    group_len = lengths[0]
    block_counts = (group_len + (BLK - 1)) // BLK
    block_ends = jnp.cumsum(block_counts)
    block_starts = block_ends - block_counts
    offsets = jnp.arange(BLK, dtype=jnp.int32)
    my_start = block_starts[my_index]
    my_count = block_counts[my_index]
    my_length = group_len[my_index]
    outbound = (
        jnp.arange(tp_count, dtype=jnp.int32)[:, None] - my_start
    ) % tp_count + tp_count * jnp.arange(per_peer, dtype=jnp.int32)[None, :]
    outbound = outbound.reshape(-1)
    sending = outbound < my_count
    picked_local = jnp.minimum(outbound, own_blocks - 1)
    page_ranks = tp_count * jnp.arange(page_count, dtype=jnp.int32) + my_index
    anchor = jnp.minimum(
        jnp.sum((block_ends[None, :] <= page_ranks[:, None]).astype(jnp.int32), axis=1),
        tp_count - 1,
    )
    block_index = page_ranks - block_starts[anchor]
    page_live = page_ranks < block_ends[-1]
    chosen = anchor * per_peer + jnp.clip(block_index // tp_count, 0, per_peer - 1)
    projected = project(normalize(hidden, input_gain), kv_weight)
    own_pos = (jnp.arange(own_blocks, dtype=jnp.int32)[:, None] * BLK + offsets[None, :]).reshape(
        -1
    )
    own_cache = finish(projected, own_pos, own_pos < my_length, key_gain).reshape(
        own_blocks, BLK, cache_width
    )
    outgoing = jnp.where(
        sending[:, None, None],
        jnp.take(own_cache, picked_local, axis=0),
        jnp.zeros((), jnp.bfloat16),
    )
    arrived = lax.all_to_all(outgoing, "tp", split_axis=0, concat_axis=0, tiled=True)
    cache_pages = jnp.take(arrived, chosen, axis=0)
    return jnp.where(page_live[:, None, None], cache_pages, jnp.zeros((), jnp.bfloat16))


flip0 = [(i, i ^ 1) for i in range(4)]
flip1 = [(i, i ^ 2) for i in range(4)]


def sides(shard):
    return lax.ppermute(shard, "grp", flip0), lax.ppermute(shard, "grp", flip1)


def opposite(side_pairs):
    half = side_pairs[0][0].shape[0] // 2
    first = jnp.concatenate([side0[:half] for side0, _ in side_pairs])
    second = jnp.concatenate([side1[half:] for _, side1 in side_pairs])
    return lax.ppermute(first, "grp", flip1), lax.ppermute(second, "grp", flip0)


def scale_kernel(lengths_ref, place_ref, x_ref, out_ref, x_buf, x_sem):
    count = (lengths_ref[place_ref[1]] + (BLK - 1)) // BLK

    def copy_of(block):
        rows = pl.ds(pl.multiple_of(block * BLK, BLK), BLK)
        return pltpu.make_async_copy(x_ref.at[rows], x_buf.at[rows], x_sem.at[block])

    def fetch(block, carry):
        copy_of(block).start()
        return carry

    def one_block(block, carry):
        copy_of(block).wait()
        rows = pl.ds(pl.multiple_of(block * BLK, BLK), BLK)
        squares = jnp.zeros((BLK, HD), jnp.float32)
        for cut in range(0, x_buf.shape[1], HD):
            values = x_buf[rows, cut : cut + HD].astype(jnp.float32)
            squares = squares + values * values
        mean = jnp.sum(squares, axis=-1, keepdims=True) / x_buf.shape[1]
        out_ref[rows, :] = jnp.broadcast_to(lax.rsqrt(mean + norm_eps), (BLK, HD))
        return carry

    lax.fori_loop(0, count, fetch, 0)
    lax.fori_loop(0, count, one_block, 0)


def row_scales(lengths, place, hidden):
    rows, width = hidden.shape
    small = pl.BlockSpec(memory_space=pltpu.SMEM)
    return pl.pallas_call(
        scale_kernel,
        in_specs=[small, small, pl.BlockSpec(memory_space=pl.ANY)],
        out_specs=pl.BlockSpec(memory_space=pltpu.VMEM),
        out_shape=jax.ShapeDtypeStruct((rows, HD), jnp.float32),
        scratch_shapes=[
            pltpu.VMEM((rows, width), hidden.dtype),
            pltpu.SemaphoreType.DMA((rows // BLK,)),
        ],
        compiler_params=pltpu.CompilerParams(vmem_limit_bytes=54 << 20),
        cost_estimate=pl.CostEstimate(
            flops=3 * rows * width, bytes_accessed=2 * rows * width, transcendentals=0
        ),
        name="row_scales",
    )(lengths, place, hidden)


def chip_facts(lengths_ref, chip):
    first = jnp.int32(0)
    for index in range(lengths_ref.shape[0]):
        count = (lengths_ref[index] + (BLK - 1)) // BLK
        first = first + jnp.where(index < 2 * chip, count, 0)
    return first, lengths_ref[2 * chip], lengths_ref[2 * chip + 1]


def project_kernel(slot_ids, tile, depth, deep, *refs):
    count = len(slot_ids)
    lengths_ref, place_ref, own_ref, sib_ref = refs[:4]
    near = refs[4 : 4 + 3 * count]
    far = refs[4 + 3 * count : 6 + 3 * count]
    turn_ref, gain_ref, own_scale, sib_scale, out_ref, over_ref = refs[6 + 3 * count : 12 + 3 * count]
    x_buf, w_buf, o_buf, x_sem, w_sem, o_sem = refs[12 + 3 * count :]
    tp_count = lengths_ref.shape[0]
    ahead = x_buf.shape[0]
    group, me = place_ref[0], place_ref[1]
    chip, core = me // 2, me % 2
    first, length0, length1 = chip_facts(lengths_ref, chip)
    count0 = (length0 + (BLK - 1)) // BLK
    own_len = jnp.where(core == 0, length0, length1)
    sib_len = jnp.where(core == 0, length1, length0)
    own_count = (own_len + (BLK - 1)) // BLK
    total = own_count + (sib_len + (BLK - 1)) // BLK
    tiles = (total + (tile - 1)) // tile

    def within(i):
        return jnp.where(i < own_count, i, i - own_count)

    def fetch(step, start):
        slot = lax.rem(step, ahead)
        for part in range(tile):
            i = step * tile + part
            rows = pl.ds(pl.multiple_of(within(i) * BLK, BLK), BLK)
            target = x_buf.at[slot, pl.ds(part * BLK, BLK)]

            @pl.when(i < own_count)
            def _():
                copy = pltpu.make_async_copy(own_ref.at[rows], target, x_sem.at[slot, part])
                copy.start() if start else copy.wait()

            @pl.when(jnp.logical_and(i >= own_count, i < total))
            def _():
                copy = pltpu.make_async_copy(sib_ref.at[rows], target, x_sem.at[slot, part])
                copy.start() if start else copy.wait()

    copies = []
    half = depth // 2
    for index in range(count):
        parts = [(near[3 * index + flip], flip, 0) for flip in range(3)]
        parts += [(far[side].at[pl.ds(index * half, half)], 3, side * half) for side in range(2)]
        for part, (source, flip, offset) in enumerate(parts):
            rows = pl.ds(pl.multiple_of((group ^ flip) * depth + offset, 16), source.shape[0])
            copies.append(
                pltpu.make_async_copy(
                    source, w_buf.at[rows, pl.ds(index * HD, HD)], w_sem.at[5 * index + part]
                )
            )
    fetch(jnp.int32(0), True)
    for copy in copies:
        copy.start()
    for step in range(1, ahead - 1):
        fetch(jnp.int32(step), True)
    for copy in copies:
        copy.wait()

    is_key = [2 * (chip ^ slot) + core < KVH for slot in slot_ids]

    def send(i, start):
        second = jnp.where(i < own_count, core, 1 - core)
        place = within(i) + second * count0

        @pl.when(jnp.logical_and(i < total, place < deep * tp_count))
        def _():
            target = out_ref.at[lax.rem(first + place, tp_count), place // tp_count]
            copy = pltpu.make_async_copy(o_buf.at[i], target, o_sem.at[i])
            copy.start() if start else copy.wait()

        @pl.when(jnp.logical_and(i < total, place >= deep * tp_count))
        def _():
            target = over_ref.at[place - deep * tp_count]
            copy = pltpu.make_async_copy(o_buf.at[i], target, o_sem.at[i])
            copy.start() if start else copy.wait()

    def finish_tile(step, product):
        for part in range(tile):
            i = jnp.minimum(step * tile + part, total - 1)
            rows = pl.ds(pl.multiple_of(within(i) * BLK, BLK), BLK)
            limit = jnp.where(i < own_count, own_len, sib_len) - within(i) * BLK
            valid = lax.broadcasted_iota(jnp.int32, (BLK, HD), 0) < limit
            scale = jnp.where(i < own_count, own_scale[rows, :], sib_scale[rows, :])
            for index in range(count):
                cut = product[part * BLK : (part + 1) * BLK, index * HD : (index + 1) * HD]
                values = cut * scale
                key_scale = lax.rsqrt(jnp.mean(values * values, axis=-1, keepdims=True) + norm_eps)
                keys = values * key_scale * gain_ref[...]
                turned = keys * turn_ref[rows, :HD] + pltpu.roll(keys, HD // 2, 1) * turn_ref[rows, HD:]
                merged = jnp.where(jnp.logical_and(valid, is_key[index]), turned, jnp.where(valid, values, 0.0))
                o_buf[step * tile + part, index] = merged.astype(jnp.bfloat16)

    def send_tile(step):
        for part in range(tile):
            send(step * tile + part, True)

    def one_tile(step, product):
        fetch(step + (ahead - 1), True)
        fetch(step, False)
        following = jnp.dot(x_buf[lax.rem(step, ahead)], w_buf[...], preferred_element_type=jnp.float32)
        finish_tile(step - 1, product)
        send_tile(step - 1)
        return following

    fetch(jnp.int32(ahead - 1), True)
    fetch(jnp.int32(0), False)
    product = jnp.dot(x_buf[0], w_buf[...], preferred_element_type=jnp.float32)
    product = lax.fori_loop(1, tiles, one_tile, product)
    finish_tile(tiles - 1, product)
    send_tile(tiles - 1)

    def drain(i, carry):
        send(i, False)
        return carry

    lax.fori_loop(0, total, drain, 0)


def project_slots(slot_ids, lengths, place, own, sibling, near, far, scales, turn, key_gain, deep):
    rows, width = own.shape
    tp_count = lengths.shape[0]
    own_blocks = rows // BLK
    depth = near[0][0].shape[0]
    count = len(slot_ids)
    tile = max(t for t in (1, 2, 3) if own_blocks % t == 0)
    ahead = 3
    spare = 2 * own_blocks - deep * tp_count
    anywhere = pl.BlockSpec(memory_space=pl.ANY)
    whole = pl.BlockSpec(memory_space=pltpu.VMEM)
    pieces = [piece for parts in near for piece in parts] + list(far)
    out_specs = [anywhere, anywhere]
    out_shape = [
        jax.ShapeDtypeStruct((tp_count, deep, count, BLK, HD), jnp.bfloat16),
        jax.ShapeDtypeStruct((max(spare, 1), count, BLK, HD), jnp.bfloat16),
    ]
    return pl.pallas_call(
        functools.partial(project_kernel, slot_ids, tile, depth, deep),
        in_specs=[pl.BlockSpec(memory_space=pltpu.SMEM)] * 2
        + [anywhere] * (2 + len(pieces))
        + [whole] * 4,
        out_specs=out_specs,
        out_shape=out_shape,
        scratch_shapes=[
            pltpu.VMEM((ahead, tile * BLK, width), jnp.bfloat16),
            pltpu.VMEM((width, count * HD), jnp.bfloat16),
            pltpu.VMEM((2 * own_blocks + tile, count, BLK, HD), jnp.bfloat16),
            pltpu.SemaphoreType.DMA((ahead, tile)),
            pltpu.SemaphoreType.DMA((5 * count,)),
            pltpu.SemaphoreType.DMA((2 * own_blocks,)),
        ],
        compiler_params=pltpu.CompilerParams(vmem_limit_bytes=54 << 20),
        cost_estimate=pl.CostEstimate(
            flops=4 * rows * width * count * HD,
            bytes_accessed=4 * rows * width + 2 * width * count * HD,
            transcendentals=0,
        ),
        name="project_slots",
    )(lengths, place, own, sibling, *pieces, turn, key_gain, *scales)


def page_source(lengths_ref, place_ref, page):
    tp_count = lengths_ref.shape[0]
    rank = page * tp_count + place_ref[1]
    end, chip, first = jnp.int32(0), jnp.int32(0), jnp.int32(0)
    for index in range(tp_count):
        end = end + (lengths_ref[index] + (BLK - 1)) // BLK
        if index % 2 == 1 and index + 1 < tp_count:
            passed = end <= rank
            chip = jnp.where(passed, index // 2 + 1, chip)
            first = jnp.where(passed, end, first)
    return rank < end, chip, rank - first


def assemble_kernel(groups, tp_count, deep, lengths_ref, place_ref, *refs):
    out_ref = refs[-1]
    live, chip, within = page_source(lengths_ref, place_ref, pl.program_id(0))
    over = within >= deep * tp_count
    spilled = refs[2 * len(groups) : -1]
    my_core = place_ref[1] % 2

    @pl.when(live)
    def _():
        for order, slot_ids in enumerate(groups):
            for core in range(2):
                for index, slot in enumerate(slot_ids):
                    column = 2 * (chip ^ slot) + core
                    target = pl.ds(pl.multiple_of(column * HD, HD), HD)
                    block = refs[2 * order + core][0, 0, index]
                    if spilled:
                        same, other = spilled
                        late = jnp.where(my_core == core, same[0, 0, slot], other[0, 0, slot])
                        block = jnp.where(over, late, block)
                    out_ref[0, :, target] = block

    @pl.when(jnp.logical_not(live))
    def _():
        out_ref[...] = jnp.zeros_like(out_ref)


def assemble(groups, lengths, place, arrived, spilled, page_count, deep):
    tp_count = lengths.shape[0]
    operands, specs = [], []

    def regular(core):
        def index_map(page, lengths_ref, place_ref):
            _, chip, within = page_source(lengths_ref, place_ref, page)
            return 2 * chip + core, jnp.clip(within // tp_count, 0, deep - 1), 0, 0, 0

        return index_map

    def late(page, lengths_ref, place_ref):
        _, chip, within = page_source(lengths_ref, place_ref, page)
        spare = spilled[0].shape[1]
        return chip ^ (place_ref[1] // 2), jnp.clip(within - deep * tp_count, 0, spare - 1), 0, 0, 0

    for order, slot_ids in enumerate(groups):
        for core in range(2):
            operands.append(arrived[order])
            specs.append(pl.BlockSpec((1, 1, len(slot_ids), BLK, HD), regular(core)))
    for part in spilled:
        operands.append(part)
        specs.append(pl.BlockSpec((1, 1) + part.shape[2:], late))
    return pl.pallas_call(
        functools.partial(assemble_kernel, groups, tp_count, deep),
        grid_spec=pltpu.PrefetchScalarGridSpec(
            num_scalar_prefetch=2,
            grid=(page_count,),
            in_specs=specs,
            out_specs=pl.BlockSpec((1, BLK, 2 * KVH * HD), lambda page, *_: (page, 0, 0)),
        ),
        out_shape=jax.ShapeDtypeStruct((page_count, BLK, 2 * KVH * HD), jnp.bfloat16),
        compiler_params=pltpu.CompilerParams(vmem_limit_bytes=24 << 20),
        name="assemble",
    )(lengths, place, *operands)


def rope_table(rows):
    inverse = np.exp(np.arange(HD // 2) * (-2.0 * math.log(rope_base) / HD))
    angles = np.arange(rows)[:, None] * inverse[None, :]
    cosine, sine_part = np.cos(angles), np.sin(angles)
    return jnp.asarray(np.concatenate([cosine, cosine, -sine_part, sine_part], axis=1), jnp.float32)


def exchange(sent):
    return lax.all_to_all(sent, "tp", split_axis=0, concat_axis=0, tiled=True)


def paired(hidden, lengths, kv_weight, input_gain, key_gain):
    tp_count = lax.axis_size("tp")
    nz = tp_count // 2
    group, me = lax.axis_index("grp"), lax.axis_index("tp")
    rows = hidden.shape[0]
    own_blocks = rows // BLK
    depth = kv_weight.shape[0]
    deep = 2 * own_blocks // tp_count
    page_count = pages_per_device(tp_count, own_blocks)
    group_len = lengths[0]
    place = jnp.stack([group, me]).astype(jnp.int32)
    swap = [(i, i ^ 1) for i in range(tp_count)]

    own_gain = lax.dynamic_slice(input_gain, (group * depth,), (depth,))
    shard = (kv_weight.astype(jnp.float32) * own_gain[:, None]).astype(jnp.bfloat16)
    sibling = lax.ppermute(hidden, "tp", swap)
    gain = key_gain.reshape(1, HD)

    def from_chip(flip, own):
        return lax.ppermute(own, "tp", [(i, i ^ (2 * flip)) for i in range(tp_count)])

    def project_group(slot_ids, near, far):
        return project_slots(
            slot_ids, group_len, place, hidden, sibling, near, far, (scale, other_scale), turn, gain, deep
        )

    groups = [tuple(range(start, min(start + 2, nz))) for start in range(0, nz, 2)]
    turn = rope_table(rows)
    slots = [shard] + [None] * (nz - 1)
    slots[1] = from_chip(1, shard)
    side0 = sides(shard)
    early = range(2, min(3, nz))
    for flip in early:
        slots[flip] = from_chip(flip, shard)
    scale = row_scales(group_len, place, hidden)
    slots[1], side0, scale, shard = lax.optimization_barrier((slots[1], side0, scale, shard))
    side1 = sides(slots[1])
    for flip in range(early.stop, nz):
        slots[flip] = from_chip(flip, shard)
    middle = slots[early.start : early.stop]
    side1, scale, sibling, middle = lax.optimization_barrier((side1, scale, sibling, middle))
    slots[early.start : early.stop] = middle
    other_scale = lax.ppermute(scale, "tp", swap)
    far = opposite([side0, side1])
    near = [(slots[0],) + side0, (slots[1],) + side1]
    far, other_scale, slots = lax.optimization_barrier((far, other_scale, slots))
    sent, rest = project_group(groups[0], near, far)
    arrived, over = [], [rest]
    for slot_ids in groups[1:]:
        crossed = sides(jnp.concatenate([slots[slot] for slot in slot_ids]))
        arrived.append(exchange(sent))
        crossed, over[-1] = lax.optimization_barrier((crossed, over[-1]))
        near = []
        for index, slot in enumerate(slot_ids):
            cut = slice(index * depth, (index + 1) * depth)
            near.append((slots[slot], crossed[0][cut], crossed[1][cut]))
        far = opposite([pair[1:] for pair in near])
        sent, rest = project_group(slot_ids, near, far)
        over.append(rest)
    arrived.append(exchange(sent))

    def plain(operands):
        return assemble(groups, group_len, place, operands[0], (), page_count, deep)

    if 2 * own_blocks == deep * tp_count:
        return plain((arrived, over))

    def spilling(operands):
        mine = jnp.concatenate(operands[1], axis=1)
        along = [mine]
        for flip in range(2, tp_count, 2):
            along.append(lax.ppermute(mine, "tp", [(i, i ^ flip) for i in range(tp_count)]))
        along = jnp.stack(along)
        other = lax.ppermute(along, "tp", swap)
        spilled = along, other
        return assemble(groups, group_len, place, operands[0], spilled, page_count, deep)

    counts = (group_len + (BLK - 1)) // BLK
    most = jnp.max(counts[0::2] + counts[1::2])
    return lax.cond(most > deep * tp_count, spilling, plain, (arrived, over))


def local(hidden, lengths, kv_weight, input_gain, key_gain):
    tp_count = lax.axis_size("tp")
    fits = (
        lax.axis_size("grp") == 4
        and tp_count >= 4
        and tp_count & (tp_count - 1) == 0
        and kv_weight.shape[1] == HD
        and kv_weight.shape[0] % 256 == 0
        and 2 * (hidden.shape[0] // BLK) >= tp_count
    )
    chosen = paired if fits else general
    return chosen(hidden, lengths, kv_weight, input_gain, key_gain)


def solution(mesh):
    placed = (P(("grp", "tp"), None), P("grp", None), P("grp", "tp"), P(), P())
    return jax.shard_map(
        local, mesh=mesh, in_specs=placed, out_specs=P(("grp", "tp"), None, None), check_vma=False
    )
```

```python
import functools
import math

import jax
import jax.numpy as jnp
import numpy as np
from jax import lax
from jax.experimental import pallas as pl
from jax.experimental.pallas import tpu as pltpu
from jax.sharding import PartitionSpec as P

HD = 128
KVH = 4
BLK = 128


rope_base = 1000000.0
norm_eps = 1e-06


def normalize(token_rows, input_gain):
    values = token_rows.astype(jnp.float32)
    row_scale = lax.rsqrt(jnp.mean(values * values, axis=-1, keepdims=True) + norm_eps)
    return (values * row_scale * input_gain).astype(jnp.bfloat16)


def finish(projected, positions, valid, key_gain):
    key_width = KVH * HD
    half_dim = HD // 2
    row_count = projected.shape[0]
    key_part = projected[:, :key_width].reshape(row_count, KVH, HD)
    key_scale = lax.rsqrt(jnp.mean(key_part * key_part, axis=-1, keepdims=True) + norm_eps)
    key_part = key_part * key_scale * key_gain
    exponent = jnp.arange(half_dim, dtype=jnp.float32) * (2.0 / HD)
    inverse = jnp.exp(exponent * -math.log(rope_base))
    angles = positions.astype(jnp.float32)[:, None] * inverse[None, :]
    cosine = jnp.cos(angles)[:, None, :]
    sine_part = jnp.sin(angles)[:, None, :]
    lower_half = key_part[..., :half_dim]
    upper_half = key_part[..., half_dim:]
    turned = jnp.concatenate(
        [
            lower_half * cosine - upper_half * sine_part,
            upper_half * cosine + lower_half * sine_part,
        ],
        axis=-1,
    )
    merged = jnp.concatenate(
        [turned.reshape(row_count, key_width), projected[:, key_width:]], axis=-1
    )
    return jnp.where(valid[:, None], merged, 0.0).astype(jnp.bfloat16)


def project(normed, kv_weight):
    all_rows = lax.all_gather(kv_weight, "grp", axis=0, tiled=True)
    return jnp.dot(
        normed,
        lax.all_gather(all_rows, "tp", axis=1, tiled=True),
        preferred_element_type=jnp.float32,
    )


def pages_per_device(tp_count, own_blocks):
    live_tokens = 2 * tp_count * own_blocks * BLK // 5
    return ((live_tokens + BLK - 1) // BLK + 2 * tp_count - 2) // tp_count


def general(hidden, lengths, kv_weight, input_gain, key_gain):
    tp_count = lax.axis_size("tp")
    my_index = lax.axis_index("tp")
    own_blocks = hidden.shape[0] // BLK
    page_count = pages_per_device(tp_count, own_blocks)
    per_peer = (own_blocks + tp_count - 1) // tp_count
    cache_width = 2 * KVH * HD
    group_len = lengths[0]
    block_counts = (group_len + (BLK - 1)) // BLK
    block_ends = jnp.cumsum(block_counts)
    block_starts = block_ends - block_counts
    offsets = jnp.arange(BLK, dtype=jnp.int32)
    my_start = block_starts[my_index]
    my_count = block_counts[my_index]
    my_length = group_len[my_index]
    outbound = (
        jnp.arange(tp_count, dtype=jnp.int32)[:, None] - my_start
    ) % tp_count + tp_count * jnp.arange(per_peer, dtype=jnp.int32)[None, :]
    outbound = outbound.reshape(-1)
    sending = outbound < my_count
    picked_local = jnp.minimum(outbound, own_blocks - 1)
    page_ranks = tp_count * jnp.arange(page_count, dtype=jnp.int32) + my_index
    anchor = jnp.minimum(
        jnp.sum((block_ends[None, :] <= page_ranks[:, None]).astype(jnp.int32), axis=1),
        tp_count - 1,
    )
    block_index = page_ranks - block_starts[anchor]
    page_live = page_ranks < block_ends[-1]
    chosen = anchor * per_peer + jnp.clip(block_index // tp_count, 0, per_peer - 1)
    projected = project(normalize(hidden, input_gain), kv_weight)
    own_pos = (jnp.arange(own_blocks, dtype=jnp.int32)[:, None] * BLK + offsets[None, :]).reshape(
        -1
    )
    own_cache = finish(projected, own_pos, own_pos < my_length, key_gain).reshape(
        own_blocks, BLK, cache_width
    )
    outgoing = jnp.where(
        sending[:, None, None],
        jnp.take(own_cache, picked_local, axis=0),
        jnp.zeros((), jnp.bfloat16),
    )
    arrived = lax.all_to_all(outgoing, "tp", split_axis=0, concat_axis=0, tiled=True)
    cache_pages = jnp.take(arrived, chosen, axis=0)
    return jnp.where(page_live[:, None, None], cache_pages, jnp.zeros((), jnp.bfloat16))


flip0 = [(i, i ^ 1) for i in range(4)]
flip1 = [(i, i ^ 2) for i in range(4)]


def sides(shard):
    return lax.ppermute(shard, "grp", flip0), lax.ppermute(shard, "grp", flip1)


def opposite(first_side0, second_side1):
    return lax.ppermute(first_side0, "grp", flip1), lax.ppermute(second_side1, "grp", flip0)


def stay(array):
    return pltpu.with_memory_space_constraint(array, pltpu.HBM)


def scale_kernel(lengths_ref, place_ref, x_ref, out_ref, x_buf, x_sem):
    count = (lengths_ref[place_ref[1]] + (BLK - 1)) // BLK

    def copy_of(block):
        rows = pl.ds(pl.multiple_of(block * BLK, BLK), BLK)
        return pltpu.make_async_copy(x_ref.at[rows], x_buf.at[rows], x_sem.at[block])

    def fetch(block, carry):
        copy_of(block).start()
        return carry

    def one_block(block, carry):
        copy_of(block).wait()
        rows = pl.ds(pl.multiple_of(block * BLK, BLK), BLK)
        squares = jnp.zeros((BLK, HD), jnp.float32)
        for cut in range(0, x_buf.shape[1], HD):
            values = x_buf[rows, cut : cut + HD].astype(jnp.float32)
            squares = squares + values * values
        mean = jnp.sum(squares, axis=-1, keepdims=True) / x_buf.shape[1]
        out_ref[rows, :] = jnp.broadcast_to(lax.rsqrt(mean + norm_eps), (BLK, HD))
        return carry

    lax.fori_loop(0, count, fetch, 0)
    lax.fori_loop(0, count, one_block, 0)


def row_scales(lengths, place, hidden):
    rows, width = hidden.shape
    small = pl.BlockSpec(memory_space=pltpu.SMEM)
    return pl.pallas_call(
        scale_kernel,
        in_specs=[small, small, pl.BlockSpec(memory_space=pltpu.HBM)],
        out_specs=pl.BlockSpec(memory_space=pltpu.VMEM),
        out_shape=jax.ShapeDtypeStruct((rows, HD), jnp.float32),
        scratch_shapes=[
            pltpu.VMEM((rows, width), hidden.dtype),
            pltpu.SemaphoreType.DMA((rows // BLK,)),
        ],
        compiler_params=pltpu.CompilerParams(vmem_limit_bytes=16 << 20),
        cost_estimate=pl.CostEstimate(
            flops=3 * rows * width, bytes_accessed=2 * rows * width, transcendentals=0
        ),
        name="row_scales",
    )(lengths, place, stay(hidden))


def tile_blocks(own_blocks):
    return max(t for t in (1, 2, 3) if own_blocks % t == 0)


class Chip:
    def __init__(self, lengths_ref, place_ref):
        self.tp_count = lengths_ref.shape[0]
        self.group, me = place_ref[0], place_ref[1]
        self.chip, self.core = me // 2, me % 2
        self.first = jnp.int32(0)
        for index in range(self.tp_count):
            count = (lengths_ref[index] + (BLK - 1)) // BLK
            self.first = self.first + jnp.where(index < 2 * self.chip, count, 0)
        length0, length1 = lengths_ref[2 * self.chip], lengths_ref[2 * self.chip + 1]
        self.count0 = (length0 + (BLK - 1)) // BLK
        self.own_len = jnp.where(self.core == 0, length0, length1)
        self.sib_len = jnp.where(self.core == 0, length1, length0)
        self.own_count = (self.own_len + (BLK - 1)) // BLK
        self.total = self.own_count + (self.sib_len + (BLK - 1)) // BLK

    def within(self, i):
        return jnp.where(i < self.own_count, i, i - self.own_count)

    def rows(self, i):
        return pl.ds(pl.multiple_of(self.within(i) * BLK, BLK), BLK)

    def fetch(self, i, own_ref, sib_ref, x_buf, x_sem, flips, depth, start):
        target = pl.ds(pl.multiple_of(i * BLK, BLK), BLK)

        def copies(source):
            for order, flip in enumerate(flips):
                columns = pl.ds(pl.multiple_of((self.group ^ flip) * depth, HD), depth)
                copy = pltpu.make_async_copy(
                    source.at[self.rows(i), columns],
                    x_buf.at[target, pl.ds(order * depth, depth)],
                    x_sem.at[i, order],
                )
                copy.start() if start else copy.wait()

        pl.when(i < self.own_count)(lambda: copies(own_ref))
        pl.when(jnp.logical_and(i >= self.own_count, i < self.total))(lambda: copies(sib_ref))

    def fetch_all(self, *args):
        def one_block(i, carry):
            self.fetch(i, *args, True)
            return carry

        lax.fori_loop(0, self.total, one_block, 0)


def near_kernel(tile, depth, pieces, *refs):
    lengths_ref, place_ref, own_ref, sib_ref = refs[:4]
    partial_ref, x_buf, w_buf, x_sem, w_sem = refs[-5:]
    near = refs[4:-5]
    chip = Chip(lengths_ref, place_ref)
    span = tile * BLK
    copies = [
        pltpu.make_async_copy(
            near[source].at[pl.ds(row, depth)],
            w_buf.at[pl.ds(part % 3 * depth, depth), pl.ds(part // 3 * HD, HD)],
            w_sem.at[part],
        )
        for part, (source, row) in enumerate(pieces)
    ]
    for copy in copies:
        copy.start()
    fetch = own_ref, sib_ref, x_buf, x_sem, (0, 1, 2), depth
    chip.fetch_all(*fetch)
    for copy in copies:
        copy.wait()

    def one_tile(step, carry):
        for part in range(tile):
            chip.fetch(step * tile + part, *fetch, False)
        rows = pl.ds(pl.multiple_of(step * span, span), span)
        partial_ref[rows, :] = jnp.dot(x_buf[rows, :], w_buf[...], preferred_element_type=jnp.float32)
        return carry

    lax.fori_loop(0, (chip.total + (tile - 1)) // tile, one_tile, 0)


def project_near(lengths, place, own, sibling, arrays, pieces, depth):
    rows, width = own.shape
    tile = tile_blocks(rows // BLK)
    columns = len(pieces) // 3 * HD
    small = pl.BlockSpec(memory_space=pltpu.SMEM)
    anywhere = pl.BlockSpec(memory_space=pl.ANY)
    in_hbm = pl.BlockSpec(memory_space=pltpu.HBM)
    held = 2 * rows + tile * BLK
    return pl.pallas_call(
        functools.partial(near_kernel, tile, depth, pieces),
        in_specs=[small] * 2 + [in_hbm] * 2 + [anywhere] * len(arrays),
        out_specs=pl.BlockSpec(memory_space=pltpu.VMEM),
        out_shape=jax.ShapeDtypeStruct((held, columns), jnp.float32),
        scratch_shapes=[
            pltpu.VMEM((held, 3 * depth), own.dtype),
            pltpu.VMEM((3 * depth, columns), jnp.bfloat16),
            pltpu.SemaphoreType.DMA((2 * rows // BLK, 3)),
            pltpu.SemaphoreType.DMA((len(pieces),)),
        ],
        compiler_params=pltpu.CompilerParams(vmem_limit_bytes=34 << 20),
        cost_estimate=pl.CostEstimate(
            flops=24 * rows * depth * columns, bytes_accessed=24 * rows * depth, transcendentals=0
        ),
        name="project_near",
    )(lengths, place, stay(own), stay(sibling), *arrays)


def far_kernel(slot_ids, tile, depth, deep, *refs):
    lengths_ref, place_ref, own_ref, sib_ref = refs[:4]
    far = refs[4:6]
    partial_ref, turn_ref, gain_ref, own_scale, sib_scale, out_ref, over_ref = refs[6:13]
    x_buf, w_buf, o_buf, x_sem, w_sem, o_sem = refs[13:]
    count = len(slot_ids)
    chip = Chip(lengths_ref, place_ref)
    tp_count, total, own_count = chip.tp_count, chip.total, chip.own_count
    tiles = (total + (tile - 1)) // tile
    span = tile * BLK
    copies = [
        pltpu.make_async_copy(far[index], w_buf.at[:, pl.ds(index * HD, HD)], w_sem.at[index])
        for index in range(count)
    ]
    for copy in copies:
        copy.start()
    fetch = own_ref, sib_ref, x_buf, x_sem, (3,), depth
    chip.fetch_all(*fetch)
    for copy in copies:
        copy.wait()
    is_key = [2 * (chip.chip ^ slot) + chip.core < KVH for slot in slot_ids]

    shift = tp_count.bit_length() - 1

    def send(i):
        second = jnp.where(i < own_count, chip.core, 1 - chip.core)
        place = chip.within(i) + second * chip.count0

        @pl.when(jnp.logical_and(i < total, place < deep * tp_count))
        def _():
            target = out_ref.at[(chip.first + place) & (tp_count - 1), lax.shift_right_logical(place, shift)]
            pltpu.make_async_copy(o_buf.at[i], target, o_sem.at[i]).start()

        @pl.when(jnp.logical_and(i < total, place >= deep * tp_count))
        def _():
            target = over_ref.at[place - deep * tp_count]
            pltpu.make_async_copy(o_buf.at[i], target, o_sem.at[i]).start()

    def multiply(step):
        for part in range(tile):
            chip.fetch(step * tile + part, *fetch, False)
        rows = pl.ds(pl.multiple_of(step * span, span), span)
        return partial_ref[rows, :] + jnp.dot(x_buf[rows, :], w_buf[...], preferred_element_type=jnp.float32)

    ones = jnp.full((HD, HD), 1.0 / HD, jnp.bfloat16)

    def head_mean(squares):
        high = squares.astype(jnp.bfloat16)
        low = (squares - high.astype(jnp.float32)).astype(jnp.bfloat16)
        return jnp.dot(high, ones, preferred_element_type=jnp.float32) + jnp.dot(
            low, ones, preferred_element_type=jnp.float32
        )

    def finish_tile(step, product):
        for part in range(tile):
            i = jnp.minimum(step * tile + part, total - 1)
            rows = chip.rows(i)
            limit = jnp.where(i < own_count, chip.own_len, chip.sib_len) - chip.within(i) * BLK
            valid = lax.broadcasted_iota(jnp.int32, (BLK, HD), 0) < limit
            scale = jnp.where(i < own_count, own_scale[rows, :], sib_scale[rows, :])
            for index in range(count):
                cut = product[part * BLK : (part + 1) * BLK, index * HD : (index + 1) * HD]
                values = cut * scale
                key_scale = lax.rsqrt(head_mean(values * values) + norm_eps)
                keys = values * key_scale * gain_ref[...]
                turned = keys * turn_ref[rows, :HD] + pltpu.roll(keys, HD // 2, 1) * turn_ref[rows, HD:]
                merged = jnp.where(jnp.logical_and(valid, is_key[index]), turned, jnp.where(valid, values, 0.0))
                o_buf[step * tile + part, index] = merged.astype(jnp.bfloat16)

    def send_tile(step):
        for part in range(tile):
            send(step * tile + part)

    def one_tile(step, product):
        following = multiply(step)
        finish_tile(step - 1, product)
        send_tile(step - 1)
        return following

    product = lax.fori_loop(1, tiles, one_tile, multiply(jnp.int32(0)))
    finish_tile(tiles - 1, product)
    send_tile(tiles - 1)

    def drain(i, carry):
        pltpu.make_async_copy(o_buf.at[i], out_ref.at[0, 0], o_sem.at[i]).wait()
        return carry

    lax.fori_loop(0, total, drain, 0)


def project_far(slot_ids, lengths, place, own, sibling, far, partial, scales, turn, key_gain, deep):
    rows, width = own.shape
    tp_count = lengths.shape[0]
    own_blocks = rows // BLK
    count = len(slot_ids)
    depth = far[0].shape[0]
    tile = tile_blocks(own_blocks)
    spare = 2 * own_blocks - deep * tp_count
    small = pl.BlockSpec(memory_space=pltpu.SMEM)
    anywhere = pl.BlockSpec(memory_space=pl.ANY)
    in_hbm = pl.BlockSpec(memory_space=pltpu.HBM)
    whole = pl.BlockSpec(memory_space=pltpu.VMEM)
    return pl.pallas_call(
        functools.partial(far_kernel, slot_ids, tile, depth, deep),
        in_specs=[small] * 2 + [in_hbm] * 2 + [anywhere] * 2 + [whole] * 5,
        out_specs=[anywhere, anywhere],
        out_shape=[
            jax.ShapeDtypeStruct((tp_count, deep, count, BLK, HD), jnp.bfloat16),
            jax.ShapeDtypeStruct((max(spare, 1), count, BLK, HD), jnp.bfloat16),
        ],
        scratch_shapes=[
            pltpu.VMEM((2 * rows + tile * BLK, depth), own.dtype),
            pltpu.VMEM((depth, count * HD), jnp.bfloat16),
            pltpu.VMEM((2 * own_blocks + tile, count, BLK, HD), jnp.bfloat16),
            pltpu.SemaphoreType.DMA((2 * own_blocks, 1)),
            pltpu.SemaphoreType.DMA((count,)),
            pltpu.SemaphoreType.DMA((2 * own_blocks + tile,)),
        ],
        compiler_params=pltpu.CompilerParams(vmem_limit_bytes=16 << 20),
        cost_estimate=pl.CostEstimate(
            flops=16 * rows * depth * count * HD, bytes_accessed=16 * rows * depth, transcendentals=0
        ),
        name="project_far",
    )(lengths, place, stay(own), stay(sibling), *far, partial, turn, key_gain, *scales)


def page_source(lengths_ref, place_ref, page):
    tp_count = lengths_ref.shape[0]
    rank = page * tp_count + place_ref[1]
    end, chip, first = jnp.int32(0), jnp.int32(0), jnp.int32(0)
    for index in range(tp_count):
        end = end + (lengths_ref[index] + (BLK - 1)) // BLK
        if index % 2 == 1 and index + 1 < tp_count:
            passed = end <= rank
            chip = jnp.where(passed, index // 2 + 1, chip)
            first = jnp.where(passed, end, first)
    return rank < end, chip, rank - first


def assemble_kernel(groups, deep, lengths_ref, place_ref, *refs):
    arrived = refs[: len(groups)]
    spilled = refs[len(groups) : -3]
    out_ref, o_buf, o_sem = refs[-3:]
    tp_count = lengths_ref.shape[0]
    me = place_ref[1]

    def copy_of(page):
        return pltpu.make_async_copy(o_buf.at[page], out_ref.at[page], o_sem.at[page])

    for page in range(o_buf.shape[0]):
        live, chip, within = page_source(lengths_ref, place_ref, page)
        over = within >= deep * tp_count

        def columns_of(slot, core):
            return pl.ds(pl.multiple_of((2 * (chip ^ slot) + core) * HD, HD), HD)

        @pl.when(jnp.logical_and(live, jnp.logical_not(over)))
        def _():
            for order, slot_ids in enumerate(groups):
                for core in range(2):
                    for index, slot in enumerate(slot_ids):
                        block = arrived[order][2 * chip + core, within // tp_count, index]
                        o_buf[page, :, columns_of(slot, core)] = block

        if spilled:

            @pl.when(jnp.logical_and(live, over))
            def _():
                late = within - deep * tp_count
                flip = chip ^ (me // 2)
                for slot in range(tp_count // 2):
                    o_buf[page, :, columns_of(slot, me % 2)] = spilled[0][flip, late, slot]
                    o_buf[page, :, columns_of(slot, 1 - me % 2)] = spilled[1][flip, late, slot]

        @pl.when(jnp.logical_not(live))
        def _():
            o_buf[page] = jnp.zeros(o_buf.shape[1:], o_buf.dtype)

        copy_of(page).start()
    for page in range(o_buf.shape[0]):
        copy_of(page).wait()


def assemble(groups, lengths, place, arrived, spilled, page_count, deep):
    small = pl.BlockSpec(memory_space=pltpu.SMEM)
    whole = pl.BlockSpec(memory_space=pltpu.VMEM)
    shape = (page_count, BLK, 2 * KVH * HD)
    return pl.pallas_call(
        functools.partial(assemble_kernel, groups, deep),
        in_specs=[small] * 2 + [whole] * (len(arrived) + len(spilled)),
        out_specs=pl.BlockSpec(memory_space=pltpu.HBM),
        out_shape=pltpu.HBM(shape, jnp.bfloat16),
        scratch_shapes=[pltpu.VMEM(shape, jnp.bfloat16), pltpu.SemaphoreType.DMA((page_count,))],
        compiler_params=pltpu.CompilerParams(vmem_limit_bytes=16 << 20),
        name="assemble",
    )(lengths, place, *arrived, *spilled)


def rope_table(rows):
    inverse = np.exp(np.arange(HD // 2) * (-2.0 * math.log(rope_base) / HD))
    angles = np.arange(rows)[:, None] * inverse[None, :]
    cosine, sine_part = np.cos(angles), np.sin(angles)
    return jnp.asarray(np.concatenate([cosine, cosine, -sine_part, sine_part], axis=1), jnp.float32)


def exchange(sent):
    return lax.all_to_all(sent, "tp", split_axis=0, concat_axis=0, tiled=True)


def paired(hidden, lengths, kv_weight, input_gain, key_gain):
    tp_count = lax.axis_size("tp")
    nz = tp_count // 2
    group, me = lax.axis_index("grp"), lax.axis_index("tp")
    rows = hidden.shape[0]
    own_blocks = rows // BLK
    depth = kv_weight.shape[0]
    deep = 2 * own_blocks // tp_count
    page_count = pages_per_device(tp_count, own_blocks)
    group_len = lengths[0]
    place = jnp.stack([group, me]).astype(jnp.int32)
    swap = [(i, i ^ 1) for i in range(tp_count)]

    own_gain = lax.dynamic_slice(input_gain, (group * depth,), (depth,))
    shard = (kv_weight.astype(jnp.float32) * own_gain[:, None]).astype(jnp.bfloat16)
    sibling = lax.ppermute(hidden, "tp", swap)
    gain = key_gain.reshape(1, HD)

    def from_chip(flip, own):
        return lax.ppermute(own, "tp", [(i, i ^ (2 * flip)) for i in range(tp_count)])

    def start_group(arrays, pieces):
        return project_near(group_len, place, hidden, sibling, arrays, pieces, depth)

    def end_group(slot_ids, far, partial):
        return project_far(
            slot_ids, group_len, place, hidden, sibling, far, partial, (scale, other_scale), turn, gain, deep
        )

    groups = [tuple(range(start, min(start + 2, nz))) for start in range(0, nz, 2)]
    turn = rope_table(rows)
    slots = [shard] + [None] * (nz - 1)
    line = nz == 4
    inward = [(2 + c, 4 + c) for c in range(2)] + [(4 + c, 2 + c) for c in range(2)]
    outward = [(2 + c, c) for c in range(2)] + [(4 + c, 6 + c) for c in range(2)]
    slots[1] = from_chip(1, shard)
    side0 = sides(shard)
    across = lax.ppermute(shard, "tp", inward) if line else shard
    slots[1], shard, across = lax.optimization_barrier((slots[1], shard, across))
    if line:
        passed = lax.ppermute(slots[1], "tp", inward), lax.ppermute(across, "tp", outward)
    else:
        slots[2:] = [from_chip(flip, shard) for flip in range(2, nz)]
    slots[1], side0, later_len = lax.optimization_barrier((slots[1], side0, group_len))
    side1 = sides(slots[1])
    scale = row_scales(later_len, place, hidden)
    last = lax.ppermute(passed[0], "tp", outward) if line else None
    side1, scale, sibling = lax.optimization_barrier((side1, scale, sibling))
    other_scale = lax.ppermute(scale, "tp", swap)
    far = opposite(side0[0], side1[1])
    partial = start_group([slots[0], *side0, slots[1], *side1], [(part, 0) for part in range(6)])
    if line:
        far, other_scale, last, partial = lax.optimization_barrier((far, other_scale, last, partial))
        inner = (me // 2 == 1) | (me // 2 == 2)
        slots[2:] = [jnp.where(inner, passed[0], passed[1]), jnp.where(inner, across, last)]
    else:
        far, other_scale, slots, partial = lax.optimization_barrier((far, other_scale, slots, partial))
    sent, rest = end_group(groups[0], far, partial)
    arrived, over = [], [rest]
    for slot_ids in groups[1:]:
        both = jnp.concatenate([slots[slot] for slot in slot_ids])
        crossed = sides(both)
        arrived.append(exchange(sent))
        crossed, over[-1] = lax.optimization_barrier((crossed, over[-1]))
        far = opposite(crossed[0][:depth], crossed[1][depth:])
        pieces = [(source, index * depth) for index in range(2) for source in range(3)]
        partial = start_group([both, *crossed], pieces)
        far, partial = lax.optimization_barrier((far, partial))
        sent, rest = end_group(slot_ids, far, partial)
        over.append(rest)
    arrived.append(exchange(sent))

    def plain(operands):
        return assemble(groups, group_len, place, operands[0], (), page_count, deep)

    if 2 * own_blocks == deep * tp_count:
        return plain((arrived, over))

    def spilling(operands):
        mine = jnp.concatenate(operands[1], axis=1)
        along = [mine]
        for flip in range(2, tp_count, 2):
            along.append(lax.ppermute(mine, "tp", [(i, i ^ flip) for i in range(tp_count)]))
        along = jnp.stack(along)
        other = lax.ppermute(along, "tp", swap)
        spilled = along, other
        return assemble(groups, group_len, place, operands[0], spilled, page_count, deep)

    counts = (group_len + (BLK - 1)) // BLK
    most = jnp.max(counts[0::2] + counts[1::2])
    return lax.cond(most > deep * tp_count, spilling, plain, (arrived, over))


def local(hidden, lengths, kv_weight, input_gain, key_gain):
    tp_count = lax.axis_size("tp")
    fits = (
        lax.axis_size("grp") == 4
        and tp_count >= 4
        and tp_count & (tp_count - 1) == 0
        and kv_weight.shape[1] == HD
        and kv_weight.shape[0] % 256 == 0
        and 2 * (hidden.shape[0] // BLK) >= tp_count
    )
    chosen = paired if fits else general
    return chosen(hidden, lengths, kv_weight, input_gain, key_gain)


def solution(mesh):
    placed = (P(("grp", "tp"), None), P("grp", None), P("grp", "tp"), P(), P())
    return jax.shard_map(
        local, mesh=mesh, in_specs=placed, out_specs=P(("grp", "tp"), None, None), check_vma=False
    )
```

```python
import functools
import math

import jax
import jax.numpy as jnp
import numpy as np
from jax import lax
from jax.experimental import pallas as pl
from jax.experimental.pallas import tpu as pltpu
from jax.sharding import PartitionSpec as P

HD = 128
KVH = 4
BLK = 128


rope_base = 1000000.0
norm_eps = 1e-06


def normalize(token_rows, input_gain):
    values = token_rows.astype(jnp.float32)
    row_scale = lax.rsqrt(jnp.mean(values * values, axis=-1, keepdims=True) + norm_eps)
    return (values * row_scale * input_gain).astype(jnp.bfloat16)


def finish(projected, positions, valid, key_gain):
    key_width = KVH * HD
    half_dim = HD // 2
    row_count = projected.shape[0]
    key_part = projected[:, :key_width].reshape(row_count, KVH, HD)
    key_scale = lax.rsqrt(jnp.mean(key_part * key_part, axis=-1, keepdims=True) + norm_eps)
    key_part = key_part * key_scale * key_gain
    exponent = jnp.arange(half_dim, dtype=jnp.float32) * (2.0 / HD)
    inverse = jnp.exp(exponent * -math.log(rope_base))
    angles = positions.astype(jnp.float32)[:, None] * inverse[None, :]
    cosine = jnp.cos(angles)[:, None, :]
    sine_part = jnp.sin(angles)[:, None, :]
    lower_half = key_part[..., :half_dim]
    upper_half = key_part[..., half_dim:]
    turned = jnp.concatenate(
        [
            lower_half * cosine - upper_half * sine_part,
            upper_half * cosine + lower_half * sine_part,
        ],
        axis=-1,
    )
    merged = jnp.concatenate(
        [turned.reshape(row_count, key_width), projected[:, key_width:]], axis=-1
    )
    return jnp.where(valid[:, None], merged, 0.0).astype(jnp.bfloat16)


def project(normed, kv_weight):
    all_rows = lax.all_gather(kv_weight, "grp", axis=0, tiled=True)
    return jnp.dot(
        normed,
        lax.all_gather(all_rows, "tp", axis=1, tiled=True),
        preferred_element_type=jnp.float32,
    )


def group_tokens(tp_count, own_blocks):
    return 2 * tp_count * own_blocks * BLK // 5


def pages_per_device(tp_count, own_blocks):
    live_tokens = group_tokens(tp_count, own_blocks)
    return ((live_tokens + BLK - 1) // BLK + 2 * tp_count - 2) // tp_count


def general(hidden, lengths, kv_weight, input_gain, key_gain):
    tp_count = lax.axis_size("tp")
    my_index = lax.axis_index("tp")
    own_blocks = hidden.shape[0] // BLK
    page_count = pages_per_device(tp_count, own_blocks)
    per_peer = (own_blocks + tp_count - 1) // tp_count
    cache_width = 2 * KVH * HD
    group_len = lengths[0]
    block_counts = (group_len + (BLK - 1)) // BLK
    block_ends = jnp.cumsum(block_counts)
    block_starts = block_ends - block_counts
    offsets = jnp.arange(BLK, dtype=jnp.int32)
    my_start = block_starts[my_index]
    my_count = block_counts[my_index]
    my_length = group_len[my_index]
    outbound = (
        jnp.arange(tp_count, dtype=jnp.int32)[:, None] - my_start
    ) % tp_count + tp_count * jnp.arange(per_peer, dtype=jnp.int32)[None, :]
    outbound = outbound.reshape(-1)
    sending = outbound < my_count
    picked_local = jnp.minimum(outbound, own_blocks - 1)
    page_ranks = tp_count * jnp.arange(page_count, dtype=jnp.int32) + my_index
    anchor = jnp.minimum(
        jnp.sum((block_ends[None, :] <= page_ranks[:, None]).astype(jnp.int32), axis=1),
        tp_count - 1,
    )
    block_index = page_ranks - block_starts[anchor]
    page_live = page_ranks < block_ends[-1]
    chosen = anchor * per_peer + jnp.clip(block_index // tp_count, 0, per_peer - 1)
    projected = project(normalize(hidden, input_gain), kv_weight)
    own_pos = (jnp.arange(own_blocks, dtype=jnp.int32)[:, None] * BLK + offsets[None, :]).reshape(
        -1
    )
    own_cache = finish(projected, own_pos, own_pos < my_length, key_gain).reshape(
        own_blocks, BLK, cache_width
    )
    outgoing = jnp.where(
        sending[:, None, None],
        jnp.take(own_cache, picked_local, axis=0),
        jnp.zeros((), jnp.bfloat16),
    )
    arrived = lax.all_to_all(outgoing, "tp", split_axis=0, concat_axis=0, tiled=True)
    cache_pages = jnp.take(arrived, chosen, axis=0)
    return jnp.where(page_live[:, None, None], cache_pages, jnp.zeros((), jnp.bfloat16))


flip0 = [(i, i ^ 1) for i in range(4)]
flip1 = [(i, i ^ 2) for i in range(4)]


def sides(shard):
    return lax.ppermute(shard, "grp", flip0), lax.ppermute(shard, "grp", flip1)


def opposite(first_side0, second_side1):
    return lax.ppermute(first_side0, "grp", flip1), lax.ppermute(second_side1, "grp", flip0)


def stay(array):
    return pltpu.with_memory_space_constraint(array, pltpu.HBM)


def scale_kernel(lengths_ref, place_ref, x_ref, out_ref, x_buf, x_sem):
    count = (lengths_ref[place_ref[1]] + (BLK - 1)) // BLK

    def copy_of(block):
        rows = pl.ds(pl.multiple_of(block * BLK, BLK), BLK)
        return pltpu.make_async_copy(x_ref.at[rows], x_buf.at[rows], x_sem.at[block])

    def fetch(block, carry):
        copy_of(block).start()
        return carry

    def one_block(block, carry):
        copy_of(block).wait()
        rows = pl.ds(pl.multiple_of(block * BLK, BLK), BLK)
        squares = jnp.zeros((BLK, HD), jnp.float32)
        for cut in range(0, x_buf.shape[1], HD):
            values = x_buf[rows, cut : cut + HD].astype(jnp.float32)
            squares = squares + values * values
        mean = jnp.sum(squares, axis=-1, keepdims=True) / x_buf.shape[1]
        out_ref[rows, :] = jnp.broadcast_to(lax.rsqrt(mean + norm_eps), (BLK, HD))
        return carry

    lax.fori_loop(0, count, fetch, 0)
    lax.fori_loop(0, count, one_block, 0)


def row_scales(lengths, place, hidden):
    rows, width = hidden.shape
    small = pl.BlockSpec(memory_space=pltpu.SMEM)
    return pl.pallas_call(
        scale_kernel,
        in_specs=[small, small, pl.BlockSpec(memory_space=pltpu.HBM)],
        out_specs=pl.BlockSpec(memory_space=pltpu.VMEM),
        out_shape=jax.ShapeDtypeStruct((rows, HD), jnp.float32),
        scratch_shapes=[
            pltpu.VMEM((rows, width), hidden.dtype),
            pltpu.SemaphoreType.DMA((rows // BLK,)),
        ],
        compiler_params=pltpu.CompilerParams(vmem_limit_bytes=16 << 20),
        cost_estimate=pl.CostEstimate(
            flops=3 * rows * width, bytes_accessed=2 * rows * width, transcendentals=0
        ),
        name="row_scales",
    )(lengths, place, stay(hidden))


def tile_blocks(own_blocks):
    return max(t for t in (1, 2, 3) if own_blocks % t == 0)


class Chip:
    def __init__(self, lengths_ref, place_ref):
        self.tp_count = lengths_ref.shape[0]
        self.group, me = place_ref[0], place_ref[1]
        self.chip, self.core = me // 2, me % 2
        self.first = jnp.int32(0)
        for index in range(self.tp_count):
            count = (lengths_ref[index] + (BLK - 1)) // BLK
            self.first = self.first + jnp.where(index < 2 * self.chip, count, 0)
        length0, length1 = lengths_ref[2 * self.chip], lengths_ref[2 * self.chip + 1]
        self.count0 = (length0 + (BLK - 1)) // BLK
        self.own_len = jnp.where(self.core == 0, length0, length1)
        self.sib_len = jnp.where(self.core == 0, length1, length0)
        self.own_count = (self.own_len + (BLK - 1)) // BLK
        self.total = self.own_count + (self.sib_len + (BLK - 1)) // BLK

    def within(self, i):
        return jnp.where(i < self.own_count, i, i - self.own_count)

    def rows(self, i):
        return pl.ds(pl.multiple_of(self.within(i) * BLK, BLK), BLK)

    def fetch(self, i, own_ref, sib_ref, x_buf, x_sem, flips, depth, start):
        target = pl.ds(pl.multiple_of(i * BLK, BLK), BLK)

        def copies(source):
            for order, flip in enumerate(flips):
                columns = pl.ds(pl.multiple_of((self.group ^ flip) * depth, HD), depth)
                copy = pltpu.make_async_copy(
                    source.at[self.rows(i), columns],
                    x_buf.at[target, pl.ds(order * depth, depth)],
                    x_sem.at[i, order],
                )
                copy.start() if start else copy.wait()

        pl.when(i < self.own_count)(lambda: copies(own_ref))
        pl.when(jnp.logical_and(i >= self.own_count, i < self.total))(lambda: copies(sib_ref))

    def fetch_all(self, *args):
        def one_block(i, carry):
            self.fetch(i, *args, True)
            return carry

        lax.fori_loop(0, self.total, one_block, 0)


def near_kernel(tile, depth, pieces, *refs):
    lengths_ref, place_ref, own_ref, sib_ref = refs[:4]
    partial_ref, x_buf, w_buf, x_sem, w_sem = refs[-5:]
    near = refs[4:-5]
    chip = Chip(lengths_ref, place_ref)
    span = tile * BLK
    copies = [
        pltpu.make_async_copy(
            near[source].at[pl.ds(row, depth)],
            w_buf.at[pl.ds(part % 3 * depth, depth), pl.ds(part // 3 * HD, HD)],
            w_sem.at[part],
        )
        for part, (source, row) in enumerate(pieces)
    ]
    for copy in copies:
        copy.start()
    fetch = own_ref, sib_ref, x_buf, x_sem, (0, 1, 2), depth
    chip.fetch_all(*fetch)
    for copy in copies:
        copy.wait()

    def one_tile(step, carry):
        for part in range(tile):
            chip.fetch(step * tile + part, *fetch, False)
        rows = pl.ds(pl.multiple_of(step * span, span), span)
        partial_ref[rows, :] = jnp.dot(x_buf[rows, :], w_buf[...], preferred_element_type=jnp.float32)
        return carry

    lax.fori_loop(0, (chip.total + (tile - 1)) // tile, one_tile, 0)


def project_near(lengths, place, own, sibling, arrays, pieces, depth):
    rows, width = own.shape
    tile = tile_blocks(rows // BLK)
    columns = len(pieces) // 3 * HD
    small = pl.BlockSpec(memory_space=pltpu.SMEM)
    anywhere = pl.BlockSpec(memory_space=pl.ANY)
    in_hbm = pl.BlockSpec(memory_space=pltpu.HBM)
    held = 2 * rows + tile * BLK
    return pl.pallas_call(
        functools.partial(near_kernel, tile, depth, pieces),
        in_specs=[small] * 2 + [in_hbm] * 2 + [anywhere] * len(arrays),
        out_specs=pl.BlockSpec(memory_space=pltpu.VMEM),
        out_shape=jax.ShapeDtypeStruct((held, columns), jnp.float32),
        scratch_shapes=[
            pltpu.VMEM((held, 3 * depth), own.dtype),
            pltpu.VMEM((3 * depth, columns), jnp.bfloat16),
            pltpu.SemaphoreType.DMA((2 * rows // BLK, 3)),
            pltpu.SemaphoreType.DMA((len(pieces),)),
        ],
        compiler_params=pltpu.CompilerParams(vmem_limit_bytes=34 << 20),
        cost_estimate=pl.CostEstimate(
            flops=24 * rows * depth * columns, bytes_accessed=24 * rows * depth, transcendentals=0
        ),
        name="project_near",
    )(lengths, place, stay(own), stay(sibling), *arrays)


def far_kernel(slot_ids, tile, depth, deep, *refs):
    lengths_ref, place_ref, own_ref, sib_ref = refs[:4]
    far = refs[4:6]
    partial_ref, turn_ref, gain_ref, own_scale, sib_scale, out_ref, over_ref = refs[6:13]
    x_buf, w_buf, o_buf, x_sem, w_sem, o_sem = refs[13:]
    count = len(slot_ids)
    chip = Chip(lengths_ref, place_ref)
    tp_count, total, own_count = chip.tp_count, chip.total, chip.own_count
    tiles = (total + (tile - 1)) // tile
    span = tile * BLK
    copies = [
        pltpu.make_async_copy(far[index], w_buf.at[:, pl.ds(index * HD, HD)], w_sem.at[index])
        for index in range(count)
    ]
    for copy in copies:
        copy.start()
    fetch = own_ref, sib_ref, x_buf, x_sem, (3,), depth
    chip.fetch_all(*fetch)
    for copy in copies:
        copy.wait()
    is_key = [2 * (chip.chip ^ slot) + chip.core < KVH for slot in slot_ids]

    shift = tp_count.bit_length() - 1

    def send(i):
        second = jnp.where(i < own_count, chip.core, 1 - chip.core)
        place = chip.within(i) + second * chip.count0

        @pl.when(jnp.logical_and(i < total, place < deep * tp_count))
        def _():
            target = out_ref.at[(chip.first + place) & (tp_count - 1), lax.shift_right_logical(place, shift)]
            pltpu.make_async_copy(o_buf.at[i], target, o_sem.at[i]).start()

        @pl.when(jnp.logical_and(i < total, place >= deep * tp_count))
        def _():
            target = over_ref.at[place - deep * tp_count]
            pltpu.make_async_copy(o_buf.at[i], target, o_sem.at[i]).start()

    def multiply(step):
        for part in range(tile):
            chip.fetch(step * tile + part, *fetch, False)
        rows = pl.ds(pl.multiple_of(step * span, span), span)
        return partial_ref[rows, :] + jnp.dot(x_buf[rows, :], w_buf[...], preferred_element_type=jnp.float32)

    ones = jnp.full((HD, HD), 1.0 / HD, jnp.bfloat16)

    def head_mean(squares):
        high = squares.astype(jnp.bfloat16)
        low = (squares - high.astype(jnp.float32)).astype(jnp.bfloat16)
        return jnp.dot(high, ones, preferred_element_type=jnp.float32) + jnp.dot(
            low, ones, preferred_element_type=jnp.float32
        )

    def finish_tile(step, product):
        for part in range(tile):
            i = jnp.minimum(step * tile + part, total - 1)
            rows = chip.rows(i)
            limit = jnp.where(i < own_count, chip.own_len, chip.sib_len) - chip.within(i) * BLK
            valid = lax.broadcasted_iota(jnp.int32, (BLK, HD), 0) < limit
            scale = jnp.where(i < own_count, own_scale[rows, :], sib_scale[rows, :])
            for index in range(count):
                cut = product[part * BLK : (part + 1) * BLK, index * HD : (index + 1) * HD]
                values = cut * scale
                key_scale = lax.rsqrt(head_mean(values * values) + norm_eps)
                keys = values * key_scale * gain_ref[...]
                turned = keys * turn_ref[rows, :HD] + pltpu.roll(keys, HD // 2, 1) * turn_ref[rows, HD:]
                merged = jnp.where(jnp.logical_and(valid, is_key[index]), turned, jnp.where(valid, values, 0.0))
                o_buf[step * tile + part, index] = merged.astype(jnp.bfloat16)

    def send_tile(step):
        for part in range(tile):
            send(step * tile + part)

    def one_tile(step, product):
        following = multiply(step)
        finish_tile(step - 1, product)
        send_tile(step - 1)
        return following

    product = lax.fori_loop(1, tiles, one_tile, multiply(jnp.int32(0)))
    finish_tile(tiles - 1, product)
    send_tile(tiles - 1)

    def drain(i, carry):
        pltpu.make_async_copy(o_buf.at[i], out_ref.at[0, 0], o_sem.at[i]).wait()
        return carry

    lax.fori_loop(0, total, drain, 0)


def project_far(slot_ids, lengths, place, own, sibling, far, partial, scales, turn, key_gain, deep):
    rows, width = own.shape
    tp_count = lengths.shape[0]
    own_blocks = rows // BLK
    count = len(slot_ids)
    depth = far[0].shape[0]
    tile = tile_blocks(own_blocks)
    spare = 2 * own_blocks - deep * tp_count
    small = pl.BlockSpec(memory_space=pltpu.SMEM)
    anywhere = pl.BlockSpec(memory_space=pl.ANY)
    in_hbm = pl.BlockSpec(memory_space=pltpu.HBM)
    whole = pl.BlockSpec(memory_space=pltpu.VMEM)
    return pl.pallas_call(
        functools.partial(far_kernel, slot_ids, tile, depth, deep),
        in_specs=[small] * 2 + [in_hbm] * 2 + [anywhere] * 2 + [whole] * 5,
        out_specs=[in_hbm, anywhere],
        out_shape=[
            pltpu.HBM((tp_count, deep, count, BLK, HD), jnp.bfloat16),
            jax.ShapeDtypeStruct((max(spare, 1), count, BLK, HD), jnp.bfloat16),
        ],
        scratch_shapes=[
            pltpu.VMEM((2 * rows + tile * BLK, depth), own.dtype),
            pltpu.VMEM((depth, count * HD), jnp.bfloat16),
            pltpu.VMEM((2 * own_blocks + tile, count, BLK, HD), jnp.bfloat16),
            pltpu.SemaphoreType.DMA((2 * own_blocks, 1)),
            pltpu.SemaphoreType.DMA((count,)),
            pltpu.SemaphoreType.DMA((2 * own_blocks + tile,)),
        ],
        compiler_params=pltpu.CompilerParams(vmem_limit_bytes=16 << 20),
        cost_estimate=pl.CostEstimate(
            flops=16 * rows * depth * count * HD, bytes_accessed=16 * rows * depth, transcendentals=0
        ),
        name="project_far",
    )(lengths, place, stay(own), stay(sibling), *far, partial, turn, key_gain, *scales)


def page_source(lengths_ref, place_ref, page):
    tp_count = lengths_ref.shape[0]
    rank = page * tp_count + place_ref[1]
    end, chip, first = jnp.int32(0), jnp.int32(0), jnp.int32(0)
    for index in range(tp_count):
        end = end + (lengths_ref[index] + (BLK - 1)) // BLK
        if index % 2 == 1 and index + 1 < tp_count:
            passed = end <= rank
            chip = jnp.where(passed, index // 2 + 1, chip)
            first = jnp.where(passed, end, first)
    return rank < end, chip, rank - first


def columns_of(chip, slot, core):
    return pl.ds(pl.multiple_of((2 * (chip ^ slot) + core) * HD, HD), HD)


def early_kernel(groups, deep, lengths_ref, place_ref, *refs):
    arrived, spilled = refs[: len(groups)], refs[len(groups) : -3]
    out_ref, o_buf, o_sem = refs[-3:]
    tp_count = lengths_ref.shape[0]
    me = place_ref[1]

    def copy_of(page):
        return pltpu.make_async_copy(o_buf.at[page], out_ref.at[page], o_sem.at[page])

    for page in range(o_buf.shape[0]):
        live, chip, within = page_source(lengths_ref, place_ref, page)
        over = within >= deep * tp_count

        @pl.when(jnp.logical_and(live, jnp.logical_not(over)))
        def _():
            for order, slot_ids in enumerate(groups):
                for core in range(2):
                    for index, slot in enumerate(slot_ids):
                        block = arrived[order][2 * chip + core, within // tp_count, index]
                        o_buf[page, :, columns_of(chip, slot, core)] = block

        @pl.when(jnp.logical_and(live, over))
        def _():
            late = within - deep * tp_count
            for slot in range(tp_count // 2):
                o_buf[page, :, columns_of(chip, slot, me % 2)] = spilled[0][late, slot]
                o_buf[page, :, columns_of(chip, slot, 1 - me % 2)] = spilled[1][late, slot]

        @pl.when(jnp.logical_not(live))
        def _():
            o_buf[page] = jnp.zeros(o_buf.shape[1:], o_buf.dtype)

        copy_of(page).start()
    for page in range(o_buf.shape[0]):
        copy_of(page).wait()


def assemble_early(groups, lengths, place, arrived, spilled, page_count, deep):
    small = pl.BlockSpec(memory_space=pltpu.SMEM)
    whole = pl.BlockSpec(memory_space=pltpu.VMEM)
    shape = (page_count, BLK, 2 * KVH * HD)
    return pl.pallas_call(
        functools.partial(early_kernel, groups, deep),
        in_specs=[small] * 2 + [whole] * (len(arrived) + len(spilled)),
        out_specs=pl.BlockSpec(memory_space=pltpu.HBM),
        out_shape=pltpu.HBM(shape, jnp.bfloat16),
        scratch_shapes=[pltpu.VMEM(shape, jnp.bfloat16), pltpu.SemaphoreType.DMA((page_count,))],
        compiler_params=pltpu.CompilerParams(vmem_limit_bytes=16 << 20),
        name="assemble_early",
    )(lengths, place, *arrived, *spilled)


def late_kernel(slot_ids, deep, lengths_ref, place_ref, arrived, base_ref, out_ref, o_sem):
    del base_ref
    tp_count = lengths_ref.shape[0]

    def each_page(start):
        for page in range(out_ref.shape[0]):
            live, chip, within = page_source(lengths_ref, place_ref, page)

            @pl.when(jnp.logical_and(live, within < deep * tp_count))
            def _():
                for core in range(2):
                    for index, slot in enumerate(slot_ids):
                        copy = pltpu.make_async_copy(
                            arrived.at[2 * chip + core, within // tp_count, index],
                            out_ref.at[page, :, columns_of(chip, slot, core)],
                            o_sem.at[page, core, index],
                        )
                        copy.start() if start else copy.wait()

    each_page(True)
    each_page(False)


def assemble_late(slot_ids, lengths, place, arrived, base, deep):
    small = pl.BlockSpec(memory_space=pltpu.SMEM)
    return pl.pallas_call(
        functools.partial(late_kernel, slot_ids, deep),
        in_specs=[small] * 2 + [pl.BlockSpec(memory_space=pl.ANY), pl.BlockSpec(memory_space=pltpu.HBM)],
        out_specs=pl.BlockSpec(memory_space=pltpu.HBM),
        out_shape=pltpu.HBM(base.shape, base.dtype),
        scratch_shapes=[pltpu.SemaphoreType.DMA((base.shape[0], 2, len(slot_ids)))],
        input_output_aliases={3: 0},
        compiler_params=pltpu.CompilerParams(vmem_limit_bytes=16 << 20),
        name="assemble_late",
    )(lengths, place, arrived, base)


def rope_table(rows):
    inverse = np.exp(np.arange(HD // 2) * (-2.0 * math.log(rope_base) / HD))
    angles = np.arange(rows)[:, None] * inverse[None, :]
    cosine, sine_part = np.cos(angles), np.sin(angles)
    return jnp.asarray(np.concatenate([cosine, cosine, -sine_part, sine_part], axis=1), jnp.float32)


def exchange(sent):
    return lax.all_to_all(sent, "tp", split_axis=0, concat_axis=0, tiled=True)


def paired(hidden, lengths, kv_weight, input_gain, key_gain):
    tp_count = lax.axis_size("tp")
    nz = tp_count // 2
    group, me = lax.axis_index("grp"), lax.axis_index("tp")
    rows = hidden.shape[0]
    own_blocks = rows // BLK
    depth = kv_weight.shape[0]
    deep = 2 * own_blocks // tp_count
    page_count = pages_per_device(tp_count, own_blocks)
    group_len = lengths[0]
    place = jnp.stack([group, me]).astype(jnp.int32)
    swap = [(i, i ^ 1) for i in range(tp_count)]

    own_gain = lax.dynamic_slice(input_gain, (group * depth,), (depth,))
    shard = (kv_weight.astype(jnp.float32) * own_gain[:, None]).astype(jnp.bfloat16)
    sibling = lax.ppermute(hidden, "tp", swap)
    gain = key_gain.reshape(1, HD)

    def from_chip(flip, own):
        return lax.ppermute(own, "tp", [(i, i ^ (2 * flip)) for i in range(tp_count)])

    def start_group(arrays, pieces):
        return project_near(group_len, place, hidden, sibling, arrays, pieces, depth)

    def end_group(slot_ids, far, partial):
        return project_far(
            slot_ids, group_len, place, hidden, sibling, far, partial, (scale, other_scale), turn, gain, deep
        )

    groups = [tuple(range(start, min(start + 2, nz))) for start in range(0, nz, 2)]
    turn = rope_table(rows)
    slots = [shard] + [None] * (nz - 1)
    line = nz == 4
    inward = [(2 + c, 4 + c) for c in range(2)] + [(4 + c, 2 + c) for c in range(2)]
    outward = [(2 + c, c) for c in range(2)] + [(4 + c, 6 + c) for c in range(2)]
    slots[1] = from_chip(1, shard)
    side0 = sides(shard)
    across = lax.ppermute(shard, "tp", inward) if line else shard
    slots[1], shard, across = lax.optimization_barrier((slots[1], shard, across))
    if line:
        passed = lax.ppermute(slots[1], "tp", inward), lax.ppermute(across, "tp", outward)
    else:
        slots[2:] = [from_chip(flip, shard) for flip in range(2, nz)]
    slots[1], side0, later_len = lax.optimization_barrier((slots[1], side0, group_len))
    side1 = sides(slots[1])
    scale = row_scales(later_len, place, hidden)
    last = lax.ppermute(passed[0], "tp", outward) if line else None
    far = opposite(side0[0], side1[1])
    side1, scale, sibling = lax.optimization_barrier((side1, scale, sibling))
    other_scale = lax.ppermute(scale, "tp", swap)
    partial = start_group([slots[0], *side0, slots[1], *side1], [(part, 0) for part in range(6)])
    if line:
        far, other_scale, last, partial = lax.optimization_barrier((far, other_scale, last, partial))
        inner = (me // 2 == 1) | (me // 2 == 2)
        slots[2:] = [jnp.where(inner, passed[0], passed[1]), jnp.where(inner, across, last)]
    else:
        far, other_scale, slots, partial = lax.optimization_barrier((far, other_scale, slots, partial))
    sent, rest = end_group(groups[0], far, partial)
    arrived, over = [], [rest]
    for slot_ids in groups[1:]:
        both = jnp.concatenate([slots[slot] for slot in slot_ids])
        crossed = sides(both)
        arrived.append(exchange(sent))
        crossed, over[-1] = lax.optimization_barrier((crossed, over[-1]))
        far = opposite(crossed[0][:depth], crossed[1][depth:])
        pieces = [(source, index * depth) for index in range(2) for source in range(3)]
        partial = start_group([both, *crossed], pieces)
        far, partial = lax.optimization_barrier((far, partial))
        sent, rest = end_group(slot_ids, far, partial)
        over.append(rest)
    last_arrived = exchange(sent)

    def spill(rests):
        held = jnp.where(counts[me & -2] + counts[me | 1] > deep * tp_count, jnp.concatenate(rests, axis=1), 0)
        for flip in range(nz.bit_length() - 1):
            held = held + from_chip(1 << flip, held)
        return held, lax.ppermute(held, "tp", swap)

    def no_spill(rests):
        shape = (rests[0].shape[0], nz) + rests[0].shape[2:]
        return jnp.zeros(shape, jnp.bfloat16), jnp.zeros(shape, jnp.bfloat16)

    counts = (group_len + (BLK - 1)) // BLK
    most = jnp.max(counts[0::2] + counts[1::2])
    spilled = lax.cond(most > deep * tp_count, spill, no_spill, over)
    base = assemble_early(groups[:-1], group_len, place, arrived, spilled, page_count, deep)
    return assemble_late(groups[-1], group_len, place, last_arrived, base, deep)


def local(hidden, lengths, kv_weight, input_gain, key_gain):
    tp_count = lax.axis_size("tp")
    own_blocks = hidden.shape[0] // BLK
    spilling = (2 * own_blocks // tp_count * tp_count - 1) * BLK + 2
    fits = (
        lax.axis_size("grp") == 4
        and tp_count >= 4
        and tp_count & (tp_count - 1) == 0
        and kv_weight.shape[1] == HD
        and kv_weight.shape[0] % 256 == 0
        and 2 * own_blocks >= tp_count
        and 2 * spilling > group_tokens(tp_count, own_blocks)
    )
    chosen = paired if fits else general
    return chosen(hidden, lengths, kv_weight, input_gain, key_gain)


def solution(mesh):
    placed = (P(("grp", "tp"), None), P("grp", None), P("grp", "tp"), P(), P())
    return jax.shard_map(
        local, mesh=mesh, in_specs=placed, out_specs=P(("grp", "tp"), None, None), check_vma=False
    )
```

```python
import functools
import math

import jax
import jax.numpy as jnp
import numpy as np
from jax import lax
from jax.experimental import pallas as pl
from jax.experimental.pallas import tpu as pltpu
from jax.sharding import PartitionSpec as P

HD = 128
KVH = 4
BLK = 128


rope_base = 1000000.0
norm_eps = 1e-06


def normalize(token_rows, input_gain):
    values = token_rows.astype(jnp.float32)
    row_scale = lax.rsqrt(jnp.mean(values * values, axis=-1, keepdims=True) + norm_eps)
    return (values * row_scale * input_gain).astype(jnp.bfloat16)


def finish(projected, positions, valid, key_gain):
    key_width = KVH * HD
    half_dim = HD // 2
    row_count = projected.shape[0]
    key_part = projected[:, :key_width].reshape(row_count, KVH, HD)
    key_scale = lax.rsqrt(jnp.mean(key_part * key_part, axis=-1, keepdims=True) + norm_eps)
    key_part = key_part * key_scale * key_gain
    exponent = jnp.arange(half_dim, dtype=jnp.float32) * (2.0 / HD)
    inverse = jnp.exp(exponent * -math.log(rope_base))
    angles = positions.astype(jnp.float32)[:, None] * inverse[None, :]
    cosine = jnp.cos(angles)[:, None, :]
    sine_part = jnp.sin(angles)[:, None, :]
    lower_half = key_part[..., :half_dim]
    upper_half = key_part[..., half_dim:]
    turned = jnp.concatenate(
        [
            lower_half * cosine - upper_half * sine_part,
            upper_half * cosine + lower_half * sine_part,
        ],
        axis=-1,
    )
    merged = jnp.concatenate(
        [turned.reshape(row_count, key_width), projected[:, key_width:]], axis=-1
    )
    return jnp.where(valid[:, None], merged, 0.0).astype(jnp.bfloat16)


def project(normed, kv_weight):
    all_rows = lax.all_gather(kv_weight, "grp", axis=0, tiled=True)
    return jnp.dot(
        normed,
        lax.all_gather(all_rows, "tp", axis=1, tiled=True),
        preferred_element_type=jnp.float32,
    )


def group_tokens(tp_count, own_blocks):
    return 2 * tp_count * own_blocks * BLK // 5


def pages_per_device(tp_count, own_blocks):
    live_tokens = group_tokens(tp_count, own_blocks)
    return ((live_tokens + BLK - 1) // BLK + 2 * tp_count - 2) // tp_count


def general(hidden, lengths, kv_weight, input_gain, key_gain):
    tp_count = lax.axis_size("tp")
    my_index = lax.axis_index("tp")
    own_blocks = hidden.shape[0] // BLK
    page_count = pages_per_device(tp_count, own_blocks)
    per_peer = (own_blocks + tp_count - 1) // tp_count
    cache_width = 2 * KVH * HD
    group_len = lengths[0]
    block_counts = (group_len + (BLK - 1)) // BLK
    block_ends = jnp.cumsum(block_counts)
    block_starts = block_ends - block_counts
    offsets = jnp.arange(BLK, dtype=jnp.int32)
    my_start = block_starts[my_index]
    my_count = block_counts[my_index]
    my_length = group_len[my_index]
    outbound = (
        jnp.arange(tp_count, dtype=jnp.int32)[:, None] - my_start
    ) % tp_count + tp_count * jnp.arange(per_peer, dtype=jnp.int32)[None, :]
    outbound = outbound.reshape(-1)
    sending = outbound < my_count
    picked_local = jnp.minimum(outbound, own_blocks - 1)
    page_ranks = tp_count * jnp.arange(page_count, dtype=jnp.int32) + my_index
    anchor = jnp.minimum(
        jnp.sum((block_ends[None, :] <= page_ranks[:, None]).astype(jnp.int32), axis=1),
        tp_count - 1,
    )
    block_index = page_ranks - block_starts[anchor]
    page_live = page_ranks < block_ends[-1]
    chosen = anchor * per_peer + jnp.clip(block_index // tp_count, 0, per_peer - 1)
    projected = project(normalize(hidden, input_gain), kv_weight)
    own_pos = (jnp.arange(own_blocks, dtype=jnp.int32)[:, None] * BLK + offsets[None, :]).reshape(
        -1
    )
    own_cache = finish(projected, own_pos, own_pos < my_length, key_gain).reshape(
        own_blocks, BLK, cache_width
    )
    outgoing = jnp.where(
        sending[:, None, None],
        jnp.take(own_cache, picked_local, axis=0),
        jnp.zeros((), jnp.bfloat16),
    )
    arrived = lax.all_to_all(outgoing, "tp", split_axis=0, concat_axis=0, tiled=True)
    cache_pages = jnp.take(arrived, chosen, axis=0)
    return jnp.where(page_live[:, None, None], cache_pages, jnp.zeros((), jnp.bfloat16))


flip0 = [(i, i ^ 1) for i in range(4)]
flip1 = [(i, i ^ 2) for i in range(4)]


def sides(shard):
    return lax.ppermute(shard, "grp", flip0), lax.ppermute(shard, "grp", flip1)


def opposite(first_side0, second_side1):
    return lax.ppermute(first_side0, "grp", flip1), lax.ppermute(second_side1, "grp", flip0)


def stay(array):
    return pltpu.with_memory_space_constraint(array, pltpu.HBM)


def scale_kernel(lengths_ref, place_ref, x_ref, out_ref, x_buf, x_sem):
    count = (lengths_ref[place_ref[1]] + (BLK - 1)) // BLK

    def copy_of(block):
        rows = pl.ds(pl.multiple_of(block * BLK, BLK), BLK)
        return pltpu.make_async_copy(x_ref.at[rows], x_buf.at[rows], x_sem.at[block])

    def fetch(block, carry):
        copy_of(block).start()
        return carry

    def one_block(block, carry):
        copy_of(block).wait()
        rows = pl.ds(pl.multiple_of(block * BLK, BLK), BLK)
        squares = jnp.zeros((BLK, HD), jnp.float32)
        for cut in range(0, x_buf.shape[1], HD):
            values = x_buf[rows, cut : cut + HD].astype(jnp.float32)
            squares = squares + values * values
        mean = jnp.sum(squares, axis=-1, keepdims=True) / x_buf.shape[1]
        out_ref[rows, :] = jnp.broadcast_to(lax.rsqrt(mean + norm_eps), (BLK, HD))
        return carry

    lax.fori_loop(0, count, fetch, 0)
    lax.fori_loop(0, count, one_block, 0)


def row_scales(lengths, place, hidden):
    rows, width = hidden.shape
    small = pl.BlockSpec(memory_space=pltpu.SMEM)
    return pl.pallas_call(
        scale_kernel,
        in_specs=[small, small, pl.BlockSpec(memory_space=pltpu.HBM)],
        out_specs=pl.BlockSpec(memory_space=pltpu.VMEM),
        out_shape=jax.ShapeDtypeStruct((rows, HD), jnp.float32),
        scratch_shapes=[
            pltpu.VMEM((rows, width), hidden.dtype),
            pltpu.SemaphoreType.DMA((rows // BLK,)),
        ],
        compiler_params=pltpu.CompilerParams(vmem_limit_bytes=16 << 20),
        cost_estimate=pl.CostEstimate(
            flops=3 * rows * width, bytes_accessed=2 * rows * width, transcendentals=0
        ),
        name="row_scales",
    )(lengths, place, stay(hidden))


def tile_blocks(own_blocks):
    return max(t for t in (1, 2, 3) if own_blocks % t == 0)


class Chip:
    def __init__(self, lengths_ref, place_ref):
        self.tp_count = lengths_ref.shape[0]
        self.group, me = place_ref[0], place_ref[1]
        self.chip, self.core = me // 2, me % 2
        self.first = jnp.int32(0)
        for index in range(self.tp_count):
            count = (lengths_ref[index] + (BLK - 1)) // BLK
            self.first = self.first + jnp.where(index < 2 * self.chip, count, 0)
        length0, length1 = lengths_ref[2 * self.chip], lengths_ref[2 * self.chip + 1]
        self.count0 = (length0 + (BLK - 1)) // BLK
        self.own_len = jnp.where(self.core == 0, length0, length1)
        self.sib_len = jnp.where(self.core == 0, length1, length0)
        self.own_count = (self.own_len + (BLK - 1)) // BLK
        self.total = self.own_count + (self.sib_len + (BLK - 1)) // BLK

    def within(self, i):
        return jnp.where(i < self.own_count, i, i - self.own_count)

    def rows(self, i):
        return pl.ds(pl.multiple_of(self.within(i) * BLK, BLK), BLK)

    def fetch(self, i, own_ref, sib_ref, x_buf, x_sem, flips, depth, start):
        target = pl.ds(pl.multiple_of(i * BLK, BLK), BLK)

        def copies(source):
            for order, flip in enumerate(flips):
                columns = pl.ds(pl.multiple_of((self.group ^ flip) * depth, HD), depth)
                copy = pltpu.make_async_copy(
                    source.at[self.rows(i), columns],
                    x_buf.at[target, pl.ds(order * depth, depth)],
                    x_sem.at[i, order],
                )
                copy.start() if start else copy.wait()

        pl.when(i < self.own_count)(lambda: copies(own_ref))
        pl.when(jnp.logical_and(i >= self.own_count, i < self.total))(lambda: copies(sib_ref))

    def fetch_all(self, *args):
        def one_block(i, carry):
            self.fetch(i, *args, True)
            return carry

        lax.fori_loop(0, self.total, one_block, 0)


def near_kernel(tile, depth, pieces, *refs):
    lengths_ref, place_ref, own_ref, sib_ref = refs[:4]
    partial_ref, x_buf, w_buf, x_sem, w_sem = refs[-5:]
    near = refs[4:-5]
    chip = Chip(lengths_ref, place_ref)
    span = tile * BLK
    copies = [
        pltpu.make_async_copy(
            near[source].at[pl.ds(row, depth)],
            w_buf.at[pl.ds(part % 3 * depth, depth), pl.ds(part // 3 * HD, HD)],
            w_sem.at[part],
        )
        for part, (source, row) in enumerate(pieces)
    ]
    for copy in copies:
        copy.start()
    fetch = own_ref, sib_ref, x_buf, x_sem, (0, 1, 2), depth
    chip.fetch_all(*fetch)
    for copy in copies:
        copy.wait()

    def one_tile(step, carry):
        for part in range(tile):
            chip.fetch(step * tile + part, *fetch, False)
        rows = pl.ds(pl.multiple_of(step * span, span), span)
        partial_ref[rows, :] = jnp.dot(x_buf[rows, :], w_buf[...], preferred_element_type=jnp.float32)
        return carry

    lax.fori_loop(0, (chip.total + (tile - 1)) // tile, one_tile, 0)


def project_near(lengths, place, own, sibling, arrays, pieces, depth):
    rows, width = own.shape
    tile = tile_blocks(rows // BLK)
    columns = len(pieces) // 3 * HD
    small = pl.BlockSpec(memory_space=pltpu.SMEM)
    anywhere = pl.BlockSpec(memory_space=pl.ANY)
    in_hbm = pl.BlockSpec(memory_space=pltpu.HBM)
    held = 2 * rows + tile * BLK
    return pl.pallas_call(
        functools.partial(near_kernel, tile, depth, pieces),
        in_specs=[small] * 2 + [in_hbm] * 2 + [anywhere] * len(arrays),
        out_specs=pl.BlockSpec(memory_space=pltpu.VMEM),
        out_shape=jax.ShapeDtypeStruct((held, columns), jnp.float32),
        scratch_shapes=[
            pltpu.VMEM((held, 3 * depth), own.dtype),
            pltpu.VMEM((3 * depth, columns), jnp.bfloat16),
            pltpu.SemaphoreType.DMA((2 * rows // BLK, 3)),
            pltpu.SemaphoreType.DMA((len(pieces),)),
        ],
        compiler_params=pltpu.CompilerParams(vmem_limit_bytes=34 << 20),
        cost_estimate=pl.CostEstimate(
            flops=24 * rows * depth * columns, bytes_accessed=24 * rows * depth, transcendentals=0
        ),
        name="project_near",
    )(lengths, place, stay(own), stay(sibling), *arrays)


def far_kernel(slot_ids, tile, depth, deep, *refs):
    lengths_ref, place_ref, own_ref, sib_ref = refs[:4]
    far = refs[4:6]
    partial_ref, turn_ref, gain_ref, own_scale, sib_scale, out_ref, over_ref = refs[6:13]
    x_buf, w_buf, o_buf, x_sem, w_sem, o_sem = refs[13:]
    count = len(slot_ids)
    chip = Chip(lengths_ref, place_ref)
    tp_count, total, own_count = chip.tp_count, chip.total, chip.own_count
    tiles = (total + (tile - 1)) // tile
    span = tile * BLK
    copies = [
        pltpu.make_async_copy(far[index], w_buf.at[:, pl.ds(index * HD, HD)], w_sem.at[index])
        for index in range(count)
    ]
    for copy in copies:
        copy.start()
    fetch = own_ref, sib_ref, x_buf, x_sem, (3,), depth
    chip.fetch_all(*fetch)
    for copy in copies:
        copy.wait()
    is_key = [2 * (chip.chip ^ slot) + chip.core < KVH for slot in slot_ids]

    shift = tp_count.bit_length() - 1

    def send(i):
        second = jnp.where(i < own_count, chip.core, 1 - chip.core)
        place = chip.within(i) + second * chip.count0

        @pl.when(jnp.logical_and(i < total, place < deep * tp_count))
        def _():
            target = out_ref.at[(chip.first + place) & (tp_count - 1), lax.shift_right_logical(place, shift)]
            pltpu.make_async_copy(o_buf.at[i], target, o_sem.at[i]).start()

        @pl.when(jnp.logical_and(i < total, place >= deep * tp_count))
        def _():
            target = over_ref.at[place - deep * tp_count]
            pltpu.make_async_copy(o_buf.at[i], target, o_sem.at[i]).start()

    def multiply(step):
        for part in range(tile):
            chip.fetch(step * tile + part, *fetch, False)
        rows = pl.ds(pl.multiple_of(step * span, span), span)
        return partial_ref[rows, :] + jnp.dot(x_buf[rows, :], w_buf[...], preferred_element_type=jnp.float32)

    ones = jnp.full((HD, HD), 1.0 / HD, jnp.bfloat16)

    def head_mean(squares):
        high = squares.astype(jnp.bfloat16)
        low = (squares - high.astype(jnp.float32)).astype(jnp.bfloat16)
        return jnp.dot(high, ones, preferred_element_type=jnp.float32) + jnp.dot(
            low, ones, preferred_element_type=jnp.float32
        )

    def finish_tile(step, product):
        for part in range(tile):
            i = jnp.minimum(step * tile + part, total - 1)
            rows = chip.rows(i)
            limit = jnp.where(i < own_count, chip.own_len, chip.sib_len) - chip.within(i) * BLK
            valid = lax.broadcasted_iota(jnp.int32, (BLK, HD), 0) < limit
            scale = jnp.where(i < own_count, own_scale[rows, :], sib_scale[rows, :])
            for index in range(count):
                cut = product[part * BLK : (part + 1) * BLK, index * HD : (index + 1) * HD]
                values = cut * scale
                key_scale = lax.rsqrt(head_mean(values * values) + norm_eps)
                keys = values * key_scale * gain_ref[...]
                turned = keys * turn_ref[rows, :HD] + pltpu.roll(keys, HD // 2, 1) * turn_ref[rows, HD:]
                merged = jnp.where(jnp.logical_and(valid, is_key[index]), turned, jnp.where(valid, values, 0.0))
                o_buf[step * tile + part, index] = merged.astype(jnp.bfloat16)

    def send_tile(step):
        for part in range(tile):
            send(step * tile + part)

    def one_tile(step, product):
        following = multiply(step)
        finish_tile(step - 1, product)
        send_tile(step - 1)
        return following

    product = lax.fori_loop(1, tiles, one_tile, multiply(jnp.int32(0)))
    finish_tile(tiles - 1, product)
    send_tile(tiles - 1)

    def drain(i, carry):
        pltpu.make_async_copy(o_buf.at[i], out_ref.at[0, 0], o_sem.at[i]).wait()
        return carry

    lax.fori_loop(0, total, drain, 0)


def project_far(slot_ids, lengths, place, own, sibling, far, partial, scales, turn, key_gain, deep):
    rows, width = own.shape
    tp_count = lengths.shape[0]
    own_blocks = rows // BLK
    count = len(slot_ids)
    depth = far[0].shape[0]
    tile = tile_blocks(own_blocks)
    spare = 2 * own_blocks - deep * tp_count
    small = pl.BlockSpec(memory_space=pltpu.SMEM)
    anywhere = pl.BlockSpec(memory_space=pl.ANY)
    in_hbm = pl.BlockSpec(memory_space=pltpu.HBM)
    whole = pl.BlockSpec(memory_space=pltpu.VMEM)
    return pl.pallas_call(
        functools.partial(far_kernel, slot_ids, tile, depth, deep),
        in_specs=[small] * 2 + [in_hbm] * 2 + [anywhere] * 2 + [whole] * 5,
        out_specs=[in_hbm, anywhere],
        out_shape=[
            pltpu.HBM((tp_count, deep, count, BLK, HD), jnp.bfloat16),
            jax.ShapeDtypeStruct((max(spare, 1), count, BLK, HD), jnp.bfloat16),
        ],
        scratch_shapes=[
            pltpu.VMEM((2 * rows + tile * BLK, depth), own.dtype),
            pltpu.VMEM((depth, count * HD), jnp.bfloat16),
            pltpu.VMEM((2 * own_blocks + tile, count, BLK, HD), jnp.bfloat16),
            pltpu.SemaphoreType.DMA((2 * own_blocks, 1)),
            pltpu.SemaphoreType.DMA((count,)),
            pltpu.SemaphoreType.DMA((2 * own_blocks + tile,)),
        ],
        compiler_params=pltpu.CompilerParams(vmem_limit_bytes=16 << 20),
        cost_estimate=pl.CostEstimate(
            flops=16 * rows * depth * count * HD, bytes_accessed=16 * rows * depth, transcendentals=0
        ),
        name="project_far",
    )(lengths, place, stay(own), stay(sibling), *far, partial, turn, key_gain, *scales)


def page_source(lengths_ref, place_ref, page):
    tp_count = lengths_ref.shape[0]
    rank = page * tp_count + place_ref[1]
    end, chip, first = jnp.int32(0), jnp.int32(0), jnp.int32(0)
    for index in range(tp_count):
        end = end + (lengths_ref[index] + (BLK - 1)) // BLK
        if index % 2 == 1 and index + 1 < tp_count:
            passed = end <= rank
            chip = jnp.where(passed, index // 2 + 1, chip)
            first = jnp.where(passed, end, first)
    return rank < end, chip, rank - first


def columns_of(chip, slot, core):
    return pl.ds(pl.multiple_of((2 * (chip ^ slot) + core) * HD, HD), HD)


def early_kernel(groups, deep, lengths_ref, place_ref, *refs):
    arrived, spilled = refs[: len(groups)], refs[len(groups) : -3]
    out_ref, o_buf, o_sem = refs[-3:]
    tp_count = lengths_ref.shape[0]
    me = place_ref[1]

    def copy_of(page):
        return pltpu.make_async_copy(o_buf.at[page], out_ref.at[page], o_sem.at[page])

    for page in range(o_buf.shape[0]):
        live, chip, within = page_source(lengths_ref, place_ref, page)
        over = within >= deep * tp_count

        @pl.when(jnp.logical_and(live, jnp.logical_not(over)))
        def _():
            for order, slot_ids in enumerate(groups):
                for core in range(2):
                    for index, slot in enumerate(slot_ids):
                        block = arrived[order][2 * chip + core, within // tp_count, index]
                        o_buf[page, :, columns_of(chip, slot, core)] = block

        @pl.when(jnp.logical_and(live, over))
        def _():
            late = within - deep * tp_count
            for slot in range(tp_count // 2):
                o_buf[page, :, columns_of(chip, slot, me % 2)] = spilled[0][late, slot]
                o_buf[page, :, columns_of(chip, slot, 1 - me % 2)] = spilled[1][late, slot]

        @pl.when(jnp.logical_not(live))
        def _():
            o_buf[page] = jnp.zeros(o_buf.shape[1:], o_buf.dtype)

        copy_of(page).start()
    for page in range(o_buf.shape[0]):
        copy_of(page).wait()


def assemble_early(groups, lengths, place, arrived, spilled, page_count, deep):
    small = pl.BlockSpec(memory_space=pltpu.SMEM)
    whole = pl.BlockSpec(memory_space=pltpu.VMEM)
    shape = (page_count, BLK, 2 * KVH * HD)
    return pl.pallas_call(
        functools.partial(early_kernel, groups, deep),
        in_specs=[small] * 2 + [whole] * (len(arrived) + len(spilled)),
        out_specs=pl.BlockSpec(memory_space=pltpu.HBM),
        out_shape=pltpu.HBM(shape, jnp.bfloat16),
        scratch_shapes=[pltpu.VMEM(shape, jnp.bfloat16), pltpu.SemaphoreType.DMA((page_count,))],
        compiler_params=pltpu.CompilerParams(vmem_limit_bytes=16 << 20),
        name="assemble_early",
    )(lengths, place, *arrived, *spilled)


def late_kernel(slot_ids, deep, lengths_ref, place_ref, arrived, base_ref, out_ref, o_sem):
    del base_ref
    tp_count = lengths_ref.shape[0]

    def each_page(start):
        for page in range(out_ref.shape[0]):
            live, chip, within = page_source(lengths_ref, place_ref, page)

            @pl.when(jnp.logical_and(live, within < deep * tp_count))
            def _():
                for core in range(2):
                    for index, slot in enumerate(slot_ids):
                        copy = pltpu.make_async_copy(
                            arrived.at[2 * chip + core, within // tp_count, index],
                            out_ref.at[page, :, columns_of(chip, slot, core)],
                            o_sem.at[page, core, index],
                        )
                        copy.start() if start else copy.wait()

    each_page(True)
    each_page(False)


def assemble_late(slot_ids, lengths, place, arrived, base, deep):
    small = pl.BlockSpec(memory_space=pltpu.SMEM)
    return pl.pallas_call(
        functools.partial(late_kernel, slot_ids, deep),
        in_specs=[small] * 2 + [pl.BlockSpec(memory_space=pl.ANY), pl.BlockSpec(memory_space=pltpu.HBM)],
        out_specs=pl.BlockSpec(memory_space=pltpu.HBM),
        out_shape=pltpu.HBM(base.shape, base.dtype),
        scratch_shapes=[pltpu.SemaphoreType.DMA((base.shape[0], 2, len(slot_ids)))],
        input_output_aliases={3: 0},
        compiler_params=pltpu.CompilerParams(vmem_limit_bytes=16 << 20),
        name="assemble_late",
    )(lengths, place, arrived, base)


def rope_table(rows):
    inverse = np.exp(np.arange(HD // 2) * (-2.0 * math.log(rope_base) / HD))
    angles = np.arange(rows)[:, None] * inverse[None, :]
    cosine, sine_part = np.cos(angles), np.sin(angles)
    return jnp.asarray(np.concatenate([cosine, cosine, -sine_part, sine_part], axis=1), jnp.float32)


def exchange(sent):
    return lax.all_to_all(sent, "tp", split_axis=0, concat_axis=0, tiled=True)


def paired(hidden, lengths, kv_weight, input_gain, key_gain):
    tp_count = lax.axis_size("tp")
    nz = tp_count // 2
    group, me = lax.axis_index("grp"), lax.axis_index("tp")
    rows = hidden.shape[0]
    own_blocks = rows // BLK
    depth = kv_weight.shape[0]
    deep = 2 * own_blocks // tp_count
    page_count = pages_per_device(tp_count, own_blocks)
    group_len = lengths[0]
    place = jnp.stack([group, me]).astype(jnp.int32)
    swap = [(i, i ^ 1) for i in range(tp_count)]

    own_gain = lax.dynamic_slice(input_gain, (group * depth,), (depth,))
    shard = (kv_weight.astype(jnp.float32) * own_gain[:, None]).astype(jnp.bfloat16)
    sibling = lax.ppermute(hidden, "tp", swap)
    gain = key_gain.reshape(1, HD)

    def from_chip(flip, own):
        return lax.ppermute(own, "tp", [(i, i ^ (2 * flip)) for i in range(tp_count)])

    def start_group(arrays, pieces):
        return project_near(group_len, place, hidden, sibling, arrays, pieces, depth)

    def end_group(slot_ids, far, partial):
        return project_far(
            slot_ids, group_len, place, hidden, sibling, far, partial, (scale, other_scale), turn, gain, deep
        )

    groups = [tuple(range(start, min(start + 2, nz))) for start in range(0, nz, 2)]
    turn = rope_table(rows)
    slots = [shard] + [None] * (nz - 1)
    line = nz == 4
    inward = [(2 + c, 4 + c) for c in range(2)] + [(4 + c, 2 + c) for c in range(2)]
    outward = [(2 + c, c) for c in range(2)] + [(4 + c, 6 + c) for c in range(2)]
    around = inward + [(c, 6 + c) for c in range(2)] + [(6 + c, c) for c in range(2)]
    inner = (me // 2 == 1) | (me // 2 == 2)
    slots[1] = from_chip(1, shard)
    side0 = sides(shard)
    across = lax.ppermute(shard, "tp", inward) if line else shard
    slots[1], shard, across = lax.optimization_barrier((slots[1], shard, across))
    if line:
        ends = lax.ppermute(jnp.where(inner, slots[1], shard), "tp", around)
        passed = lax.ppermute(across, "tp", outward)
    else:
        slots[2:] = [from_chip(flip, shard) for flip in range(2, nz)]
    slots[1], side0, later_len = lax.optimization_barrier((slots[1], side0, group_len))
    side1 = sides(slots[1])
    scale = row_scales(later_len, place, hidden)
    far = opposite(side0[0], side1[1])
    side1, scale, sibling = lax.optimization_barrier((side1, scale, sibling))
    other_scale = lax.ppermute(scale, "tp", swap)
    partial = start_group([slots[0], *side0, slots[1], *side1], [(part, 0) for part in range(6)])
    if line:
        far, other_scale, ends, passed, partial = lax.optimization_barrier((far, other_scale, ends, passed, partial))
        slots[2:] = [jnp.where(inner, ends, passed), jnp.where(inner, across, ends)]
    else:
        far, other_scale, slots, partial = lax.optimization_barrier((far, other_scale, slots, partial))
    sent, rest = end_group(groups[0], far, partial)
    arrived, over = [], [rest]
    for slot_ids in groups[1:]:
        both = jnp.concatenate([slots[slot] for slot in slot_ids])
        crossed = sides(both)
        arrived.append(exchange(sent))
        crossed, over[-1] = lax.optimization_barrier((crossed, over[-1]))
        far = opposite(crossed[0][:depth], crossed[1][depth:])
        pieces = [(source, index * depth) for index in range(2) for source in range(3)]
        partial = start_group([both, *crossed], pieces)
        far, partial = lax.optimization_barrier((far, partial))
        sent, rest = end_group(slot_ids, far, partial)
        over.append(rest)
    last_arrived = exchange(sent)

    def spill(rests):
        held = jnp.where(counts[me & -2] + counts[me | 1] > deep * tp_count, jnp.concatenate(rests, axis=1), 0)
        for flip in range(nz.bit_length() - 1):
            held = held + from_chip(1 << flip, held)
        return held, lax.ppermute(held, "tp", swap)

    def no_spill(rests):
        shape = (rests[0].shape[0], nz) + rests[0].shape[2:]
        return jnp.zeros(shape, jnp.bfloat16), jnp.zeros(shape, jnp.bfloat16)

    counts = (group_len + (BLK - 1)) // BLK
    most = jnp.max(counts[0::2] + counts[1::2])
    spilled = lax.cond(most > deep * tp_count, spill, no_spill, over)
    base = assemble_early(groups[:-1], group_len, place, arrived, spilled, page_count, deep)
    return assemble_late(groups[-1], group_len, place, last_arrived, base, deep)


def local(hidden, lengths, kv_weight, input_gain, key_gain):
    tp_count = lax.axis_size("tp")
    own_blocks = hidden.shape[0] // BLK
    spilling = (2 * own_blocks // tp_count * tp_count - 1) * BLK + 2
    fits = (
        lax.axis_size("grp") == 4
        and tp_count >= 4
        and tp_count & (tp_count - 1) == 0
        and kv_weight.shape[1] == HD
        and kv_weight.shape[0] % 256 == 0
        and 2 * own_blocks >= tp_count
        and 2 * spilling > group_tokens(tp_count, own_blocks)
    )
    chosen = paired if fits else general
    return chosen(hidden, lengths, kv_weight, input_gain, key_gain)


def solution(mesh):
    placed = (P(("grp", "tp"), None), P("grp", None), P("grp", "tp"), P(), P())
    return jax.shard_map(
        local, mesh=mesh, in_specs=placed, out_specs=P(("grp", "tp"), None, None), check_vma=False
    )
```

```python
import functools
import math

import jax
import jax.numpy as jnp
import numpy as np
from jax import lax
from jax.experimental import pallas as pl
from jax.experimental.pallas import tpu as pltpu
from jax.sharding import PartitionSpec as P

HD = 128
KVH = 4
BLK = 128


rope_base = 1000000.0
norm_eps = 1e-06


def normalize(token_rows, input_gain):
    values = token_rows.astype(jnp.float32)
    row_scale = lax.rsqrt(jnp.mean(values * values, axis=-1, keepdims=True) + norm_eps)
    return (values * row_scale * input_gain).astype(jnp.bfloat16)


def finish(projected, positions, valid, key_gain):
    key_width = KVH * HD
    half_dim = HD // 2
    row_count = projected.shape[0]
    key_part = projected[:, :key_width].reshape(row_count, KVH, HD)
    key_scale = lax.rsqrt(jnp.mean(key_part * key_part, axis=-1, keepdims=True) + norm_eps)
    key_part = key_part * key_scale * key_gain
    exponent = jnp.arange(half_dim, dtype=jnp.float32) * (2.0 / HD)
    inverse = jnp.exp(exponent * -math.log(rope_base))
    angles = positions.astype(jnp.float32)[:, None] * inverse[None, :]
    cosine = jnp.cos(angles)[:, None, :]
    sine_part = jnp.sin(angles)[:, None, :]
    lower_half = key_part[..., :half_dim]
    upper_half = key_part[..., half_dim:]
    turned = jnp.concatenate(
        [
            lower_half * cosine - upper_half * sine_part,
            upper_half * cosine + lower_half * sine_part,
        ],
        axis=-1,
    )
    merged = jnp.concatenate(
        [turned.reshape(row_count, key_width), projected[:, key_width:]], axis=-1
    )
    return jnp.where(valid[:, None], merged, 0.0).astype(jnp.bfloat16)


def project(normed, kv_weight):
    all_rows = lax.all_gather(kv_weight, "grp", axis=0, tiled=True)
    return jnp.dot(
        normed,
        lax.all_gather(all_rows, "tp", axis=1, tiled=True),
        preferred_element_type=jnp.float32,
    )


def group_tokens(tp_count, own_blocks):
    return 2 * tp_count * own_blocks * BLK // 5


def pages_per_device(tp_count, own_blocks):
    live_tokens = group_tokens(tp_count, own_blocks)
    return ((live_tokens + BLK - 1) // BLK + 2 * tp_count - 2) // tp_count


def general(hidden, lengths, kv_weight, input_gain, key_gain):
    tp_count = lax.axis_size("tp")
    my_index = lax.axis_index("tp")
    own_blocks = hidden.shape[0] // BLK
    page_count = pages_per_device(tp_count, own_blocks)
    per_peer = (own_blocks + tp_count - 1) // tp_count
    cache_width = 2 * KVH * HD
    group_len = lengths[0]
    block_counts = (group_len + (BLK - 1)) // BLK
    block_ends = jnp.cumsum(block_counts)
    block_starts = block_ends - block_counts
    offsets = jnp.arange(BLK, dtype=jnp.int32)
    my_start = block_starts[my_index]
    my_count = block_counts[my_index]
    my_length = group_len[my_index]
    outbound = (
        jnp.arange(tp_count, dtype=jnp.int32)[:, None] - my_start
    ) % tp_count + tp_count * jnp.arange(per_peer, dtype=jnp.int32)[None, :]
    outbound = outbound.reshape(-1)
    sending = outbound < my_count
    picked_local = jnp.minimum(outbound, own_blocks - 1)
    page_ranks = tp_count * jnp.arange(page_count, dtype=jnp.int32) + my_index
    anchor = jnp.minimum(
        jnp.sum((block_ends[None, :] <= page_ranks[:, None]).astype(jnp.int32), axis=1),
        tp_count - 1,
    )
    block_index = page_ranks - block_starts[anchor]
    page_live = page_ranks < block_ends[-1]
    chosen = anchor * per_peer + jnp.clip(block_index // tp_count, 0, per_peer - 1)
    projected = project(normalize(hidden, input_gain), kv_weight)
    own_pos = (jnp.arange(own_blocks, dtype=jnp.int32)[:, None] * BLK + offsets[None, :]).reshape(
        -1
    )
    own_cache = finish(projected, own_pos, own_pos < my_length, key_gain).reshape(
        own_blocks, BLK, cache_width
    )
    outgoing = jnp.where(
        sending[:, None, None],
        jnp.take(own_cache, picked_local, axis=0),
        jnp.zeros((), jnp.bfloat16),
    )
    arrived = lax.all_to_all(outgoing, "tp", split_axis=0, concat_axis=0, tiled=True)
    cache_pages = jnp.take(arrived, chosen, axis=0)
    return jnp.where(page_live[:, None, None], cache_pages, jnp.zeros((), jnp.bfloat16))


flip0 = [(i, i ^ 1) for i in range(4)]
flip1 = [(i, i ^ 2) for i in range(4)]


def sides(shard):
    return lax.ppermute(shard, "grp", flip0), lax.ppermute(shard, "grp", flip1)


def opposite(first_side0, second_side1):
    return lax.ppermute(first_side0, "grp", flip1), lax.ppermute(second_side1, "grp", flip0)


def stay(array):
    return pltpu.with_memory_space_constraint(array, pltpu.HBM)


def scale_kernel(lengths_ref, place_ref, x_ref, out_ref, x_buf, x_sem):
    count = (lengths_ref[place_ref[1]] + (BLK - 1)) // BLK

    def copy_of(block):
        rows = pl.ds(pl.multiple_of(block * BLK, BLK), BLK)
        return pltpu.make_async_copy(x_ref.at[rows], x_buf.at[rows], x_sem.at[block])

    def fetch(block, carry):
        copy_of(block).start()
        return carry

    def one_block(block, carry):
        copy_of(block).wait()
        rows = pl.ds(pl.multiple_of(block * BLK, BLK), BLK)
        squares = jnp.zeros((BLK, HD), jnp.float32)
        for cut in range(0, x_buf.shape[1], HD):
            values = x_buf[rows, cut : cut + HD].astype(jnp.float32)
            squares = squares + values * values
        mean = jnp.sum(squares, axis=-1, keepdims=True) / x_buf.shape[1]
        out_ref[rows, :] = jnp.broadcast_to(lax.rsqrt(mean + norm_eps), (BLK, HD))
        return carry

    lax.fori_loop(0, count, fetch, 0)
    lax.fori_loop(0, count, one_block, 0)


def row_scales(lengths, place, hidden):
    rows, width = hidden.shape
    small = pl.BlockSpec(memory_space=pltpu.SMEM)
    return pl.pallas_call(
        scale_kernel,
        in_specs=[small, small, pl.BlockSpec(memory_space=pltpu.HBM)],
        out_specs=pl.BlockSpec(memory_space=pltpu.VMEM),
        out_shape=jax.ShapeDtypeStruct((rows, HD), jnp.float32),
        scratch_shapes=[
            pltpu.VMEM((rows, width), hidden.dtype),
            pltpu.SemaphoreType.DMA((rows // BLK,)),
        ],
        compiler_params=pltpu.CompilerParams(vmem_limit_bytes=16 << 20),
        cost_estimate=pl.CostEstimate(
            flops=3 * rows * width, bytes_accessed=2 * rows * width, transcendentals=0
        ),
        name="row_scales",
    )(lengths, place, stay(hidden))


def tile_blocks(own_blocks):
    return max(t for t in (1, 2, 3) if own_blocks % t == 0)


class Chip:
    def __init__(self, lengths_ref, place_ref):
        self.tp_count = lengths_ref.shape[0]
        self.group, me = place_ref[0], place_ref[1]
        self.chip, self.core = me // 2, me % 2
        self.first = jnp.int32(0)
        for index in range(self.tp_count):
            count = (lengths_ref[index] + (BLK - 1)) // BLK
            self.first = self.first + jnp.where(index < 2 * self.chip, count, 0)
        length0, length1 = lengths_ref[2 * self.chip], lengths_ref[2 * self.chip + 1]
        self.count0 = (length0 + (BLK - 1)) // BLK
        self.own_len = jnp.where(self.core == 0, length0, length1)
        self.sib_len = jnp.where(self.core == 0, length1, length0)
        self.own_count = (self.own_len + (BLK - 1)) // BLK
        self.total = self.own_count + (self.sib_len + (BLK - 1)) // BLK

    def within(self, i):
        return jnp.where(i < self.own_count, i, i - self.own_count)

    def rows(self, i):
        return pl.ds(pl.multiple_of(self.within(i) * BLK, BLK), BLK)

    def fetch(self, i, own_ref, sib_ref, x_buf, x_sem, flips, depth, start):
        target = pl.ds(pl.multiple_of(i * BLK, BLK), BLK)

        def copies(source):
            for order, flip in enumerate(flips):
                columns = pl.ds(pl.multiple_of((self.group ^ flip) * depth, HD), depth)
                copy = pltpu.make_async_copy(
                    source.at[self.rows(i), columns],
                    x_buf.at[target, pl.ds(order * depth, depth)],
                    x_sem.at[i, order],
                )
                copy.start() if start else copy.wait()

        pl.when(i < self.own_count)(lambda: copies(own_ref))
        pl.when(jnp.logical_and(i >= self.own_count, i < self.total))(lambda: copies(sib_ref))

    def fetch_all(self, *args):
        def one_block(i, carry):
            self.fetch(i, *args, True)
            return carry

        lax.fori_loop(0, self.total, one_block, 0)


def near_kernel(tile, depth, pieces, *refs):
    lengths_ref, place_ref, own_ref, sib_ref = refs[:4]
    partial_ref, x_buf, w_buf, x_sem, w_sem = refs[-5:]
    near = refs[4:-5]
    chip = Chip(lengths_ref, place_ref)
    span = tile * BLK
    copies = [
        pltpu.make_async_copy(
            near[source].at[pl.ds(row, depth)],
            w_buf.at[pl.ds(part % 3 * depth, depth), pl.ds(part // 3 * HD, HD)],
            w_sem.at[part],
        )
        for part, (source, row) in enumerate(pieces)
    ]
    for copy in copies:
        copy.start()
    fetch = own_ref, sib_ref, x_buf, x_sem, (0, 1, 2), depth
    chip.fetch_all(*fetch)
    for copy in copies:
        copy.wait()

    def one_tile(step, carry):
        for part in range(tile):
            chip.fetch(step * tile + part, *fetch, False)
        rows = pl.ds(pl.multiple_of(step * span, span), span)
        partial_ref[rows, :] = jnp.dot(x_buf[rows, :], w_buf[...], preferred_element_type=jnp.float32)
        return carry

    lax.fori_loop(0, (chip.total + (tile - 1)) // tile, one_tile, 0)


def project_near(lengths, place, own, sibling, arrays, pieces, depth):
    rows, width = own.shape
    tile = tile_blocks(rows // BLK)
    columns = len(pieces) // 3 * HD
    small = pl.BlockSpec(memory_space=pltpu.SMEM)
    anywhere = pl.BlockSpec(memory_space=pl.ANY)
    in_hbm = pl.BlockSpec(memory_space=pltpu.HBM)
    held = 2 * rows + tile * BLK
    return pl.pallas_call(
        functools.partial(near_kernel, tile, depth, pieces),
        in_specs=[small] * 2 + [in_hbm] * 2 + [anywhere] * len(arrays),
        out_specs=pl.BlockSpec(memory_space=pltpu.VMEM),
        out_shape=jax.ShapeDtypeStruct((held, columns), jnp.float32),
        scratch_shapes=[
            pltpu.VMEM((held, 3 * depth), own.dtype),
            pltpu.VMEM((3 * depth, columns), jnp.bfloat16),
            pltpu.SemaphoreType.DMA((2 * rows // BLK, 3)),
            pltpu.SemaphoreType.DMA((len(pieces),)),
        ],
        compiler_params=pltpu.CompilerParams(vmem_limit_bytes=34 << 20),
        cost_estimate=pl.CostEstimate(
            flops=24 * rows * depth * columns, bytes_accessed=24 * rows * depth, transcendentals=0
        ),
        name="project_near",
    )(lengths, place, stay(own), stay(sibling), *arrays)


def far_kernel(slot_ids, tile, depth, deep, *refs):
    lengths_ref, place_ref, own_ref, sib_ref = refs[:4]
    far = refs[4:6]
    partial_ref, turn_ref, gain_ref, own_scale, sib_scale, out_ref, over_ref = refs[6:13]
    x_buf, w_buf, o_buf, x_sem, w_sem, o_sem = refs[13:]
    count = len(slot_ids)
    chip = Chip(lengths_ref, place_ref)
    tp_count, total, own_count = chip.tp_count, chip.total, chip.own_count
    tiles = (total + (tile - 1)) // tile
    span = tile * BLK
    copies = [
        pltpu.make_async_copy(far[index], w_buf.at[:, pl.ds(index * HD, HD)], w_sem.at[index])
        for index in range(count)
    ]
    for copy in copies:
        copy.start()
    fetch = own_ref, sib_ref, x_buf, x_sem, (3,), depth
    chip.fetch_all(*fetch)
    for copy in copies:
        copy.wait()
    is_key = [2 * (chip.chip ^ slot) + chip.core < KVH for slot in slot_ids]

    shift = tp_count.bit_length() - 1

    def send(i):
        second = jnp.where(i < own_count, chip.core, 1 - chip.core)
        place = chip.within(i) + second * chip.count0

        @pl.when(jnp.logical_and(i < total, place < deep * tp_count))
        def _():
            target = out_ref.at[(chip.first + place) & (tp_count - 1), lax.shift_right_logical(place, shift)]
            pltpu.make_async_copy(o_buf.at[i], target, o_sem.at[i]).start()

        @pl.when(jnp.logical_and(i < total, place >= deep * tp_count))
        def _():
            target = over_ref.at[place - deep * tp_count]
            pltpu.make_async_copy(o_buf.at[i], target, o_sem.at[i]).start()

    def multiply(step):
        for part in range(tile):
            chip.fetch(step * tile + part, *fetch, False)
        rows = pl.ds(pl.multiple_of(step * span, span), span)
        return partial_ref[rows, :] + jnp.dot(x_buf[rows, :], w_buf[...], preferred_element_type=jnp.float32)

    ones = jnp.full((HD, HD), 1.0 / HD, jnp.bfloat16)

    def head_mean(squares):
        high = squares.astype(jnp.bfloat16)
        low = (squares - high.astype(jnp.float32)).astype(jnp.bfloat16)
        return jnp.dot(high, ones, preferred_element_type=jnp.float32) + jnp.dot(
            low, ones, preferred_element_type=jnp.float32
        )

    def finish_tile(step, product):
        for part in range(tile):
            i = jnp.minimum(step * tile + part, total - 1)
            rows = chip.rows(i)
            limit = jnp.where(i < own_count, chip.own_len, chip.sib_len) - chip.within(i) * BLK
            valid = lax.broadcasted_iota(jnp.int32, (BLK, HD), 0) < limit
            scale = jnp.where(i < own_count, own_scale[rows, :], sib_scale[rows, :])
            for index in range(count):
                cut = product[part * BLK : (part + 1) * BLK, index * HD : (index + 1) * HD]
                values = cut * scale
                key_scale = lax.rsqrt(head_mean(values * values) + norm_eps)
                keys = values * key_scale * gain_ref[...]
                turned = keys * turn_ref[rows, :HD] + pltpu.roll(keys, HD // 2, 1) * turn_ref[rows, HD:]
                merged = jnp.where(jnp.logical_and(valid, is_key[index]), turned, jnp.where(valid, values, 0.0))
                o_buf[step * tile + part, index] = merged.astype(jnp.bfloat16)

    def send_tile(step):
        for part in range(tile):
            send(step * tile + part)

    def one_tile(step, product):
        following = multiply(step)
        finish_tile(step - 1, product)
        send_tile(step - 1)
        return following

    product = lax.fori_loop(1, tiles, one_tile, multiply(jnp.int32(0)))
    finish_tile(tiles - 1, product)
    send_tile(tiles - 1)

    def drain(i, carry):
        pltpu.make_async_copy(o_buf.at[i], out_ref.at[0, 0], o_sem.at[i]).wait()
        return carry

    lax.fori_loop(0, total, drain, 0)


def project_far(slot_ids, lengths, place, own, sibling, far, partial, scales, turn, key_gain, deep):
    rows, width = own.shape
    tp_count = lengths.shape[0]
    own_blocks = rows // BLK
    count = len(slot_ids)
    depth = far[0].shape[0]
    tile = tile_blocks(own_blocks)
    spare = 2 * own_blocks - deep * tp_count
    small = pl.BlockSpec(memory_space=pltpu.SMEM)
    anywhere = pl.BlockSpec(memory_space=pl.ANY)
    in_hbm = pl.BlockSpec(memory_space=pltpu.HBM)
    whole = pl.BlockSpec(memory_space=pltpu.VMEM)
    return pl.pallas_call(
        functools.partial(far_kernel, slot_ids, tile, depth, deep),
        in_specs=[small] * 2 + [in_hbm] * 2 + [anywhere] * 2 + [whole] * 5,
        out_specs=[in_hbm, anywhere],
        out_shape=[
            pltpu.HBM((tp_count, deep, count, BLK, HD), jnp.bfloat16),
            jax.ShapeDtypeStruct((max(spare, 1), count, BLK, HD), jnp.bfloat16),
        ],
        scratch_shapes=[
            pltpu.VMEM((2 * rows + tile * BLK, depth), own.dtype),
            pltpu.VMEM((depth, count * HD), jnp.bfloat16),
            pltpu.VMEM((2 * own_blocks + tile, count, BLK, HD), jnp.bfloat16),
            pltpu.SemaphoreType.DMA((2 * own_blocks, 1)),
            pltpu.SemaphoreType.DMA((count,)),
            pltpu.SemaphoreType.DMA((2 * own_blocks + tile,)),
        ],
        compiler_params=pltpu.CompilerParams(vmem_limit_bytes=16 << 20),
        cost_estimate=pl.CostEstimate(
            flops=16 * rows * depth * count * HD, bytes_accessed=16 * rows * depth, transcendentals=0
        ),
        name="project_far",
    )(lengths, place, stay(own), stay(sibling), *far, partial, turn, key_gain, *scales)


def page_source(lengths_ref, place_ref, page):
    tp_count = lengths_ref.shape[0]
    rank = page * tp_count + place_ref[1]
    end, chip, first = jnp.int32(0), jnp.int32(0), jnp.int32(0)
    for index in range(tp_count):
        end = end + (lengths_ref[index] + (BLK - 1)) // BLK
        if index % 2 == 1 and index + 1 < tp_count:
            passed = end <= rank
            chip = jnp.where(passed, index // 2 + 1, chip)
            first = jnp.where(passed, end, first)
    return rank < end, chip, rank - first


def columns_of(chip, slot, core):
    return pl.ds(pl.multiple_of((2 * (chip ^ slot) + core) * HD, HD), HD)


def early_kernel(groups, deep, lengths_ref, place_ref, *refs):
    arrived, spilled = refs[: len(groups)], refs[len(groups) : -3]
    out_ref, o_buf, o_sem = refs[-3:]
    tp_count = lengths_ref.shape[0]
    me = place_ref[1]

    def copy_of(page):
        return pltpu.make_async_copy(o_buf.at[page], out_ref.at[page], o_sem.at[page])

    for page in range(o_buf.shape[0]):
        live, chip, within = page_source(lengths_ref, place_ref, page)
        over = within >= deep * tp_count

        @pl.when(jnp.logical_and(live, jnp.logical_not(over)))
        def _():
            for order, slot_ids in enumerate(groups):
                for core in range(2):
                    for index, slot in enumerate(slot_ids):
                        block = arrived[order][2 * chip + core, within // tp_count, index]
                        o_buf[page, :, columns_of(chip, slot, core)] = block

        @pl.when(jnp.logical_and(live, over))
        def _():
            late = within - deep * tp_count
            for slot in range(tp_count // 2):
                o_buf[page, :, columns_of(chip, slot, me % 2)] = spilled[0][late, slot]
                o_buf[page, :, columns_of(chip, slot, 1 - me % 2)] = spilled[1][late, slot]

        @pl.when(jnp.logical_not(live))
        def _():
            o_buf[page] = jnp.zeros(o_buf.shape[1:], o_buf.dtype)

        copy_of(page).start()
    for page in range(o_buf.shape[0]):
        copy_of(page).wait()


def assemble_early(groups, lengths, place, arrived, spilled, page_count, deep):
    small = pl.BlockSpec(memory_space=pltpu.SMEM)
    whole = pl.BlockSpec(memory_space=pltpu.VMEM)
    shape = (page_count, BLK, 2 * KVH * HD)
    return pl.pallas_call(
        functools.partial(early_kernel, groups, deep),
        in_specs=[small] * 2 + [whole] * (len(arrived) + len(spilled)),
        out_specs=pl.BlockSpec(memory_space=pltpu.HBM),
        out_shape=pltpu.HBM(shape, jnp.bfloat16),
        scratch_shapes=[pltpu.VMEM(shape, jnp.bfloat16), pltpu.SemaphoreType.DMA((page_count,))],
        compiler_params=pltpu.CompilerParams(vmem_limit_bytes=16 << 20),
        name="assemble_early",
    )(lengths, place, *arrived, *spilled)


def late_kernel(slot_ids, deep, lengths_ref, place_ref, arrived, base_ref, out_ref, o_sem):
    del base_ref
    tp_count = lengths_ref.shape[0]

    def each_page(start):
        for page in range(out_ref.shape[0]):
            live, chip, within = page_source(lengths_ref, place_ref, page)

            @pl.when(jnp.logical_and(live, within < deep * tp_count))
            def _():
                for core in range(2):
                    for index, slot in enumerate(slot_ids):
                        copy = pltpu.make_async_copy(
                            arrived.at[2 * chip + core, within // tp_count, index],
                            out_ref.at[page, :, columns_of(chip, slot, core)],
                            o_sem.at[page, core, index],
                        )
                        copy.start() if start else copy.wait()

    each_page(True)
    each_page(False)


def assemble_late(slot_ids, lengths, place, arrived, base, deep):
    small = pl.BlockSpec(memory_space=pltpu.SMEM)
    return pl.pallas_call(
        functools.partial(late_kernel, slot_ids, deep),
        in_specs=[small] * 2 + [pl.BlockSpec(memory_space=pl.ANY), pl.BlockSpec(memory_space=pltpu.HBM)],
        out_specs=pl.BlockSpec(memory_space=pltpu.HBM),
        out_shape=pltpu.HBM(base.shape, base.dtype),
        scratch_shapes=[pltpu.SemaphoreType.DMA((base.shape[0], 2, len(slot_ids)))],
        input_output_aliases={3: 0},
        compiler_params=pltpu.CompilerParams(vmem_limit_bytes=16 << 20),
        name="assemble_late",
    )(lengths, place, arrived, base)


def rope_table(rows):
    inverse = np.exp(np.arange(HD // 2) * (-2.0 * math.log(rope_base) / HD))
    angles = np.arange(rows)[:, None] * inverse[None, :]
    cosine, sine_part = np.cos(angles), np.sin(angles)
    return jnp.asarray(np.concatenate([cosine, cosine, -sine_part, sine_part], axis=1), jnp.float32)


def exchange(sent):
    return lax.all_to_all(sent, "tp", split_axis=0, concat_axis=0, tiled=True)


def paired(hidden, lengths, kv_weight, input_gain, key_gain):
    tp_count = lax.axis_size("tp")
    nz = tp_count // 2
    group, me = lax.axis_index("grp"), lax.axis_index("tp")
    rows = hidden.shape[0]
    own_blocks = rows // BLK
    depth = kv_weight.shape[0]
    deep = 2 * own_blocks // tp_count
    page_count = pages_per_device(tp_count, own_blocks)
    group_len = lengths[0]
    place = jnp.stack([group, me]).astype(jnp.int32)
    swap = [(i, i ^ 1) for i in range(tp_count)]

    own_gain = lax.dynamic_slice(input_gain, (group * depth,), (depth,))
    shard = (kv_weight.astype(jnp.float32) * own_gain[:, None]).astype(jnp.bfloat16)
    sibling = lax.ppermute(hidden, "tp", swap)
    gain = key_gain.reshape(1, HD)

    def from_chip(flip, own):
        return lax.ppermute(own, "tp", [(i, i ^ (2 * flip)) for i in range(tp_count)])

    def start_group(arrays, pieces):
        return project_near(group_len, place, hidden, sibling, arrays, pieces, depth)

    def end_group(slot_ids, far, partial):
        return project_far(
            slot_ids, group_len, place, hidden, sibling, far, partial, (scale, other_scale), turn, gain, deep
        )

    groups = [tuple(range(start, min(start + 2, nz))) for start in range(0, nz, 2)]
    turn = rope_table(rows)
    slots = [shard] + [None] * (nz - 1)
    line = nz == 4
    inward = [(2 + c, 4 + c) for c in range(2)] + [(4 + c, 2 + c) for c in range(2)]
    outward = [(2 + c, c) for c in range(2)] + [(4 + c, 6 + c) for c in range(2)]
    around = inward + [(c, 6 + c) for c in range(2)] + [(6 + c, c) for c in range(2)]
    inner = (me // 2 == 1) | (me // 2 == 2)
    slots[1] = from_chip(1, shard)
    side0 = sides(shard)
    across = lax.ppermute(shard, "tp", inward) if line else shard
    slots[1], shard, across = lax.optimization_barrier((slots[1], shard, across))
    if line:
        ends = lax.ppermute(jnp.where(inner, slots[1], shard), "tp", around)
        passed = lax.ppermute(across, "tp", outward)
    else:
        slots[2:] = [from_chip(flip, shard) for flip in range(2, nz)]
    slots[1], side0, later_len = lax.optimization_barrier((slots[1], side0, group_len))
    side1 = sides(slots[1])
    scale = row_scales(later_len, place, hidden)
    far = opposite(side0[0], side1[1])
    side1, scale, sibling = lax.optimization_barrier((side1, scale, sibling))
    other_scale = lax.ppermute(scale, "tp", swap)
    partial = start_group([slots[0], *side0, slots[1], *side1], [(part, 0) for part in range(6)])
    if line:
        far, other_scale, ends, passed, partial = lax.optimization_barrier((far, other_scale, ends, passed, partial))
        slots[2:] = [jnp.where(inner, ends, passed), jnp.where(inner, across, ends)]
    else:
        far, other_scale, slots, partial = lax.optimization_barrier((far, other_scale, slots, partial))
    sent, rest = end_group(groups[0], far, partial)
    arrived, over = [], [rest]
    for slot_ids in groups[1:]:
        both = jnp.concatenate([slots[slot] for slot in slot_ids])
        crossed = sides(both)
        arrived.append(exchange(sent))
        crossed, over[-1] = lax.optimization_barrier((crossed, over[-1]))
        far = opposite(crossed[0][:depth], crossed[1][depth:])
        pieces = [(source, index * depth) for index in range(2) for source in range(3)]
        partial = start_group([both, *crossed], pieces)
        far, partial = lax.optimization_barrier((far, partial))
        sent, rest = end_group(slot_ids, far, partial)
        over.append(rest)
    last_arrived = exchange(sent)

    counts = (group_len + (BLK - 1)) // BLK
    chip_counts = counts[0::2] + counts[1::2]
    most = jnp.max(chip_counts)

    def spill(rests):
        held = jnp.concatenate(rests, axis=1)
        source = jnp.argmax(chip_counts).astype(jnp.int32)
        first = jnp.sum(jnp.where(jnp.arange(nz) < source, chip_counts, 0))
        moved = []
        for late in range(held.shape[0]):
            rank = deep * tp_count + late
            flip = jnp.where(rank < most, source ^ ((first + rank) % tp_count // 2), 0)
            ways = [lambda block: block] + [functools.partial(from_chip, way) for way in range(1, nz)]
            moved.append(lax.switch(flip, ways, held[late]))
        moved = jnp.stack(moved)
        return moved, lax.ppermute(moved, "tp", swap)

    def no_spill(rests):
        shape = (rests[0].shape[0], nz) + rests[0].shape[2:]
        return jnp.zeros(shape, jnp.bfloat16), jnp.zeros(shape, jnp.bfloat16)

    spilled = lax.cond(most > deep * tp_count, spill, no_spill, over)
    base = assemble_early(groups[:-1], group_len, place, arrived, spilled, page_count, deep)
    return assemble_late(groups[-1], group_len, place, last_arrived, base, deep)


def local(hidden, lengths, kv_weight, input_gain, key_gain):
    tp_count = lax.axis_size("tp")
    own_blocks = hidden.shape[0] // BLK
    spilling = (2 * own_blocks // tp_count * tp_count - 1) * BLK + 2
    fits = (
        lax.axis_size("grp") == 4
        and tp_count >= 4
        and tp_count & (tp_count - 1) == 0
        and kv_weight.shape[1] == HD
        and kv_weight.shape[0] % 256 == 0
        and 2 * own_blocks >= tp_count
        and 2 * spilling > group_tokens(tp_count, own_blocks)
    )
    chosen = paired if fits else general
    return chosen(hidden, lengths, kv_weight, input_gain, key_gain)


def solution(mesh):
    placed = (P(("grp", "tp"), None), P("grp", None), P("grp", "tp"), P(), P())
    return jax.shard_map(
        local, mesh=mesh, in_specs=placed, out_specs=P(("grp", "tp"), None, None), check_vma=False
    )
```

```python
import functools
import math

import jax
import jax.numpy as jnp
import numpy as np
from jax import lax
from jax.experimental import pallas as pl
from jax.experimental.pallas import tpu as pltpu
from jax.sharding import PartitionSpec as P

HD = 128
KVH = 4
BLK = 128


rope_base = 1000000.0
norm_eps = 1e-06


def normalize(token_rows, input_gain):
    values = token_rows.astype(jnp.float32)
    row_scale = lax.rsqrt(jnp.mean(values * values, axis=-1, keepdims=True) + norm_eps)
    return (values * row_scale * input_gain).astype(jnp.bfloat16)


def finish(projected, positions, valid, key_gain):
    key_width = KVH * HD
    half_dim = HD // 2
    row_count = projected.shape[0]
    key_part = projected[:, :key_width].reshape(row_count, KVH, HD)
    key_scale = lax.rsqrt(jnp.mean(key_part * key_part, axis=-1, keepdims=True) + norm_eps)
    key_part = key_part * key_scale * key_gain
    exponent = jnp.arange(half_dim, dtype=jnp.float32) * (2.0 / HD)
    inverse = jnp.exp(exponent * -math.log(rope_base))
    angles = positions.astype(jnp.float32)[:, None] * inverse[None, :]
    cosine = jnp.cos(angles)[:, None, :]
    sine_part = jnp.sin(angles)[:, None, :]
    lower_half = key_part[..., :half_dim]
    upper_half = key_part[..., half_dim:]
    turned = jnp.concatenate(
        [
            lower_half * cosine - upper_half * sine_part,
            upper_half * cosine + lower_half * sine_part,
        ],
        axis=-1,
    )
    merged = jnp.concatenate(
        [turned.reshape(row_count, key_width), projected[:, key_width:]], axis=-1
    )
    return jnp.where(valid[:, None], merged, 0.0).astype(jnp.bfloat16)


def project(normed, kv_weight):
    all_rows = lax.all_gather(kv_weight, "grp", axis=0, tiled=True)
    return jnp.dot(
        normed,
        lax.all_gather(all_rows, "tp", axis=1, tiled=True),
        preferred_element_type=jnp.float32,
    )


def group_tokens(tp_count, own_blocks):
    return 2 * tp_count * own_blocks * BLK // 5


def pages_per_device(tp_count, own_blocks):
    live_tokens = group_tokens(tp_count, own_blocks)
    return ((live_tokens + BLK - 1) // BLK + 2 * tp_count - 2) // tp_count


def general(hidden, lengths, kv_weight, input_gain, key_gain):
    tp_count = lax.axis_size("tp")
    my_index = lax.axis_index("tp")
    own_blocks = hidden.shape[0] // BLK
    page_count = pages_per_device(tp_count, own_blocks)
    per_peer = (own_blocks + tp_count - 1) // tp_count
    cache_width = 2 * KVH * HD
    group_len = lengths[0]
    block_counts = (group_len + (BLK - 1)) // BLK
    block_ends = jnp.cumsum(block_counts)
    block_starts = block_ends - block_counts
    offsets = jnp.arange(BLK, dtype=jnp.int32)
    my_start = block_starts[my_index]
    my_count = block_counts[my_index]
    my_length = group_len[my_index]
    outbound = (
        jnp.arange(tp_count, dtype=jnp.int32)[:, None] - my_start
    ) % tp_count + tp_count * jnp.arange(per_peer, dtype=jnp.int32)[None, :]
    outbound = outbound.reshape(-1)
    sending = outbound < my_count
    picked_local = jnp.minimum(outbound, own_blocks - 1)
    page_ranks = tp_count * jnp.arange(page_count, dtype=jnp.int32) + my_index
    anchor = jnp.minimum(
        jnp.sum((block_ends[None, :] <= page_ranks[:, None]).astype(jnp.int32), axis=1),
        tp_count - 1,
    )
    block_index = page_ranks - block_starts[anchor]
    page_live = page_ranks < block_ends[-1]
    chosen = anchor * per_peer + jnp.clip(block_index // tp_count, 0, per_peer - 1)
    projected = project(normalize(hidden, input_gain), kv_weight)
    own_pos = (jnp.arange(own_blocks, dtype=jnp.int32)[:, None] * BLK + offsets[None, :]).reshape(
        -1
    )
    own_cache = finish(projected, own_pos, own_pos < my_length, key_gain).reshape(
        own_blocks, BLK, cache_width
    )
    outgoing = jnp.where(
        sending[:, None, None],
        jnp.take(own_cache, picked_local, axis=0),
        jnp.zeros((), jnp.bfloat16),
    )
    arrived = lax.all_to_all(outgoing, "tp", split_axis=0, concat_axis=0, tiled=True)
    cache_pages = jnp.take(arrived, chosen, axis=0)
    return jnp.where(page_live[:, None, None], cache_pages, jnp.zeros((), jnp.bfloat16))


flip0 = [(i, i ^ 1) for i in range(4)]
flip1 = [(i, i ^ 2) for i in range(4)]


def sides(shard):
    return lax.ppermute(shard, "grp", flip0), lax.ppermute(shard, "grp", flip1)


def opposite(first_side0, second_side1):
    return lax.ppermute(first_side0, "grp", flip1), lax.ppermute(second_side1, "grp", flip0)


def stay(array):
    return pltpu.with_memory_space_constraint(array, pltpu.HBM)


def scale_kernel(lengths_ref, place_ref, x_ref, out_ref, x_buf, x_sem):
    count = (lengths_ref[place_ref[1]] + (BLK - 1)) // BLK

    def copy_of(block):
        rows = pl.ds(pl.multiple_of(block * BLK, BLK), BLK)
        return pltpu.make_async_copy(x_ref.at[rows], x_buf.at[rows], x_sem.at[block])

    def fetch(block, carry):
        copy_of(block).start()
        return carry

    def one_block(block, carry):
        copy_of(block).wait()
        rows = pl.ds(pl.multiple_of(block * BLK, BLK), BLK)
        squares = jnp.zeros((BLK, HD), jnp.float32)
        for cut in range(0, x_buf.shape[1], HD):
            values = x_buf[rows, cut : cut + HD].astype(jnp.float32)
            squares = squares + values * values
        mean = jnp.sum(squares, axis=-1, keepdims=True) / x_buf.shape[1]
        out_ref[rows, :] = jnp.broadcast_to(lax.rsqrt(mean + norm_eps), (BLK, HD))
        return carry

    lax.fori_loop(0, count, fetch, 0)
    lax.fori_loop(0, count, one_block, 0)


def row_scales(lengths, place, hidden):
    rows, width = hidden.shape
    small = pl.BlockSpec(memory_space=pltpu.SMEM)
    return pl.pallas_call(
        scale_kernel,
        in_specs=[small, small, pl.BlockSpec(memory_space=pltpu.HBM)],
        out_specs=pl.BlockSpec(memory_space=pltpu.VMEM),
        out_shape=jax.ShapeDtypeStruct((rows, HD), jnp.float32),
        scratch_shapes=[
            pltpu.VMEM((rows, width), hidden.dtype),
            pltpu.SemaphoreType.DMA((rows // BLK,)),
        ],
        compiler_params=pltpu.CompilerParams(vmem_limit_bytes=16 << 20),
        cost_estimate=pl.CostEstimate(
            flops=3 * rows * width, bytes_accessed=2 * rows * width, transcendentals=0
        ),
        name="row_scales",
    )(lengths, place, stay(hidden))


def tile_blocks(own_blocks):
    return max(t for t in (1, 2, 3) if own_blocks % t == 0)


class Chip:
    def __init__(self, lengths_ref, place_ref):
        self.tp_count = lengths_ref.shape[0]
        self.group, me = place_ref[0], place_ref[1]
        self.chip, self.core = me // 2, me % 2
        self.first = jnp.int32(0)
        for index in range(self.tp_count):
            count = (lengths_ref[index] + (BLK - 1)) // BLK
            self.first = self.first + jnp.where(index < 2 * self.chip, count, 0)
        length0, length1 = lengths_ref[2 * self.chip], lengths_ref[2 * self.chip + 1]
        self.count0 = (length0 + (BLK - 1)) // BLK
        self.own_len = jnp.where(self.core == 0, length0, length1)
        self.sib_len = jnp.where(self.core == 0, length1, length0)
        self.own_count = (self.own_len + (BLK - 1)) // BLK
        self.total = self.own_count + (self.sib_len + (BLK - 1)) // BLK

    def within(self, i):
        return jnp.where(i < self.own_count, i, i - self.own_count)

    def rows(self, i):
        return pl.ds(pl.multiple_of(self.within(i) * BLK, BLK), BLK)

    def fetch(self, i, own_ref, sib_ref, x_buf, x_sem, flips, depth, start):
        target = pl.ds(pl.multiple_of(i * BLK, BLK), BLK)

        def copies(source):
            for order, flip in enumerate(flips):
                columns = pl.ds(pl.multiple_of((self.group ^ flip) * depth, HD), depth)
                copy = pltpu.make_async_copy(
                    source.at[self.rows(i), columns],
                    x_buf.at[target, pl.ds(order * depth, depth)],
                    x_sem.at[i, order],
                )
                copy.start() if start else copy.wait()

        pl.when(i < self.own_count)(lambda: copies(own_ref))
        pl.when(jnp.logical_and(i >= self.own_count, i < self.total))(lambda: copies(sib_ref))

    def fetch_all(self, *args):
        def one_block(i, carry):
            self.fetch(i, *args, True)
            return carry

        lax.fori_loop(0, self.total, one_block, 0)


def near_kernel(tile, depth, pieces, *refs):
    lengths_ref, place_ref, own_ref, sib_ref = refs[:4]
    partial_ref, x_buf, w_buf, x_sem, w_sem = refs[-5:]
    near = refs[4:-5]
    chip = Chip(lengths_ref, place_ref)
    span = tile * BLK
    copies = [
        pltpu.make_async_copy(
            near[source].at[pl.ds(row, depth)],
            w_buf.at[pl.ds(part % 3 * depth, depth), pl.ds(part // 3 * HD, HD)],
            w_sem.at[part],
        )
        for part, (source, row) in enumerate(pieces)
    ]
    for copy in copies:
        copy.start()
    fetch = own_ref, sib_ref, x_buf, x_sem, (0, 1, 2), depth
    chip.fetch_all(*fetch)
    for copy in copies:
        copy.wait()

    def one_tile(step, carry):
        for part in range(tile):
            chip.fetch(step * tile + part, *fetch, False)
        rows = pl.ds(pl.multiple_of(step * span, span), span)
        partial_ref[rows, :] = jnp.dot(x_buf[rows, :], w_buf[...], preferred_element_type=jnp.float32)
        return carry

    lax.fori_loop(0, (chip.total + (tile - 1)) // tile, one_tile, 0)


def project_near(lengths, place, own, sibling, arrays, pieces, depth):
    rows, width = own.shape
    tile = tile_blocks(rows // BLK)
    columns = len(pieces) // 3 * HD
    small = pl.BlockSpec(memory_space=pltpu.SMEM)
    anywhere = pl.BlockSpec(memory_space=pl.ANY)
    in_hbm = pl.BlockSpec(memory_space=pltpu.HBM)
    held = 2 * rows + tile * BLK
    return pl.pallas_call(
        functools.partial(near_kernel, tile, depth, pieces),
        in_specs=[small] * 2 + [in_hbm] * 2 + [anywhere] * len(arrays),
        out_specs=pl.BlockSpec(memory_space=pltpu.VMEM),
        out_shape=jax.ShapeDtypeStruct((held, columns), jnp.float32),
        scratch_shapes=[
            pltpu.VMEM((held, 3 * depth), own.dtype),
            pltpu.VMEM((3 * depth, columns), jnp.bfloat16),
            pltpu.SemaphoreType.DMA((2 * rows // BLK, 3)),
            pltpu.SemaphoreType.DMA((len(pieces),)),
        ],
        compiler_params=pltpu.CompilerParams(vmem_limit_bytes=34 << 20),
        cost_estimate=pl.CostEstimate(
            flops=24 * rows * depth * columns, bytes_accessed=24 * rows * depth, transcendentals=0
        ),
        name="project_near",
    )(lengths, place, stay(own), stay(sibling), *arrays)


def far_kernel(slot_ids, tile, depth, deep, *refs):
    lengths_ref, place_ref, own_ref, sib_ref = refs[:4]
    far = refs[4:6]
    partial_ref, turn_ref, gain_ref, own_scale, sib_scale, out_ref, over_ref = refs[6:13]
    x_buf, w_buf, o_buf, x_sem, w_sem, o_sem = refs[13:]
    count = len(slot_ids)
    chip = Chip(lengths_ref, place_ref)
    tp_count, total, own_count = chip.tp_count, chip.total, chip.own_count
    tiles = (total + (tile - 1)) // tile
    span = tile * BLK
    copies = [
        pltpu.make_async_copy(far[index], w_buf.at[:, pl.ds(index * HD, HD)], w_sem.at[index])
        for index in range(count)
    ]
    for copy in copies:
        copy.start()
    fetch = own_ref, sib_ref, x_buf, x_sem, (3,), depth
    chip.fetch_all(*fetch)
    for copy in copies:
        copy.wait()
    is_key = [2 * (chip.chip ^ slot) + chip.core < KVH for slot in slot_ids]

    shift = tp_count.bit_length() - 1

    def send(i):
        second = jnp.where(i < own_count, chip.core, 1 - chip.core)
        place = chip.within(i) + second * chip.count0

        @pl.when(jnp.logical_and(i < total, place < deep * tp_count))
        def _():
            target = out_ref.at[(chip.first + place) & (tp_count - 1), lax.shift_right_logical(place, shift)]
            pltpu.make_async_copy(o_buf.at[i], target, o_sem.at[i]).start()

        @pl.when(jnp.logical_and(i < total, place >= deep * tp_count))
        def _():
            target = over_ref.at[place - deep * tp_count]
            pltpu.make_async_copy(o_buf.at[i], target, o_sem.at[i]).start()

    def multiply(step):
        for part in range(tile):
            chip.fetch(step * tile + part, *fetch, False)
        rows = pl.ds(pl.multiple_of(step * span, span), span)
        return partial_ref[rows, :] + jnp.dot(x_buf[rows, :], w_buf[...], preferred_element_type=jnp.float32)

    ones = jnp.full((HD, HD), 1.0 / HD, jnp.bfloat16)

    def head_mean(squares):
        high = squares.astype(jnp.bfloat16)
        low = (squares - high.astype(jnp.float32)).astype(jnp.bfloat16)
        return jnp.dot(high, ones, preferred_element_type=jnp.float32) + jnp.dot(
            low, ones, preferred_element_type=jnp.float32
        )

    def finish_tile(step, product):
        for part in range(tile):
            i = jnp.minimum(step * tile + part, total - 1)
            rows = chip.rows(i)
            limit = jnp.where(i < own_count, chip.own_len, chip.sib_len) - chip.within(i) * BLK
            valid = lax.broadcasted_iota(jnp.int32, (BLK, HD), 0) < limit
            scale = jnp.where(i < own_count, own_scale[rows, :], sib_scale[rows, :])
            for index in range(count):
                cut = product[part * BLK : (part + 1) * BLK, index * HD : (index + 1) * HD]
                values = cut * scale
                key_scale = lax.rsqrt(head_mean(values * values) + norm_eps)
                keys = values * key_scale * gain_ref[...]
                turned = keys * turn_ref[rows, :HD] + pltpu.roll(keys, HD // 2, 1) * turn_ref[rows, HD:]
                merged = jnp.where(jnp.logical_and(valid, is_key[index]), turned, jnp.where(valid, values, 0.0))
                o_buf[step * tile + part, index] = merged.astype(jnp.bfloat16)

    def send_tile(step):
        for part in range(tile):
            send(step * tile + part)

    def one_tile(step, product):
        following = multiply(step)
        finish_tile(step - 1, product)
        send_tile(step - 1)
        return following

    product = lax.fori_loop(1, tiles, one_tile, multiply(jnp.int32(0)))
    finish_tile(tiles - 1, product)
    send_tile(tiles - 1)

    def drain(i, carry):
        pltpu.make_async_copy(o_buf.at[i], out_ref.at[0, 0], o_sem.at[i]).wait()
        return carry

    lax.fori_loop(0, total, drain, 0)


def project_far(slot_ids, lengths, place, own, sibling, far, partial, scales, turn, key_gain, deep):
    rows, width = own.shape
    tp_count = lengths.shape[0]
    own_blocks = rows // BLK
    count = len(slot_ids)
    depth = far[0].shape[0]
    tile = tile_blocks(own_blocks)
    spare = 2 * own_blocks - deep * tp_count
    small = pl.BlockSpec(memory_space=pltpu.SMEM)
    anywhere = pl.BlockSpec(memory_space=pl.ANY)
    in_hbm = pl.BlockSpec(memory_space=pltpu.HBM)
    whole = pl.BlockSpec(memory_space=pltpu.VMEM)
    return pl.pallas_call(
        functools.partial(far_kernel, slot_ids, tile, depth, deep),
        in_specs=[small] * 2 + [in_hbm] * 2 + [anywhere] * 2 + [whole] * 5,
        out_specs=[in_hbm, anywhere],
        out_shape=[
            pltpu.HBM((tp_count, deep, count, BLK, HD), jnp.bfloat16),
            jax.ShapeDtypeStruct((max(spare, 1), count, BLK, HD), jnp.bfloat16),
        ],
        scratch_shapes=[
            pltpu.VMEM((2 * rows + tile * BLK, depth), own.dtype),
            pltpu.VMEM((depth, count * HD), jnp.bfloat16),
            pltpu.VMEM((2 * own_blocks + tile, count, BLK, HD), jnp.bfloat16),
            pltpu.SemaphoreType.DMA((2 * own_blocks, 1)),
            pltpu.SemaphoreType.DMA((count,)),
            pltpu.SemaphoreType.DMA((2 * own_blocks + tile,)),
        ],
        compiler_params=pltpu.CompilerParams(vmem_limit_bytes=16 << 20),
        cost_estimate=pl.CostEstimate(
            flops=16 * rows * depth * count * HD, bytes_accessed=16 * rows * depth, transcendentals=0
        ),
        name="project_far",
    )(lengths, place, stay(own), stay(sibling), *far, partial, turn, key_gain, *scales)


def page_source(lengths_ref, place_ref, page):
    tp_count = lengths_ref.shape[0]
    rank = page * tp_count + place_ref[1]
    end, chip, first = jnp.int32(0), jnp.int32(0), jnp.int32(0)
    for index in range(tp_count):
        end = end + (lengths_ref[index] + (BLK - 1)) // BLK
        if index % 2 == 1 and index + 1 < tp_count:
            passed = end <= rank
            chip = jnp.where(passed, index // 2 + 1, chip)
            first = jnp.where(passed, end, first)
    return rank < end, chip, rank - first


def columns_of(chip, slot, core):
    return pl.ds(pl.multiple_of((2 * (chip ^ slot) + core) * HD, HD), HD)


def early_kernel(groups, deep, lengths_ref, place_ref, *refs):
    arrived, spilled = refs[: len(groups)], refs[len(groups) : -3]
    out_ref, o_buf, o_sem = refs[-3:]
    tp_count = lengths_ref.shape[0]
    me = place_ref[1]

    def copy_of(page):
        return pltpu.make_async_copy(o_buf.at[page], out_ref.at[page], o_sem.at[page])

    for page in range(o_buf.shape[0]):
        live, chip, within = page_source(lengths_ref, place_ref, page)
        over = within >= deep * tp_count

        @pl.when(jnp.logical_and(live, jnp.logical_not(over)))
        def _():
            for order, slot_ids in enumerate(groups):
                for core in range(2):
                    for index, slot in enumerate(slot_ids):
                        block = arrived[order][2 * chip + core, within // tp_count, index]
                        o_buf[page, :, columns_of(chip, slot, core)] = block

        @pl.when(jnp.logical_and(live, over))
        def _():
            late = within - deep * tp_count
            for slot in range(tp_count // 2):
                o_buf[page, :, columns_of(chip, slot, me % 2)] = spilled[0][late, slot]
                o_buf[page, :, columns_of(chip, slot, 1 - me % 2)] = spilled[1][late, slot]

        @pl.when(jnp.logical_not(live))
        def _():
            o_buf[page] = jnp.zeros(o_buf.shape[1:], o_buf.dtype)

        copy_of(page).start()
    for page in range(o_buf.shape[0]):
        copy_of(page).wait()


def assemble_early(groups, lengths, place, arrived, spilled, page_count, deep):
    small = pl.BlockSpec(memory_space=pltpu.SMEM)
    whole = pl.BlockSpec(memory_space=pltpu.VMEM)
    shape = (page_count, BLK, 2 * KVH * HD)
    return pl.pallas_call(
        functools.partial(early_kernel, groups, deep),
        in_specs=[small] * 2 + [whole] * (len(arrived) + len(spilled)),
        out_specs=pl.BlockSpec(memory_space=pltpu.HBM),
        out_shape=pltpu.HBM(shape, jnp.bfloat16),
        scratch_shapes=[pltpu.VMEM(shape, jnp.bfloat16), pltpu.SemaphoreType.DMA((page_count,))],
        compiler_params=pltpu.CompilerParams(vmem_limit_bytes=16 << 20),
        name="assemble_early",
    )(lengths, place, *arrived, *spilled)


def late_kernel(slot_ids, deep, lengths_ref, place_ref, arrived, base_ref, out_ref, o_sem):
    del base_ref
    tp_count = lengths_ref.shape[0]

    def each_page(start):
        for page in range(out_ref.shape[0]):
            live, chip, within = page_source(lengths_ref, place_ref, page)

            @pl.when(jnp.logical_and(live, within < deep * tp_count))
            def _():
                for core in range(2):
                    for index, slot in enumerate(slot_ids):
                        copy = pltpu.make_async_copy(
                            arrived.at[2 * chip + core, within // tp_count, index],
                            out_ref.at[page, :, columns_of(chip, slot, core)],
                            o_sem.at[page, core, index],
                        )
                        copy.start() if start else copy.wait()

    each_page(True)
    each_page(False)


def assemble_late(slot_ids, lengths, place, arrived, base, deep):
    small = pl.BlockSpec(memory_space=pltpu.SMEM)
    return pl.pallas_call(
        functools.partial(late_kernel, slot_ids, deep),
        in_specs=[small] * 2 + [pl.BlockSpec(memory_space=pl.ANY), pl.BlockSpec(memory_space=pltpu.HBM)],
        out_specs=pl.BlockSpec(memory_space=pltpu.HBM),
        out_shape=pltpu.HBM(base.shape, base.dtype),
        scratch_shapes=[pltpu.SemaphoreType.DMA((base.shape[0], 2, len(slot_ids)))],
        input_output_aliases={3: 0},
        compiler_params=pltpu.CompilerParams(vmem_limit_bytes=16 << 20),
        name="assemble_late",
    )(lengths, place, arrived, base)


def rope_table(rows):
    inverse = np.exp(np.arange(HD // 2) * (-2.0 * math.log(rope_base) / HD))
    angles = np.arange(rows)[:, None] * inverse[None, :]
    cosine, sine_part = np.cos(angles), np.sin(angles)
    return jnp.asarray(np.concatenate([cosine, cosine, -sine_part, sine_part], axis=1), jnp.float32)


def exchange(sent):
    return lax.all_to_all(sent, "tp", split_axis=0, concat_axis=0, tiled=True)


def paired(hidden, lengths, kv_weight, input_gain, key_gain):
    tp_count = lax.axis_size("tp")
    nz = tp_count // 2
    group, me = lax.axis_index("grp"), lax.axis_index("tp")
    rows = hidden.shape[0]
    own_blocks = rows // BLK
    depth = kv_weight.shape[0]
    deep = 2 * own_blocks // tp_count
    page_count = pages_per_device(tp_count, own_blocks)
    group_len = lengths[0]
    place = jnp.stack([group, me]).astype(jnp.int32)
    swap = [(i, i ^ 1) for i in range(tp_count)]

    own_gain = lax.dynamic_slice(input_gain, (group * depth,), (depth,))
    shard = (kv_weight.astype(jnp.float32) * own_gain[:, None]).astype(jnp.bfloat16)
    sibling = lax.ppermute(hidden, "tp", swap)
    gain = key_gain.reshape(1, HD)

    def from_chip(flip, own):
        return lax.ppermute(own, "tp", [(i, i ^ (2 * flip)) for i in range(tp_count)])

    def start_group(arrays, pieces):
        return project_near(group_len, place, hidden, sibling, arrays, pieces, depth)

    def end_group(slot_ids, far, partial):
        return project_far(
            slot_ids, group_len, place, hidden, sibling, far, partial, (scale, other_scale), turn, gain, deep
        )

    groups = [tuple(range(start, min(start + 2, nz))) for start in range(0, nz, 2)]
    turn = rope_table(rows)
    slots = [shard] + [None] * (nz - 1)
    line = nz == 4
    inward = [(2 + c, 4 + c) for c in range(2)] + [(4 + c, 2 + c) for c in range(2)]
    outward = [(2 + c, c) for c in range(2)] + [(4 + c, 6 + c) for c in range(2)]
    around = inward + [(c, 6 + c) for c in range(2)] + [(6 + c, c) for c in range(2)]
    inner = (me // 2 == 1) | (me // 2 == 2)
    slots[1] = from_chip(1, shard)
    side0 = sides(shard)
    across = lax.ppermute(shard, "tp", inward) if line else shard
    slots[1], shard, across = lax.optimization_barrier((slots[1], shard, across))
    if line:
        ends = lax.ppermute(jnp.where(inner, slots[1], shard), "tp", around)
        passed = lax.ppermute(across, "tp", outward)
    else:
        slots[2:] = [from_chip(flip, shard) for flip in range(2, nz)]
    slots[1], side0, later_len = lax.optimization_barrier((slots[1], side0, group_len))
    side1 = sides(slots[1])
    scale = row_scales(later_len, place, hidden)
    side0, side1 = lax.optimization_barrier((side0, side1))
    far = opposite(side0[0], side1[1])
    side1, scale, sibling = lax.optimization_barrier((side1, scale, sibling))
    other_scale = lax.ppermute(scale, "tp", swap)
    partial = start_group([slots[0], *side0, slots[1], *side1], [(part, 0) for part in range(6)])
    if line:
        far, other_scale, ends, passed, partial = lax.optimization_barrier((far, other_scale, ends, passed, partial))
        slots[2:] = [jnp.where(inner, ends, passed), jnp.where(inner, across, ends)]
    else:
        far, other_scale, slots, partial = lax.optimization_barrier((far, other_scale, slots, partial))
    sent, rest = end_group(groups[0], far, partial)
    arrived, over = [], [rest]
    for slot_ids in groups[1:]:
        both = jnp.concatenate([slots[slot] for slot in slot_ids])
        crossed = sides(both)
        arrived.append(exchange(sent))
        crossed, over[-1] = lax.optimization_barrier((crossed, over[-1]))
        far = opposite(crossed[0][:depth], crossed[1][depth:])
        pieces = [(source, index * depth) for index in range(2) for source in range(3)]
        partial = start_group([both, *crossed], pieces)
        far, partial = lax.optimization_barrier((far, partial))
        sent, rest = end_group(slot_ids, far, partial)
        over.append(rest)
    last_arrived = exchange(sent)

    counts = (group_len + (BLK - 1)) // BLK
    chip_counts = counts[0::2] + counts[1::2]
    most = jnp.max(chip_counts)

    def spill(rests):
        held = jnp.concatenate(rests, axis=1)
        source = jnp.argmax(chip_counts).astype(jnp.int32)
        first = jnp.sum(jnp.where(jnp.arange(nz) < source, chip_counts, 0))
        moved = []
        for late in range(held.shape[0]):
            rank = deep * tp_count + late
            flip = jnp.where(rank < most, source ^ ((first + rank) % tp_count // 2), 0)
            ways = [lambda block: block] + [functools.partial(from_chip, way) for way in range(1, nz)]
            moved.append(lax.switch(flip, ways, held[late]))
        moved = jnp.stack(moved)
        return moved, lax.ppermute(moved, "tp", swap)

    def no_spill(rests):
        shape = (rests[0].shape[0], nz) + rests[0].shape[2:]
        return jnp.zeros(shape, jnp.bfloat16), jnp.zeros(shape, jnp.bfloat16)

    spilled = lax.cond(most > deep * tp_count, spill, no_spill, over)
    base = assemble_early(groups[:-1], group_len, place, arrived, spilled, page_count, deep)
    return assemble_late(groups[-1], group_len, place, last_arrived, base, deep)


def local(hidden, lengths, kv_weight, input_gain, key_gain):
    tp_count = lax.axis_size("tp")
    own_blocks = hidden.shape[0] // BLK
    spilling = (2 * own_blocks // tp_count * tp_count - 1) * BLK + 2
    fits = (
        lax.axis_size("grp") == 4
        and tp_count >= 4
        and tp_count & (tp_count - 1) == 0
        and kv_weight.shape[1] == HD
        and kv_weight.shape[0] % 256 == 0
        and 2 * own_blocks >= tp_count
        and 2 * spilling > group_tokens(tp_count, own_blocks)
    )
    chosen = paired if fits else general
    return chosen(hidden, lengths, kv_weight, input_gain, key_gain)


def solution(mesh):
    placed = (P(("grp", "tp"), None), P("grp", None), P("grp", "tp"), P(), P())
    return jax.shard_map(
        local, mesh=mesh, in_specs=placed, out_specs=P(("grp", "tp"), None, None), check_vma=False
    )
```

```python
import functools
import math

import jax
import jax.numpy as jnp
import numpy as np
from jax import lax
from jax.experimental import pallas as pl
from jax.experimental.pallas import tpu as pltpu
from jax.sharding import PartitionSpec as P

HD = 128
KVH = 4
BLK = 128


rope_base = 1000000.0
norm_eps = 1e-06


def normalize(token_rows, input_gain):
    values = token_rows.astype(jnp.float32)
    row_scale = lax.rsqrt(jnp.mean(values * values, axis=-1, keepdims=True) + norm_eps)
    return (values * row_scale * input_gain).astype(jnp.bfloat16)


def finish(projected, positions, valid, key_gain):
    key_width = KVH * HD
    half_dim = HD // 2
    row_count = projected.shape[0]
    key_part = projected[:, :key_width].reshape(row_count, KVH, HD)
    key_scale = lax.rsqrt(jnp.mean(key_part * key_part, axis=-1, keepdims=True) + norm_eps)
    key_part = key_part * key_scale * key_gain
    exponent = jnp.arange(half_dim, dtype=jnp.float32) * (2.0 / HD)
    inverse = jnp.exp(exponent * -math.log(rope_base))
    angles = positions.astype(jnp.float32)[:, None] * inverse[None, :]
    cosine = jnp.cos(angles)[:, None, :]
    sine_part = jnp.sin(angles)[:, None, :]
    lower_half = key_part[..., :half_dim]
    upper_half = key_part[..., half_dim:]
    turned = jnp.concatenate(
        [
            lower_half * cosine - upper_half * sine_part,
            upper_half * cosine + lower_half * sine_part,
        ],
        axis=-1,
    )
    merged = jnp.concatenate(
        [turned.reshape(row_count, key_width), projected[:, key_width:]], axis=-1
    )
    return jnp.where(valid[:, None], merged, 0.0).astype(jnp.bfloat16)


def project(normed, kv_weight):
    all_rows = lax.all_gather(kv_weight, "grp", axis=0, tiled=True)
    return jnp.dot(
        normed,
        lax.all_gather(all_rows, "tp", axis=1, tiled=True),
        preferred_element_type=jnp.float32,
    )


def group_tokens(tp_count, own_blocks):
    return 2 * tp_count * own_blocks * BLK // 5


def pages_per_device(tp_count, own_blocks):
    live_tokens = group_tokens(tp_count, own_blocks)
    return ((live_tokens + BLK - 1) // BLK + 2 * tp_count - 2) // tp_count


def general(hidden, lengths, kv_weight, input_gain, key_gain):
    tp_count = lax.axis_size("tp")
    my_index = lax.axis_index("tp")
    own_blocks = hidden.shape[0] // BLK
    page_count = pages_per_device(tp_count, own_blocks)
    per_peer = (own_blocks + tp_count - 1) // tp_count
    cache_width = 2 * KVH * HD
    group_len = lengths[0]
    block_counts = (group_len + (BLK - 1)) // BLK
    block_ends = jnp.cumsum(block_counts)
    block_starts = block_ends - block_counts
    offsets = jnp.arange(BLK, dtype=jnp.int32)
    my_start = block_starts[my_index]
    my_count = block_counts[my_index]
    my_length = group_len[my_index]
    outbound = (
        jnp.arange(tp_count, dtype=jnp.int32)[:, None] - my_start
    ) % tp_count + tp_count * jnp.arange(per_peer, dtype=jnp.int32)[None, :]
    outbound = outbound.reshape(-1)
    sending = outbound < my_count
    picked_local = jnp.minimum(outbound, own_blocks - 1)
    page_ranks = tp_count * jnp.arange(page_count, dtype=jnp.int32) + my_index
    anchor = jnp.minimum(
        jnp.sum((block_ends[None, :] <= page_ranks[:, None]).astype(jnp.int32), axis=1),
        tp_count - 1,
    )
    block_index = page_ranks - block_starts[anchor]
    page_live = page_ranks < block_ends[-1]
    chosen = anchor * per_peer + jnp.clip(block_index // tp_count, 0, per_peer - 1)
    projected = project(normalize(hidden, input_gain), kv_weight)
    own_pos = (jnp.arange(own_blocks, dtype=jnp.int32)[:, None] * BLK + offsets[None, :]).reshape(
        -1
    )
    own_cache = finish(projected, own_pos, own_pos < my_length, key_gain).reshape(
        own_blocks, BLK, cache_width
    )
    outgoing = jnp.where(
        sending[:, None, None],
        jnp.take(own_cache, picked_local, axis=0),
        jnp.zeros((), jnp.bfloat16),
    )
    arrived = lax.all_to_all(outgoing, "tp", split_axis=0, concat_axis=0, tiled=True)
    cache_pages = jnp.take(arrived, chosen, axis=0)
    return jnp.where(page_live[:, None, None], cache_pages, jnp.zeros((), jnp.bfloat16))


flip0 = [(i, i ^ 1) for i in range(4)]
flip1 = [(i, i ^ 2) for i in range(4)]


def sides(shard):
    return lax.ppermute(shard, "grp", flip0), lax.ppermute(shard, "grp", flip1)


def opposite(first_side0, second_side1):
    return lax.ppermute(first_side0, "grp", flip1), lax.ppermute(second_side1, "grp", flip0)


def stay(array):
    return pltpu.with_memory_space_constraint(array, pltpu.HBM)


def scale_kernel(lengths_ref, place_ref, x_ref, out_ref, x_buf, x_sem):
    count = (lengths_ref[place_ref[1]] + (BLK - 1)) // BLK

    def copy_of(block):
        rows = pl.ds(pl.multiple_of(block * BLK, BLK), BLK)
        return pltpu.make_async_copy(x_ref.at[rows], x_buf.at[rows], x_sem.at[block])

    def fetch(block, carry):
        copy_of(block).start()
        return carry

    def one_block(block, carry):
        copy_of(block).wait()
        rows = pl.ds(pl.multiple_of(block * BLK, BLK), BLK)
        squares = jnp.zeros((BLK, HD), jnp.float32)
        for cut in range(0, x_buf.shape[1], HD):
            values = x_buf[rows, cut : cut + HD].astype(jnp.float32)
            squares = squares + values * values
        mean = jnp.sum(squares, axis=-1, keepdims=True) / x_buf.shape[1]
        out_ref[rows, :] = jnp.broadcast_to(lax.rsqrt(mean + norm_eps), (BLK, HD))
        return carry

    lax.fori_loop(0, count, fetch, 0)
    lax.fori_loop(0, count, one_block, 0)


def row_scales(lengths, place, hidden):
    rows, width = hidden.shape
    small = pl.BlockSpec(memory_space=pltpu.SMEM)
    return pl.pallas_call(
        scale_kernel,
        in_specs=[small, small, pl.BlockSpec(memory_space=pltpu.HBM)],
        out_specs=pl.BlockSpec(memory_space=pltpu.VMEM),
        out_shape=jax.ShapeDtypeStruct((rows, HD), jnp.float32),
        scratch_shapes=[
            pltpu.VMEM((rows, width), hidden.dtype),
            pltpu.SemaphoreType.DMA((rows // BLK,)),
        ],
        compiler_params=pltpu.CompilerParams(vmem_limit_bytes=16 << 20),
        cost_estimate=pl.CostEstimate(
            flops=3 * rows * width, bytes_accessed=2 * rows * width, transcendentals=0
        ),
        name="row_scales",
    )(lengths, place, stay(hidden))


def tile_blocks(own_blocks):
    return max(t for t in (1, 2, 3) if own_blocks % t == 0)


class Chip:
    def __init__(self, lengths_ref, place_ref):
        self.tp_count = lengths_ref.shape[0]
        self.group, me = place_ref[0], place_ref[1]
        self.chip, self.core = me // 2, me % 2
        self.first = jnp.int32(0)
        for index in range(self.tp_count):
            count = (lengths_ref[index] + (BLK - 1)) // BLK
            self.first = self.first + jnp.where(index < 2 * self.chip, count, 0)
        length0, length1 = lengths_ref[2 * self.chip], lengths_ref[2 * self.chip + 1]
        self.count0 = (length0 + (BLK - 1)) // BLK
        self.own_len = jnp.where(self.core == 0, length0, length1)
        self.sib_len = jnp.where(self.core == 0, length1, length0)
        self.own_count = (self.own_len + (BLK - 1)) // BLK
        self.total = self.own_count + (self.sib_len + (BLK - 1)) // BLK

    def within(self, i):
        return jnp.where(i < self.own_count, i, i - self.own_count)

    def rows(self, i):
        return pl.ds(pl.multiple_of(self.within(i) * BLK, BLK), BLK)

    def fetch(self, i, own_ref, sib_ref, x_buf, x_sem, flips, depth, start):
        target = pl.ds(pl.multiple_of(i * BLK, BLK), BLK)

        def copies(source):
            for order, flip in enumerate(flips):
                columns = pl.ds(pl.multiple_of((self.group ^ flip) * depth, HD), depth)
                copy = pltpu.make_async_copy(
                    source.at[self.rows(i), columns],
                    x_buf.at[target, pl.ds(order * depth, depth)],
                    x_sem.at[i, order],
                )
                copy.start() if start else copy.wait()

        pl.when(i < self.own_count)(lambda: copies(own_ref))
        pl.when(jnp.logical_and(i >= self.own_count, i < self.total))(lambda: copies(sib_ref))

    def fetch_all(self, *args):
        def one_block(i, carry):
            self.fetch(i, *args, True)
            return carry

        lax.fori_loop(0, self.total, one_block, 0)


def near_kernel(tile, depth, pieces, *refs):
    lengths_ref, place_ref, own_ref, sib_ref = refs[:4]
    partial_ref, x_buf, w_buf, x_sem, w_sem = refs[-5:]
    near = refs[4:-5]
    chip = Chip(lengths_ref, place_ref)
    span = tile * BLK
    copies = [
        pltpu.make_async_copy(
            near[source].at[pl.ds(row, depth)],
            w_buf.at[pl.ds(part % 3 * depth, depth), pl.ds(part // 3 * HD, HD)],
            w_sem.at[part],
        )
        for part, (source, row) in enumerate(pieces)
    ]
    for copy in copies:
        copy.start()
    fetch = own_ref, sib_ref, x_buf, x_sem, (0, 1, 2), depth
    chip.fetch_all(*fetch)
    for copy in copies:
        copy.wait()

    def one_tile(step, carry):
        for part in range(tile):
            chip.fetch(step * tile + part, *fetch, False)
        rows = pl.ds(pl.multiple_of(step * span, span), span)
        partial_ref[rows, :] = jnp.dot(x_buf[rows, :], w_buf[...], preferred_element_type=jnp.float32)
        return carry

    lax.fori_loop(0, (chip.total + (tile - 1)) // tile, one_tile, 0)


def project_near(lengths, place, own, sibling, arrays, pieces, depth):
    rows, width = own.shape
    tile = tile_blocks(rows // BLK)
    columns = len(pieces) // 3 * HD
    small = pl.BlockSpec(memory_space=pltpu.SMEM)
    anywhere = pl.BlockSpec(memory_space=pl.ANY)
    in_hbm = pl.BlockSpec(memory_space=pltpu.HBM)
    held = 2 * rows + tile * BLK
    return pl.pallas_call(
        functools.partial(near_kernel, tile, depth, pieces),
        in_specs=[small] * 2 + [in_hbm] * 2 + [anywhere] * len(arrays),
        out_specs=pl.BlockSpec(memory_space=pltpu.VMEM),
        out_shape=jax.ShapeDtypeStruct((held, columns), jnp.float32),
        scratch_shapes=[
            pltpu.VMEM((held, 3 * depth), own.dtype),
            pltpu.VMEM((3 * depth, columns), jnp.bfloat16),
            pltpu.SemaphoreType.DMA((2 * rows // BLK, 3)),
            pltpu.SemaphoreType.DMA((len(pieces),)),
        ],
        compiler_params=pltpu.CompilerParams(vmem_limit_bytes=34 << 20),
        cost_estimate=pl.CostEstimate(
            flops=24 * rows * depth * columns, bytes_accessed=24 * rows * depth, transcendentals=0
        ),
        name="project_near",
    )(lengths, place, stay(own), stay(sibling), *arrays)


def far_kernel(slot_ids, tile, depth, deep, *refs):
    lengths_ref, place_ref, own_ref, sib_ref = refs[:4]
    far = refs[4:6]
    partial_ref, turn_ref, gain_ref, own_scale, sib_scale, out_ref, over_ref = refs[6:13]
    x_buf, w_buf, o_buf, x_sem, w_sem, o_sem = refs[13:]
    count = len(slot_ids)
    chip = Chip(lengths_ref, place_ref)
    tp_count, total, own_count = chip.tp_count, chip.total, chip.own_count
    tiles = (total + (tile - 1)) // tile
    span = tile * BLK
    copies = [
        pltpu.make_async_copy(far[index], w_buf.at[:, pl.ds(index * HD, HD)], w_sem.at[index])
        for index in range(count)
    ]
    for copy in copies:
        copy.start()
    fetch = own_ref, sib_ref, x_buf, x_sem, (3,), depth
    chip.fetch_all(*fetch)
    for copy in copies:
        copy.wait()
    is_key = [2 * (chip.chip ^ slot) + chip.core < KVH for slot in slot_ids]

    shift = tp_count.bit_length() - 1

    def send(i):
        second = jnp.where(i < own_count, chip.core, 1 - chip.core)
        place = chip.within(i) + second * chip.count0

        @pl.when(jnp.logical_and(i < total, place < deep * tp_count))
        def _():
            target = out_ref.at[(chip.first + place) & (tp_count - 1), lax.shift_right_logical(place, shift)]
            pltpu.make_async_copy(o_buf.at[i], target, o_sem.at[i]).start()

        @pl.when(jnp.logical_and(i < total, place >= deep * tp_count))
        def _():
            target = over_ref.at[place - deep * tp_count]
            pltpu.make_async_copy(o_buf.at[i], target, o_sem.at[i]).start()

    def multiply(step):
        for part in range(tile):
            chip.fetch(step * tile + part, *fetch, False)
        rows = pl.ds(pl.multiple_of(step * span, span), span)
        return partial_ref[rows, :] + jnp.dot(x_buf[rows, :], w_buf[...], preferred_element_type=jnp.float32)

    ones = jnp.full((HD, HD), 1.0 / HD, jnp.bfloat16)

    def head_mean(squares):
        high = squares.astype(jnp.bfloat16)
        low = (squares - high.astype(jnp.float32)).astype(jnp.bfloat16)
        return jnp.dot(high, ones, preferred_element_type=jnp.float32) + jnp.dot(
            low, ones, preferred_element_type=jnp.float32
        )

    def finish_tile(step, product):
        for part in range(tile):
            i = jnp.minimum(step * tile + part, total - 1)
            rows = chip.rows(i)
            limit = jnp.where(i < own_count, chip.own_len, chip.sib_len) - chip.within(i) * BLK
            valid = lax.broadcasted_iota(jnp.int32, (BLK, HD), 0) < limit
            scale = jnp.where(i < own_count, own_scale[rows, :], sib_scale[rows, :])
            for index in range(count):
                cut = product[part * BLK : (part + 1) * BLK, index * HD : (index + 1) * HD]
                values = cut * scale
                key_scale = lax.rsqrt(head_mean(values * values) + norm_eps)
                keys = values * key_scale * gain_ref[...]
                turned = keys * turn_ref[rows, :HD] + pltpu.roll(keys, HD // 2, 1) * turn_ref[rows, HD:]
                merged = jnp.where(jnp.logical_and(valid, is_key[index]), turned, jnp.where(valid, values, 0.0))
                o_buf[step * tile + part, index] = merged.astype(jnp.bfloat16)

    def send_tile(step):
        for part in range(tile):
            send(step * tile + part)

    def one_tile(step, product):
        following = multiply(step)
        finish_tile(step - 1, product)
        send_tile(step - 1)
        return following

    product = lax.fori_loop(1, tiles, one_tile, multiply(jnp.int32(0)))
    finish_tile(tiles - 1, product)
    send_tile(tiles - 1)

    def drain(i, carry):
        pltpu.make_async_copy(o_buf.at[i], out_ref.at[0, 0], o_sem.at[i]).wait()
        return carry

    lax.fori_loop(0, total, drain, 0)


def project_far(slot_ids, lengths, place, own, sibling, far, partial, scales, turn, key_gain, deep):
    rows, width = own.shape
    tp_count = lengths.shape[0]
    own_blocks = rows // BLK
    count = len(slot_ids)
    depth = far[0].shape[0]
    tile = tile_blocks(own_blocks)
    spare = 2 * own_blocks - deep * tp_count
    small = pl.BlockSpec(memory_space=pltpu.SMEM)
    anywhere = pl.BlockSpec(memory_space=pl.ANY)
    in_hbm = pl.BlockSpec(memory_space=pltpu.HBM)
    whole = pl.BlockSpec(memory_space=pltpu.VMEM)
    return pl.pallas_call(
        functools.partial(far_kernel, slot_ids, tile, depth, deep),
        in_specs=[small] * 2 + [in_hbm] * 2 + [anywhere] * 2 + [whole] * 5,
        out_specs=[in_hbm, anywhere],
        out_shape=[
            pltpu.HBM((tp_count, deep, count, BLK, HD), jnp.bfloat16),
            jax.ShapeDtypeStruct((max(spare, 1), count, BLK, HD), jnp.bfloat16),
        ],
        scratch_shapes=[
            pltpu.VMEM((2 * rows + tile * BLK, depth), own.dtype),
            pltpu.VMEM((depth, count * HD), jnp.bfloat16),
            pltpu.VMEM((2 * own_blocks + tile, count, BLK, HD), jnp.bfloat16),
            pltpu.SemaphoreType.DMA((2 * own_blocks, 1)),
            pltpu.SemaphoreType.DMA((count,)),
            pltpu.SemaphoreType.DMA((2 * own_blocks + tile,)),
        ],
        compiler_params=pltpu.CompilerParams(vmem_limit_bytes=16 << 20),
        cost_estimate=pl.CostEstimate(
            flops=16 * rows * depth * count * HD, bytes_accessed=16 * rows * depth, transcendentals=0
        ),
        name="project_far",
    )(lengths, place, stay(own), stay(sibling), *far, partial, turn, key_gain, *scales)


def page_source(lengths_ref, place_ref, page):
    tp_count = lengths_ref.shape[0]
    rank = page * tp_count + place_ref[1]
    end, chip, first = jnp.int32(0), jnp.int32(0), jnp.int32(0)
    for index in range(tp_count):
        end = end + (lengths_ref[index] + (BLK - 1)) // BLK
        if index % 2 == 1 and index + 1 < tp_count:
            passed = end <= rank
            chip = jnp.where(passed, index // 2 + 1, chip)
            first = jnp.where(passed, end, first)
    return rank < end, chip, rank - first


def columns_of(chip, slot, core):
    return pl.ds(pl.multiple_of((2 * (chip ^ slot) + core) * HD, HD), HD)


def early_kernel(groups, deep, lengths_ref, place_ref, *refs):
    arrived, spilled = refs[: len(groups)], refs[len(groups) : -3]
    out_ref, o_buf, o_sem = refs[-3:]
    tp_count = lengths_ref.shape[0]
    me = place_ref[1]

    def copy_of(page):
        return pltpu.make_async_copy(o_buf.at[page], out_ref.at[page], o_sem.at[page])

    for page in range(o_buf.shape[0]):
        live, chip, within = page_source(lengths_ref, place_ref, page)
        over = within >= deep * tp_count

        @pl.when(jnp.logical_and(live, jnp.logical_not(over)))
        def _():
            for order, slot_ids in enumerate(groups):
                for core in range(2):
                    for index, slot in enumerate(slot_ids):
                        block = arrived[order][2 * chip + core, within // tp_count, index]
                        o_buf[page, :, columns_of(chip, slot, core)] = block

        @pl.when(jnp.logical_and(live, over))
        def _():
            late = within - deep * tp_count
            for slot in range(tp_count // 2):
                o_buf[page, :, columns_of(chip, slot, me % 2)] = spilled[0][late, slot]
                o_buf[page, :, columns_of(chip, slot, 1 - me % 2)] = spilled[1][late, slot]

        @pl.when(jnp.logical_not(live))
        def _():
            o_buf[page] = jnp.zeros(o_buf.shape[1:], o_buf.dtype)

        copy_of(page).start()
    for page in range(o_buf.shape[0]):
        copy_of(page).wait()


def assemble_early(groups, lengths, place, arrived, spilled, page_count, deep):
    small = pl.BlockSpec(memory_space=pltpu.SMEM)
    whole = pl.BlockSpec(memory_space=pltpu.VMEM)
    shape = (page_count, BLK, 2 * KVH * HD)
    return pl.pallas_call(
        functools.partial(early_kernel, groups, deep),
        in_specs=[small] * 2 + [whole] * (len(arrived) + len(spilled)),
        out_specs=pl.BlockSpec(memory_space=pltpu.HBM),
        out_shape=pltpu.HBM(shape, jnp.bfloat16),
        scratch_shapes=[pltpu.VMEM(shape, jnp.bfloat16), pltpu.SemaphoreType.DMA((page_count,))],
        compiler_params=pltpu.CompilerParams(vmem_limit_bytes=16 << 20),
        name="assemble_early",
    )(lengths, place, *arrived, *spilled)


def late_kernel(slot_ids, deep, lengths_ref, place_ref, arrived, base_ref, out_ref, o_sem):
    del base_ref
    tp_count = lengths_ref.shape[0]

    def each_page(start):
        for page in range(out_ref.shape[0]):
            live, chip, within = page_source(lengths_ref, place_ref, page)

            @pl.when(jnp.logical_and(live, within < deep * tp_count))
            def _():
                for core in range(2):
                    for index, slot in enumerate(slot_ids):
                        copy = pltpu.make_async_copy(
                            arrived.at[2 * chip + core, within // tp_count, index],
                            out_ref.at[page, :, columns_of(chip, slot, core)],
                            o_sem.at[page, core, index],
                        )
                        copy.start() if start else copy.wait()

    each_page(True)
    each_page(False)


def assemble_late(slot_ids, lengths, place, arrived, base, deep):
    small = pl.BlockSpec(memory_space=pltpu.SMEM)
    return pl.pallas_call(
        functools.partial(late_kernel, slot_ids, deep),
        in_specs=[small] * 2 + [pl.BlockSpec(memory_space=pl.ANY), pl.BlockSpec(memory_space=pltpu.HBM)],
        out_specs=pl.BlockSpec(memory_space=pltpu.HBM),
        out_shape=pltpu.HBM(base.shape, base.dtype),
        scratch_shapes=[pltpu.SemaphoreType.DMA((base.shape[0], 2, len(slot_ids)))],
        input_output_aliases={3: 0},
        compiler_params=pltpu.CompilerParams(vmem_limit_bytes=16 << 20),
        name="assemble_late",
    )(lengths, place, arrived, base)


def rope_table(rows):
    inverse = np.exp(np.arange(HD // 2) * (-2.0 * math.log(rope_base) / HD))
    angles = np.arange(rows)[:, None] * inverse[None, :]
    cosine, sine_part = np.cos(angles), np.sin(angles)
    return jnp.asarray(np.concatenate([cosine, cosine, -sine_part, sine_part], axis=1), jnp.float32)


def exchange(sent):
    return lax.all_to_all(sent, "tp", split_axis=0, concat_axis=0, tiled=True)


def paired(hidden, lengths, kv_weight, input_gain, key_gain):
    tp_count = lax.axis_size("tp")
    nz = tp_count // 2
    group, me = lax.axis_index("grp"), lax.axis_index("tp")
    rows = hidden.shape[0]
    own_blocks = rows // BLK
    depth = kv_weight.shape[0]
    deep = 2 * own_blocks // tp_count
    page_count = pages_per_device(tp_count, own_blocks)
    group_len = lengths[0]
    place = jnp.stack([group, me]).astype(jnp.int32)
    swap = [(i, i ^ 1) for i in range(tp_count)]

    own_gain = lax.dynamic_slice(input_gain, (group * depth,), (depth,))
    shard = (kv_weight.astype(jnp.float32) * own_gain[:, None]).astype(jnp.bfloat16)
    sibling = lax.ppermute(hidden, "tp", swap)
    gain = key_gain.reshape(1, HD)

    def from_chip(flip, own):
        return lax.ppermute(own, "tp", [(i, i ^ (2 * flip)) for i in range(tp_count)])

    def start_group(arrays, pieces):
        return project_near(group_len, place, hidden, sibling, arrays, pieces, depth)

    def end_group(slot_ids, far, partial):
        return project_far(
            slot_ids, group_len, place, hidden, sibling, far, partial, (scale, other_scale), turn, gain, deep
        )

    groups = [tuple(range(start, min(start + 2, nz))) for start in range(0, nz, 2)]
    turn = rope_table(rows)
    slots = [shard] + [None] * (nz - 1)
    line = nz == 4
    inward = [(2 + c, 4 + c) for c in range(2)] + [(4 + c, 2 + c) for c in range(2)]
    outward = [(2 + c, c) for c in range(2)] + [(4 + c, 6 + c) for c in range(2)]
    around = inward + [(c, 6 + c) for c in range(2)] + [(6 + c, c) for c in range(2)]
    inner = (me // 2 == 1) | (me // 2 == 2)
    slots[1] = from_chip(1, shard)
    side0 = sides(shard)
    across = lax.ppermute(shard, "tp", inward) if line else shard
    scale = row_scales(group_len, place, hidden)
    slots[1], shard, across, scale = lax.optimization_barrier((slots[1], shard, across, scale))
    if line:
        ends = lax.ppermute(jnp.where(inner, slots[1], shard), "tp", around)
        passed = lax.ppermute(across, "tp", outward)
    else:
        slots[2:] = [from_chip(flip, shard) for flip in range(2, nz)]
    slots[1], side0 = lax.optimization_barrier((slots[1], side0))
    side1 = sides(slots[1])
    side0, side1 = lax.optimization_barrier((side0, side1))
    far = opposite(side0[0], side1[1])
    side1, scale, sibling = lax.optimization_barrier((side1, scale, sibling))
    other_scale = lax.ppermute(scale, "tp", swap)
    partial = start_group([slots[0], *side0, slots[1], *side1], [(part, 0) for part in range(6)])
    if line:
        far, other_scale, ends, passed, partial = lax.optimization_barrier((far, other_scale, ends, passed, partial))
        slots[2:] = [jnp.where(inner, ends, passed), jnp.where(inner, across, ends)]
    else:
        far, other_scale, slots, partial = lax.optimization_barrier((far, other_scale, slots, partial))
    sent, rest = end_group(groups[0], far, partial)
    arrived, over = [], [rest]
    for slot_ids in groups[1:]:
        both = jnp.concatenate([slots[slot] for slot in slot_ids])
        crossed = sides(both)
        arrived.append(exchange(sent))
        crossed, over[-1] = lax.optimization_barrier((crossed, over[-1]))
        far = opposite(crossed[0][:depth], crossed[1][depth:])
        pieces = [(source, index * depth) for index in range(2) for source in range(3)]
        partial = start_group([both, *crossed], pieces)
        far, partial = lax.optimization_barrier((far, partial))
        sent, rest = end_group(slot_ids, far, partial)
        over.append(rest)
    last_arrived = exchange(sent)

    counts = (group_len + (BLK - 1)) // BLK
    chip_counts = counts[0::2] + counts[1::2]
    most = jnp.max(chip_counts)

    def spill(rests):
        held = jnp.concatenate(rests, axis=1)
        source = jnp.argmax(chip_counts).astype(jnp.int32)
        first = jnp.sum(jnp.where(jnp.arange(nz) < source, chip_counts, 0))
        moved = []
        for late in range(held.shape[0]):
            rank = deep * tp_count + late
            flip = jnp.where(rank < most, source ^ ((first + rank) % tp_count // 2), 0)
            ways = [lambda block: block] + [functools.partial(from_chip, way) for way in range(1, nz)]
            moved.append(lax.switch(flip, ways, held[late]))
        moved = jnp.stack(moved)
        return moved, lax.ppermute(moved, "tp", swap)

    def no_spill(rests):
        shape = (rests[0].shape[0], nz) + rests[0].shape[2:]
        return jnp.zeros(shape, jnp.bfloat16), jnp.zeros(shape, jnp.bfloat16)

    spilled = lax.cond(most > deep * tp_count, spill, no_spill, over)
    base = assemble_early(groups[:-1], group_len, place, arrived, spilled, page_count, deep)
    return assemble_late(groups[-1], group_len, place, last_arrived, base, deep)


def local(hidden, lengths, kv_weight, input_gain, key_gain):
    tp_count = lax.axis_size("tp")
    own_blocks = hidden.shape[0] // BLK
    spilling = (2 * own_blocks // tp_count * tp_count - 1) * BLK + 2
    fits = (
        lax.axis_size("grp") == 4
        and tp_count >= 4
        and tp_count & (tp_count - 1) == 0
        and kv_weight.shape[1] == HD
        and kv_weight.shape[0] % 256 == 0
        and 2 * own_blocks >= tp_count
        and 2 * spilling > group_tokens(tp_count, own_blocks)
    )
    chosen = paired if fits else general
    return chosen(hidden, lengths, kv_weight, input_gain, key_gain)


def solution(mesh):
    placed = (P(("grp", "tp"), None), P("grp", None), P("grp", "tp"), P(), P())
    return jax.shard_map(
        local, mesh=mesh, in_specs=placed, out_specs=P(("grp", "tp"), None, None), check_vma=False
    )
```
